128 devices in a mesh: grp: 8 (over y, core), mid: 16 (over x, z).
Axes of the slice: x: 4, y: 4, z: 4, core: 2. Of those that a mesh axis runs over, the one named last changes fastest.
Arguments:
- queries: bfloat16 [16384, 768], P('grp'), may hold values from -6 to 6
- coarse_vectors: bfloat16 [2048, 768], replicated, may hold values from -0.4375 to 0.4375
- mid_vectors: bfloat16 [262144, 768], P(('grp', 'mid')), may hold values from -0.4375 to 0.4375
- leaf_vectors: bfloat16 [131072, 768], P(('grp', 'mid')), may hold values from -0.4375 to 0.4375
- coarse_pos: int32 [16384, 4], P(('grp', 'mid')), may hold values from 0 to 2047
- mid_pos: int32 [16384, 4], P('grp'), may hold values from 0 to 4095
- leaf_pos: int32 [16384, 4], P('grp'), may hold values from 0 to 4095
- mid_cand: int32 [128, 8], P('grp'), may hold values from 0 to 511, as said below
- leaf_cand: int32 [128, 8], P('grp'), may hold values from 0 to 255, as said below
- leaf_owner: int32 [256], replicated, may hold values from 0 to 255, as said below
Outputs:
- grad_query: float32 [16384, 768], P(('grp', 'mid'))
- grad_coarse: float32 [2048, 768], P(('grp', 'mid'))
- grad_mid: float32 [262144, 768], P(('grp', 'mid'))
- grad_leaf: float32 [131072, 768], P(('grp', 'mid'))
The draws below stay inside these ranges and needn't reach their ends.
Inputs may be any that keep to these rules, and one draw needn't show every extreme that they name: `mid_cand`: mid block b lies on device b // 4 in grp+mid order. Among the candidates of the tiles of one group, at most 2 lie on devices of one mid index within one group; in every draw some device receives 2 such candidates from every group. `leaf_cand`: storage block s lies on device s // 2 in grp+mid order. Among the candidates of the tiles of one group, at most 2 are stored on devices of one mid index within one group; in every draw some device receives 2 such candidates from every group. `leaf_owner`: A permutation of the leaf blocks.
All inputs are finite; a program needn't handle non-finite values.
Results may differ from the reference program's by a relative error of at most 0.0065.
Values may be sent and summed in bfloat16 or wider, within the bound.
A program may use at most 256 MiB of HBM per device.

```python
import jax
import jax.numpy as jnp
from jax import lax

D = 768
TILE = 128
BLOCK = 512
COARSE = 2048
MID_DEV = 2048
LB_DEV = 2
Q_DEV = 128
K_CAND = 8
POS = 4
QUERIES = 16384
TILES = 128
MIDS = 262144
MID_BLOCKS = 512
LEAF_BLOCKS = 256
LEAVES = 131072
N_GRP = 8
N_MID = 16


def pair_plan(key, per_device):
    capacity = max(2, (2 * Q_DEV * K_CAND // TILE + N_GRP - 1) // N_GRP)
    group_tiles = Q_DEV * N_MID // TILE
    pair_count = group_tiles * K_CAND
    slot_count = N_MID * N_GRP * capacity
    hot_key, group_key = jax.random.split(key)
    hot_sender = jax.random.randint(jax.random.fold_in(hot_key, 1), (), 0, N_MID)
    hot_target = jax.random.randint(jax.random.fold_in(hot_key, 2), (), 0, N_GRP)
    position = jnp.arange(slot_count, dtype=jnp.int32)
    sender = position // (N_GRP * capacity)
    target = position // capacity % N_GRP
    priority = jnp.where((sender == hot_sender) & (target == hot_target), 1 << 29, 0)

    def one_group(group_seed):
        first_key, second_key, third_key = jax.random.split(group_seed, 3)
        scores = jax.random.randint(first_key, (slot_count,), 0, 1 << 16) * slot_count + position + priority
        chosen = jnp.argsort(-scores, stable=True)[:pair_count]
        block_slot = jax.random.randint(second_key, (pair_count,), 0, per_device)
        storage = (target[chosen] * N_MID + sender[chosen]) * per_device + block_slot
        return storage[jax.random.permutation(third_key, pair_count)]
    planned = jax.vmap(one_group)(jax.random.split(group_key, N_GRP))
    return planned.reshape(N_GRP * group_tiles, K_CAND).astype(jnp.int32)


def leaf_tables(key):
    storage = pair_plan(jax.random.fold_in(key, 101), LB_DEV)
    mapping = jax.random.permutation(jax.random.fold_in(key, 102), LEAF_BLOCKS).astype(jnp.int32)
    inverse = jnp.argsort(mapping, stable=True).astype(jnp.int32)
    return (inverse[storage], mapping)


def draw_mid_cand(key, part):
    key = jax.random.fold_in(key, 3)
    return pair_plan(key, MID_DEV // BLOCK)


def draw_leaf_cand(key, part):
    candidates, mapping = leaf_tables(key)
    return candidates


def draw_leaf_owner(key, part):
    candidates, mapping = leaf_tables(key)
    return mapping


def plant(result, own_key, low, largest):
    longest = result.shape.index(max(result.shape))
    spots = []
    for shift in (0, 1):
        where = [jax.random.randint(jax.random.fold_in(own_key, axis), (), 0, length) for axis, length in enumerate(result.shape)]
        where[longest] = (where[longest] + shift) % result.shape[longest]
        spots.append(tuple(where))
    return result.at[spots[0]].set(low).at[spots[1]].set(largest)


def level_of(key, shape, shards, least, top_value):
    gain = 1.0
    for axis_at, blocks in shards:
        draws = jax.random.uniform(jax.random.fold_in(jax.random.fold_in(key, 6), axis_at), (blocks,), jnp.float32, least / len(shards), top_value / len(shards))
        gain = gain * jnp.repeat(jnp.exp(draws), shape[axis_at] // blocks).reshape((-1,) + (1,) * (len(shape) - 1 - axis_at))
    return gain


def gaussian(key, extent, deviation, most, shards=(), kind=jnp.bfloat16):
    values = jax.random.normal(key, extent, jnp.float32) * deviation
    if len(shards) > 0:
        values = level_of(key, extent, shards, -0.22, 0.18) * values
    return jnp.clip(values, min=-most, max=most).astype(kind)


def setup_inputs(seed: int = 0) -> dict:
    splits = jax.random.split(jax.random.key(seed), 11)
    return {
        "queries": gaussian(splits[0], (QUERIES, D), 1.0, 6.0, ((0, 8),)),
        "coarse_vectors": gaussian(splits[1], (COARSE, D), (D // 4) ** -0.5, 0.4375),
        "mid_vectors": gaussian(splits[2], (MIDS, D), (D // 4) ** -0.5, 0.4375, ((0, 128),)),
        "leaf_vectors": gaussian(splits[3], (LEAVES, D), (D // 4) ** -0.5, 0.4375, ((0, 128),)),
        "coarse_pos": plant(jax.random.randint(splits[4], (QUERIES, POS), 0, COARSE), jax.random.fold_in(splits[4], 1), 0, COARSE - 1).astype(jnp.int32),
        "mid_pos": plant(jax.random.randint(splits[5], (QUERIES, POS), 0, K_CAND * BLOCK), jax.random.fold_in(splits[5], 1), 0, (K_CAND * BLOCK) - 1).astype(jnp.int32),
        "leaf_pos": plant(jax.random.randint(splits[6], (QUERIES, POS), 0, K_CAND * BLOCK), jax.random.fold_in(splits[6], 1), 0, (K_CAND * BLOCK) - 1).astype(jnp.int32),
        "mid_cand": draw_mid_cand(jax.random.fold_in(splits[10], 71), 0),
        "leaf_cand": draw_leaf_cand(jax.random.fold_in(splits[10], 71), 0),
        "leaf_owner": draw_leaf_owner(jax.random.fold_in(splits[10], 71), 0),
    }


loss_scale = 0.25


def targets(relative, span):
    columns = jnp.arange(span, dtype=jnp.int32)
    return jnp.any(relative[..., None] == columns, axis=-2).astype(jnp.float32)


def pair_terms(tile_queries, tile_positives, block_ids, blocks):
    vectors = blocks[block_ids].astype(jnp.float32)
    queries_wide = tile_queries.astype(jnp.float32)
    scores = jnp.einsum('qd,kld->kql', queries_wide, vectors)
    shifts = (jnp.arange(K_CAND, dtype=jnp.int32) * BLOCK)[:, None, None]
    relative = tile_positives[None] - shifts
    delta = ((jax.nn.sigmoid(scores) - targets(relative, BLOCK)) * loss_scale).astype(jnp.bfloat16)
    delta_wide = delta.astype(jnp.float32)
    query_part = jnp.einsum('kql,kld->kqd', delta_wide, vectors).astype(jnp.bfloat16)
    query_part = lax.optimization_barrier(query_part).astype(jnp.float32)
    block_part = jnp.einsum('kql,qd->kld', delta_wide, queries_wide)
    return jnp.sum(query_part, axis=0), block_part


def reference(queries, coarse_vectors, mid_vectors, leaf_vectors, coarse_pos, mid_pos, leaf_pos, mid_cand, leaf_cand, leaf_owner):
    mid_blocks = mid_vectors.reshape(MID_BLOCKS, BLOCK, D)
    leaf_blocks = leaf_vectors.reshape(LEAF_BLOCKS, BLOCK, D)
    leaf_ids = leaf_owner[leaf_cand].astype(jnp.int32)

    def step(totals, inputs):
        coarse_grad, mid_grad, leaf_grad = totals
        tile_queries, coarse_tile, mid_tile, leaf_tile, mid_ids, leaf_tile_ids = inputs
        coarse_scores = jnp.dot(tile_queries, coarse_vectors.T, preferred_element_type=jnp.float32)
        coarse_delta = ((jax.nn.sigmoid(coarse_scores) - targets(coarse_tile, COARSE)) * loss_scale).astype(jnp.bfloat16)
        query_grad = jnp.dot(coarse_delta, coarse_vectors, preferred_element_type=jnp.float32)
        coarse_grad = coarse_grad + jnp.dot(coarse_delta.T, tile_queries, preferred_element_type=jnp.float32)
        mid_query, mid_part = pair_terms(tile_queries, mid_tile, mid_ids, mid_blocks)
        mid_grad = mid_grad.at[mid_ids].add(mid_part)
        leaf_query, leaf_part = pair_terms(tile_queries, leaf_tile, leaf_tile_ids, leaf_blocks)
        leaf_grad = leaf_grad.at[leaf_tile_ids].add(leaf_part)
        return (coarse_grad, mid_grad, leaf_grad), query_grad + mid_query + leaf_query

    start = (jnp.zeros((COARSE, D), jnp.float32), jnp.zeros((MID_BLOCKS, BLOCK, D), jnp.float32), jnp.zeros((LEAF_BLOCKS, BLOCK, D), jnp.float32))
    inputs = (queries.reshape(TILES, TILE, D), coarse_pos.reshape(TILES, TILE, POS), mid_pos.reshape(TILES, TILE, POS), leaf_pos.reshape(TILES, TILE, POS), mid_cand, leaf_ids)
    totals, query_grads = lax.scan(step, start, inputs)
    coarse_grad, mid_grad, leaf_grad = totals
    return query_grads.reshape(QUERIES, D), coarse_grad, mid_grad.reshape(MIDS, D), leaf_grad.reshape(LEAVES, D)
```

```python
import jax
import jax.numpy as jnp
from jax import lax
from jax.experimental import pallas as pl
from jax.experimental.pallas import tpu as pltpu
from jax.sharding import PartitionSpec as P

TILE = 128
BLOCK = 512
COARSE = 2048
K_CAND = 8
D = 768
NY, NX, NZ = 4, 4, 4
TILES = NX * NZ
BIG = 1 << 20
F32 = jnp.float32
BF16 = jnp.bfloat16
MESH = pl.DeviceIdType.MESH
R0, R1, R2 = (0, 32), (32, 48), (80, 48)
ROWS0, ROWS1, ROWS2 = pl.ds(*R0), pl.ds(*R1), pl.ds(*R2)
THIRD = D // 3
HALF = D // 2


def mm(a, b, ca, cb):
    return lax.dot_general(a, b, (((ca,), (cb,)), ((), ())), preferred_element_type=F32)


def delta_of(scores, labels, positives):
    hit = labels == positives[0:1]
    for p in range(1, 4):
        hit = hit | (labels == positives[p : p + 1])
    return (0.125 * jnp.tanh(0.5 * scores) + jnp.where(hit, -0.125, 0.125)).astype(BF16)


class Place:
    def __init__(self):
        grp, mid = lax.axis_index("grp"), lax.axis_index("mid")
        self.y, self.c = grp // 2, lax.rem(grp, 2)
        self.x, self.z = mid // NZ, lax.rem(mid, NZ)
        self.mid = mid
        self.ahead = 1 + 2 * self.c
        self.behind = 3 - 2 * self.c

    def at(self, dy=0, dx=0, dz=0):
        y, x, z = lax.rem(self.y + dy, NY), lax.rem(self.x + dx, NX), lax.rem(self.z + dz, NZ)
        return (2 * y + self.c, NZ * x + z)

    def sibling(self):
        return (2 * self.y + 1 - self.c, self.mid)

    def tile(self, dx, dz):
        return NZ * lax.rem(self.x + dx, NX) + lax.rem(self.z + dz, NZ)

    def greet(self):
        near = [self.sibling()]
        for step in (self.ahead, self.behind):
            near += [self.at(dy=step), self.at(dx=step), self.at(dz=step)]
        barrier = pltpu.get_barrier_semaphore()
        for device in near:
            pl.semaphore_signal(barrier, inc=1, device_id=device, device_id_type=MESH)
        pl.semaphore_wait(barrier, len(near))


class Net:
    def __init__(self, send_sem, recv_sem):
        self.send_sem, self.recv_sem, self.made = send_sem, recv_sem, []

    def send(self, src, dst, device):
        i = len(self.made)
        copy = pltpu.make_async_remote_copy(
            src_ref=src,
            dst_ref=dst,
            send_sem=self.send_sem.at[i],
            recv_sem=self.recv_sem.at[i],
            device_id=device,
            device_id_type=MESH,
        )
        copy.start()
        self.made.append(copy)
        return copy

    def finish(self):
        for copy in self.made:
            copy.wait_send()


COPIES = 200
OWN, BACK, FRONT, ACROSS = range(4)
SLOTS = 32


def role_step(color, role):
    return (0, 3 - 2 * color, 1 + 2 * color, 2)[role]


def main_kernel(
    q, mp, lp, mc, lc, cp, owner, cv, midv, leafv,
    gq, gco, sel, deltas, plan,
    q_own, q_b, q_a, q_2, p_own, p_b, p_a, p_2, cvv, cvm, cpall, packo, packs, packr,
    metao, metas, metar, planv, planr, plans, planrs, vectors, held_delta, gc, qc,
    own0, own1, own2, own3, sib0, sib1, sib2, sib3, gsib, gbuf,
    s2, sb, r2, rb, ra, u2, ub, ua, w2, wb, wa, local_sem, send_sem, recv_sem,
):
    me = Place()
    c, a, b = me.c, me.ahead, me.behind
    net = Net(send_sem, recv_sem)
    local = []

    def start_local(src, dst):
        copy = pltpu.make_async_copy(src, dst, local_sem.at[len(local)])
        copy.start()
        local.append(copy)
        return copy

    load_q = start_local(q, q_own)
    load_v = [start_local(midv, vectors.at[pl.ds(0, 4)]), start_local(leafv, vectors.at[pl.ds(4, 2)])]
    load_c = start_local(cv, cvv)
    for t in range(TILES):
        p_own[t, 0:4, :] = mp[:, t * TILE : (t + 1) * TILE]
        p_own[t, 4:8, :] = lp[:, t * TILE : (t + 1) * TILE]
    p_own[16:18] = jnp.full((2, 8, 128), -1, jnp.int32)
    p_own[16, :, 0:TILES] = mc[...]
    p_own[17, :, 0:TILES] = lc[...]
    cpall[me.x, me.z, 0:4, :] = cp[...]
    cpall[me.x, me.z, 4:8, :] = cp[...]
    me.greet()

    m = me.mid
    small = pl.ds(R1[0], R1[1] + R2[1])
    up, down = me.at(dy=a), me.at(dy=b)
    xa, xb, za, zb = me.at(dx=a), me.at(dx=b), me.at(dz=a), me.at(dz=b)
    sib = me.sibling()
    planes = {BACK: q_b, FRONT: q_a, ACROSS: q_2}

    y_a = net.send(q.at[m, small], q_b.at[m, small], up)
    y_b = net.send(q.at[m, small], q_a.at[m, small], down)
    at_y = {BACK: y_a, FRONT: y_b}
    pos_own = cpall.at[me.x, me.z]
    cz_a = net.send(pos_own, pos_own, za)
    cz_b = net.send(pos_own, pos_own, zb)
    pr_a = net.send(p_own, p_b, up)
    pr_b = net.send(p_own, p_a, down)

    def bulk(i):
        return pl.ds(4 * i, 4)

    t0_a, t0_b, t0_f = [], [], []

    def bulk_own(i):
        t0_a.append(net.send(q.at[bulk(i), ROWS0], q_b.at[bulk(i), ROWS0], up))
        t0_b.append(net.send(q.at[bulk(i), ROWS0], q_a.at[bulk(i), ROWS0], down))

    def bulk_forward(i):
        t0_a[i].wait_recv()
        t0_f.append(net.send(q_b.at[bulk(i), ROWS0], q_2.at[bulk(i), ROWS0], up))

    bulk_own(0)

    axes = ((ROWS1, za, zb, xa, xb), (ROWS2, xa, xb, za, zb))

    def tile_of(h, first, last):
        return me.tile(last, first) if h == 0 else me.tile(first, last)

    second, second_f, last, last_f = {}, {}, {}, {}
    walk = (0, b, a, 2)

    def send_second(role):
        for h, (rows, to_a, to_b, _, _) in enumerate(axes):
            piece = planes[role].at[m, rows]
            second[role, h] = (net.send(piece, piece, to_a), net.send(piece, piece, to_b))

    def send_last(role, key):
        step = walk[key]
        for h, (rows, _, _, to_a, to_b) in enumerate(axes):
            piece = planes[role].at[tile_of(h, step, 0), rows]
            last[role, h, key] = (net.send(piece, piece, to_a), net.send(piece, piece, to_b))

    def second_stage(role):
        for h, (rows, to_a, _, _, _) in enumerate(axes):
            second[role, h][0].wait_recv()
            piece = planes[role].at[tile_of(h, b, 0), rows]
            second_f[role, h] = net.send(piece, piece, to_a)
        send_last(role, BACK)
        for h in range(2):
            second[role, h][1].wait_recv()
        send_last(role, FRONT)

    def across_stage(role):
        for h in range(2):
            second_f[role, h].wait_recv()
        send_last(role, ACROSS)

    def forward_last(role):
        for key, step in enumerate(walk):
            for h, (rows, _, _, to_a, _) in enumerate(axes):
                last[role, h, key][0].wait_recv()
                piece = planes[role].at[tile_of(h, step, b), rows]
                last_f[role, h, key] = net.send(piece, piece, to_a)

    def complete(role):
        for key in range(4):
            for h in range(2):
                last[role, h, key][1].wait_recv()
                last_f[role, h, key].wait_recv()

    y_a.wait_recv()
    y_f = net.send(q_b.at[m, small], q_2.at[m, small], up)
    send_second(BACK)
    y_b.wait_recv()
    send_second(FRONT)
    cz_a.wait_recv()
    pos_b = cpall.at[me.x, lax.rem(me.z + b, NZ)]
    cz_f = net.send(pos_b, pos_b, za)
    pr_a.wait_recv()
    pr_f = net.send(p_b, p_2, up)
    bulk_own(1)
    send_last(BACK, OWN)
    second_stage(BACK)
    y_f.wait_recv()
    send_second(ACROSS)
    bulk_own(2)
    bulk_own(3)
    across_stage(BACK)
    send_last(FRONT, OWN)
    second_stage(FRONT)
    cz_b.wait_recv()
    cz_f.wait_recv()
    pos_row = cpall.at[me.x]
    cx_a = net.send(pos_row, pos_row, xa)
    cx_b = net.send(pos_row, pos_row, xb)
    bulk_forward(0)
    pr_b.wait_recv()
    pr_f.wait_recv()
    index = lax.broadcasted_iota(jnp.int32, (2, 128), 0) * 128 + lax.broadcasted_iota(
        jnp.int32, (2, 128), 1
    )
    code = 4 * (
        TILES * lax.broadcasted_iota(jnp.int32, (8, 128), 0)
        + lax.broadcasted_iota(jnp.int32, (8, 128), 1)
    )
    lane = lax.broadcasted_iota(jnp.int32, (1, 128), 1)
    tables = {OWN: p_own, BACK: p_b, FRONT: p_a, ACROSS: p_2}
    for which, core in enumerate((c, 1 - c)):
        device = (2 * me.y + core) * TILES + m
        held = [
            jnp.sum(jnp.where(owner[...] == 2 * device + i, index, 0), axis=(0, 1), keepdims=True)
            for i in range(2)
        ]
        for role, table in tables.items():
            mids, leaves = table[16], table[17]
            entries = []
            for live, block in (
                ((mids >> 2) == device, mids & 3),
                ((leaves == held[0]) | (leaves == held[1]), (leaves == held[1]).astype(jnp.int32)),
            ):
                found = code + block
                first = jnp.min(jnp.where(live, found, BIG), axis=(0, 1), keepdims=True)
                final = jnp.max(jnp.where(live, found, -1), axis=(0, 1), keepdims=True)
                some = first < BIG
                entries.append((some, jnp.where(some, first, 0)))
                two = some & (final != first)
                entries.append((two, jnp.where(two, final, 0)))
            tiles = [(value >> 2) & 15 for _, value in entries]
            spots = jnp.full((1, 128), 4, jnp.int32)
            for e in (3, 2, 1, 0):
                spots = jnp.where(entries[e][0] & (tiles[e] == lane), e, spots)
            at = 32 + 4 * which + role
            planv[at : at + 1, :] = spots
            for e, (valid, value) in enumerate(entries):
                slot = jnp.full((1, 1), e, jnp.int32)
                for f in range(e - 1, -1, -1):
                    slot = jnp.where(entries[f][0] & (tiles[f] == tiles[e]), f, slot)
                slot = jnp.where(valid, slot, e)
                row = jnp.where(lane == 0, jnp.where(valid, value & 3, -1), slot)
                row = jnp.where(lane == 2, tiles[e], row)
                row = jnp.where(lane == 3, value >> 6, row)
                row = jnp.where(lane == 4, (value & 3) + 4 * (e // 2), row)
                at = 16 * which + 4 * role + e
                planv[at : at + 1, :] = row

    owns, sibs = (own0, own1, own2, own3), (sib0, sib1, sib2, sib3)
    tiles_of = (q_own, q_b, q_a, q_2)
    notes_of = (p_own, p_b, p_a, p_2)
    labels = lax.broadcasted_iota(jnp.int32, (BLOCK, TILE), 0)
    for role in range(4):
        owns[role][4] = jnp.zeros((TILE, D), BF16)
        sibs[role][4] = jnp.zeros((TILE, D), BF16)
    slot_sends, slot_notes, term_sends = {}, {}, {}

    def pack(role):
        rows, table = tiles_of[role], notes_of[role]
        group = pl.ds(4 * role, 4)
        for which, slots, notes in ((1, packs, metas), (0, packo, metao)):
            for e in range(4):
                at = 4 * role + e
                tile, cand = plans[16 * which + at, 2], plans[16 * which + at, 3]
                slots[at] = rows[tile]
                level = 4 * (e // 2)
                positives = table[tile][level : level + 4] - BLOCK * cand
                notes[at, 0:4, :] = positives
                notes[at, 4:8, :] = positives
            if which:
                slot_sends[role] = net.send(packs.at[group], packr.at[group], sib)
                slot_notes[role] = net.send(metas.at[group], metar.at[group], sib)
        start_local(packo.at[group], sel.at[0, group])

    def pairs(role, which):
        group = pl.ds(4 * role, 4)
        if which == 0:
            slots, notes, table, out, base = packo, metao, plans, owns[role], 0
        else:
            slot_sends[role].wait_recv()
            slot_notes[role].wait_recv()
            slot_sends[role].wait_send()
            start_local(packr.at[group], sel.at[1, group])
            slots, notes, table, out, base = packr, metar, planrs, packs, 4 * role

        def body(e, carry):
            at = 4 * role + e
            block = vectors[table[at, 4]]
            delta = delta_of(mm(block, slots[at], 1, 1), labels, notes[at])
            held_delta[which, at] = delta
            out[base + e] = mm(delta, block, 0, 0).astype(BF16)
            return carry

        lax.fori_loop(0, 4, body, 0)
        start_local(held_delta.at[which, group], deltas.at[which, group])
        for e in range(3):
            value = out[base + e]
            for f in range(e + 1, 4):
                same = table[4 * role + f, 1] == e
                value += jnp.where(same, out[base + f], jnp.zeros((TILE, D), BF16))
            out[base + e] = value
        if which == 1:
            term_sends[role] = net.send(packs.at[group], sibs[role].at[pl.ds(0, 4)], sib)

    steps = (0, b, a, 2)
    first_axis = ((xa, xb), (za, zb))
    first2, firsta, firstb = {}, {}, {}
    second2, seconda, secondb = {}, {}, {}

    def part(h, role, unit, j):
        tile = me.tile(steps[unit], steps[j]) if h == 0 else me.tile(steps[j], steps[unit])
        cols = slice(h * HALF, (h + 1) * HALF)
        mine = owns[role][plans[32 + role, tile], :, cols]
        return mine + sibs[role][plans[36 + role, tile], :, cols]

    def begin_sum(role):
        term_sends[role].wait_recv()
        for h in range(2):
            for j in range(4):
                s2[h, role, j] = part(h, role, ACROSS, j)
            first2[h, role] = net.send(s2.at[h, role], r2.at[h, role], first_axis[h][0])
        for h in range(2):
            for j in range(4):
                sb[h, role, j] = part(h, role, BACK, j)
            firstb[h, role] = net.send(sb.at[h, role], rb.at[h, role], first_axis[h][1])

    def pass_sum(role):
        for h in range(2):
            first2[h, role].wait_recv()
            for j in range(4):
                r2[h, role, j] = r2[h, role, j] + part(h, role, FRONT, j)
            firsta[h, role] = net.send(r2.at[h, role], ra.at[h, role], first_axis[h][0])

    def begin_second(role):
        for h in range(2):
            firstb[h, role].wait_recv()
            firsta[h, role].wait_recv()
            for j in (ACROSS, BACK, FRONT, OWN):
                rb[h, role, j] = part(h, role, OWN, j) + rb[h, role, j] + ra[h, role, j]
                if j == ACROSS:
                    second2[h, role] = net.send(
                        rb.at[h, role, j], u2.at[h, role], first_axis[1 - h][0]
                    )
                if j == BACK:
                    secondb[h, role] = net.send(
                        rb.at[h, role, j], ub.at[h, role], first_axis[1 - h][1]
                    )

    def pass_second(role):
        for h in range(2):
            second2[h, role].wait_recv()
            u2[h, role] = u2[h, role] + rb[h, role, FRONT]
            seconda[h, role] = net.send(u2.at[h, role], ua.at[h, role], first_axis[1 - h][0])

    def end_second(role):
        for h in range(2):
            secondb[h, role].wait_recv()
            seconda[h, role].wait_recv()
            ub[h, role] = rb[h, role, OWN] + ub[h, role] + ua[h, role]


    to_smem = pltpu.make_async_copy(planv, plans, local_sem.at[len(local)])
    local.append(to_smem)
    to_smem.start()
    plan_send = net.send(planv.at[pl.ds(16, 16)], planr, sib)
    to_smem.wait()
    load_q.wait()
    pack(OWN)
    across_stage(FRONT)
    send_last(ACROSS, OWN)
    forward_last(BACK)
    second_stage(ACROSS)
    bulk_forward(1)
    across_stage(ACROSS)
    for load in load_v:
        load.wait()
    pairs(OWN, 0)
    cx_a.wait_recv()
    pos_row_b = cpall.at[lax.rem(me.x + b, NX)]
    cx_f = net.send(pos_row_b, pos_row_b, xa)
    bulk_forward(2)
    forward_last(FRONT)
    plan_send.wait_recv()
    plan_in = start_local(planr, planrs)
    plan_in.wait()
    pairs(OWN, 1)
    bulk_forward(3)
    forward_last(ACROSS)
    for i in range(4):
        t0_b[i].wait_recv()
    complete(BACK)
    pack(BACK)
    begin_sum(OWN)
    pairs(BACK, 0)
    complete(FRONT)
    pack(FRONT)
    pairs(BACK, 1)
    pass_sum(OWN)
    begin_sum(BACK)
    pairs(FRONT, 0)
    for i in range(4):
        t0_f[i].wait_recv()
    complete(ACROSS)
    pack(ACROSS)
    pairs(FRONT, 1)
    begin_second(OWN)
    pass_sum(BACK)
    begin_sum(FRONT)
    pairs(ACROSS, 0)
    load_c.wait()
    for j in range(8):
        color, role = j // 4, j % 4
        row = (2 * lax.rem(me.y + role_step(color, role), NY) + color) * TILES + m
        start = pl.multiple_of(row * 16, 16)
        cvm[pl.ds(16 * j, 16), :] = cvv[pl.ds(start, 16), :]
    place = lax.broadcasted_iota(jnp.int32, (128, 128), 0)
    chunk = place // 16
    color, role = chunk // 4, lax.rem(chunk, 4)
    step = jnp.where(role == ACROSS, 2, jnp.where(role == FRONT, 1 + 2 * color, 3 - 2 * color))
    step = jnp.where(role == OWN, 0, step)
    owner_grp = 2 * lax.rem(me.y + step, NY) + color
    coarse_ids = (owner_grp * TILES + m) * 16 + lax.rem(place, 16)

    def own_coarse():
        qm = q_own[m]
        total = jnp.zeros((TILE, D), F32)
        for i in range(COARSE // BLOCK):
            vectors = cvv[i * BLOCK : (i + 1) * BLOCK, :]
            labels = lax.broadcasted_iota(jnp.int32, (BLOCK, TILE), 0) + i * BLOCK
            delta = delta_of(mm(vectors, qm, 1, 1), labels, cpall[me.x, me.z])
            total += mm(delta, vectors, 0, 0)
        qc[...] = total

    def rows_coarse(lo, hi):
        def body(t, carry):
            qt = q_own[t]
            delta = delta_of(mm(cvm[...], qt, 1, 1), coarse_ids, cpall[t // NZ, lax.rem(t, NZ)])
            gc[...] += mm(delta, qt, 1, 0)
            return carry

        lax.fori_loop(lo, hi, body, 0)


    gc[...] = jnp.zeros_like(gc)
    pass_second(OWN)
    begin_second(BACK)
    pairs(ACROSS, 1)
    pass_sum(FRONT)
    own_coarse()
    begin_sum(ACROSS)
    end_second(OWN)
    pass_second(BACK)
    cx_b.wait_recv()
    cx_f.wait_recv()
    rows_coarse(0, 8)
    pass_sum(ACROSS)
    begin_second(FRONT)
    rows_coarse(8, 16)
    coarse = net.send(gc.at[pl.ds(64 * (1 - c), 64)], gsib, sib)
    pass_second(FRONT)
    begin_second(ACROSS)
    end_second(BACK)
    third_b = net.send(ub.at[:, BACK], wb, down)
    end_second(FRONT)
    coarse.wait_recv()
    for role in range(4):
        gbuf[role] = gc[pl.ds(64 * c + 16 * role, 16)] + gsib[16 * role : 16 * role + 16]
    coarse2 = net.send(gbuf.at[ACROSS], gbuf.at[5], up)
    coarseb = net.send(gbuf.at[BACK], gbuf.at[6], down)
    pass_second(ACROSS)
    coarse2.wait_recv()
    gbuf[4] = gbuf[FRONT] + gbuf[5]
    coarsea = net.send(gbuf.at[4], gbuf.at[7], up)
    end_second(ACROSS)

    third_2 = net.send(ub.at[:, ACROSS], w2, up)
    coarsea.wait_recv()
    coarseb.wait_recv()
    gco[...] = gbuf[OWN] + gbuf[6] + gbuf[7]
    start_local(planv.at[pl.ds(0, 16)], plan.at[0])
    start_local(planr, plan.at[1])
    third_2.wait_recv()
    w2[...] = w2[...] + ub[:, FRONT]
    third_a = net.send(w2, wa, up)
    third_b.wait_recv()
    third_a.wait_recv()
    for h in range(2):
        cols = slice(h * HALF, (h + 1) * HALF)
        gq[:, cols] = (
            qc[:, cols] + ub[h, OWN].astype(F32) + wb[h].astype(F32) + wa[h].astype(F32)
        )
    waited = [load_q, load_c, to_smem, plan_in] + load_v
    for copy in local:
        if not any(copy is done for done in waited):
            copy.wait()
    for copy in net.made:
        if not any(copy is done for done in slot_sends.values()):
            copy.wait_send()


PLACES = SLOTS + 6


def grads_kernel(
    plan, sel, deltas,
    gm, gl,
    counts, bases, entries, rows, held, acc, row_sem, delta_sem, grad_sem,
):
    stores = [(gm, 0), (gm, 1), (gm, 2), (gm, 3), (gl, 0), (gl, 1)]
    for key in range(6):
        counts[key] = 0

    def key_of(e):
        return plan[e // 16, lax.rem(e, 16), 0] + 4 * lax.rem(e // 2, 2)

    def live(e):
        return plan[e // 16, lax.rem(e, 16), 0] >= 0

    def count(e, carry):
        @pl.when(live(e))
        def _():
            counts[key_of(e)] += 1

        return carry

    lax.fori_loop(0, SLOTS, count, 0)
    base = 0
    for key in range(6):
        bases[key] = base
        n = counts[key]
        base += n + lax.rem(n, 2)
        counts[key] = 0

    def row_copy(e, at):
        return pltpu.make_async_copy(sel.at[e // 16, lax.rem(e, 16)], rows.at[at], row_sem.at[at])

    def delta_copy(e, at):
        return pltpu.make_async_copy(
            deltas.at[e // 16, lax.rem(e, 16)], held.at[at], delta_sem.at[at]
        )

    def register(e, carry):
        @pl.when(live(e))
        def _():
            key = key_of(e)
            n = counts[key]
            at = bases[key] + n
            entries[at] = e
            counts[key] = n + 1
            row_copy(e, at).start()
            delta_copy(e, at).start()

        return carry

    lax.fori_loop(0, SLOTS, register, 0)

    def per_key(key, carry):
        n = counts[key]
        start = bases[key]

        @pl.when(n == 0)
        def _():
            acc[key] = jnp.zeros((BLOCK, D), F32)

        def batch(i, inner):
            at = start + 2 * i
            full = 2 * i + 1 < n
            row_copy(entries[at], at).wait()
            delta_copy(entries[at], at).wait()

            @pl.when(full)
            def _():
                row_copy(entries[at + 1], at + 1).wait()
                delta_copy(entries[at + 1], at + 1).wait()

            @pl.when(jnp.logical_not(full))
            def _():
                rows[at + 1] = jnp.zeros((TILE, D), BF16)
                held[at + 1] = jnp.zeros((BLOCK, TILE), BF16)

            both = rows[pl.ds(at, 2)].reshape(2 * TILE, D)
            delta = jnp.concatenate([held[at], held[at + 1]], axis=1)

            @pl.when(i == 0)
            def _():
                for n_col in range(3):
                    cols = slice(n_col * THIRD, (n_col + 1) * THIRD)
                    acc[key, :, cols] = mm(delta, both[:, cols], 1, 0)

            @pl.when(i != 0)
            def _():
                for n_col in range(3):
                    cols = slice(n_col * THIRD, (n_col + 1) * THIRD)
                    acc[key, :, cols] += mm(delta, both[:, cols], 1, 0)

            return inner

        lax.fori_loop(0, (n + 1) // 2, batch, 0)
        for i, (out, j) in enumerate(stores):

            @pl.when(key == i)
            def _():
                pltpu.make_async_copy(acc.at[i], out.at[j], grad_sem.at[i]).start()

        return carry

    lax.fori_loop(0, 6, per_key, 0)
    for i, (out, j) in enumerate(stores):
        pltpu.make_async_copy(acc.at[i], out.at[j], grad_sem.at[i]).wait()


def vmem():
    return pl.BlockSpec(memory_space=pltpu.VMEM)


def smem():
    return pl.BlockSpec(memory_space=pltpu.SMEM)


def hbm():
    return pl.BlockSpec(memory_space=pl.ANY)


def shape(dims, dtype):
    return jax.ShapeDtypeStruct(dims, dtype)


def shards(
    queries,
    coarse_vectors,
    mid_vectors,
    leaf_vectors,
    coarse_pos,
    mid_pos,
    leaf_pos,
    mid_cand,
    leaf_cand,
    leaf_owner,
):
    dma = pltpu.SemaphoreType.DMA
    mib = 1024 * 1024
    group = pltpu.VMEM((TILES, TILE, D), BF16)
    notes = pltpu.VMEM((18, 8, 128), jnp.int32)
    packed = pltpu.VMEM((16, TILE, D), BF16)
    packed_notes = pltpu.VMEM((16, 8, 128), jnp.int32)
    slots = pltpu.VMEM((5, TILE, D), BF16)
    first = pltpu.VMEM((2, 4, 4, TILE, HALF), BF16)
    second = pltpu.VMEM((2, 4, TILE, HALF), BF16)
    third = pltpu.VMEM((2, TILE, HALF), BF16)
    gq, gco, sel, deltas, plan = pl.pallas_call(
        main_kernel,
        out_shape=(
            shape((TILE, D), F32),
            shape((16, D), F32),
            shape((2, 16, TILE, D), BF16),
            shape((2, 16, BLOCK, TILE), BF16),
            shape((2, 16, 128), jnp.int32),
        ),
        in_specs=[hbm(), vmem(), vmem(), vmem(), vmem(), vmem(), vmem(), hbm(), hbm(), hbm()],
        out_specs=(vmem(), vmem(), hbm(), hbm(), hbm()),
        scratch_shapes=[
            group, group, group, group,
            notes, notes, notes, notes,
            pltpu.VMEM((COARSE, D), BF16),
            pltpu.VMEM((128, D), BF16),
            pltpu.VMEM((NX, NZ, 8, TILE), jnp.int32),
            packed, packed, packed, packed_notes, packed_notes, packed_notes,
            pltpu.VMEM((40, 128), jnp.int32),
            pltpu.VMEM((16, 128), jnp.int32),
            pltpu.SMEM((40, 128), jnp.int32),
            pltpu.SMEM((16, 128), jnp.int32),
            pltpu.VMEM((6, BLOCK, D), BF16),
            pltpu.VMEM((2, 16, BLOCK, TILE), BF16),
            pltpu.VMEM((128, D), F32),
            pltpu.VMEM((TILE, D), F32),
            slots, slots, slots, slots, slots, slots, slots, slots,
            pltpu.VMEM((64, D), F32),
            pltpu.VMEM((8, 16, D), F32),
            first, first, first, first, first,
            second, second, second,
            third, third, third,
            dma((32,)),
            dma((COPIES,)),
            dma((COPIES,)),
        ],
        compiler_params=pltpu.CompilerParams(
            collective_id=0, has_side_effects=True, vmem_limit_bytes=63 * mib
        ),
        name="main",
    )(
        queries.reshape(TILES, TILE, D),
        mid_pos.T,
        leaf_pos.T,
        mid_cand.T,
        leaf_cand.T,
        coarse_pos.T,
        leaf_owner.reshape(2, 128),
        coarse_vectors,
        mid_vectors.reshape(4, BLOCK, D),
        leaf_vectors.reshape(2, BLOCK, D),
    )
    gm, gl = pl.pallas_call(
        grads_kernel,
        out_shape=(shape((4, BLOCK, D), F32), shape((2, BLOCK, D), F32)),
        in_specs=[smem(), hbm(), hbm()],
        out_specs=(hbm(), hbm()),
        scratch_shapes=[
            pltpu.SMEM((6,), jnp.int32),
            pltpu.SMEM((6,), jnp.int32),
            pltpu.SMEM((PLACES,), jnp.int32),
            pltpu.VMEM((PLACES, TILE, D), BF16),
            pltpu.VMEM((PLACES, BLOCK, TILE), BF16),
            pltpu.VMEM((6, BLOCK, D), F32),
            dma((PLACES,)),
            dma((PLACES,)),
            dma((6,)),
        ],
        compiler_params=pltpu.CompilerParams(vmem_limit_bytes=40 * mib),
        name="grads",
    )(plan, sel, deltas)
    return gq, gco, gm.reshape(4 * BLOCK, D), gl.reshape(2 * BLOCK, D)


def solution(mesh):
    placed = (
        P("grp", None),
        P(),
        P(("grp", "mid"), None),
        P(("grp", "mid"), None),
        P(("grp", "mid"), None),
        P("grp", None),
        P("grp", None),
        P("grp", None),
        P("grp", None),
        P(),
    )
    return jax.shard_map(
        shards,
        mesh=mesh,
        in_specs=placed,
        out_specs=(
            P(("grp", "mid"), None),
            P(("grp", "mid"), None),
            P(("grp", "mid"), None),
            P(("grp", "mid"), None),
        ),
        check_vma=False,
    )
```

```python
import jax
import jax.numpy as jnp
from jax import lax
from jax.experimental import pallas as pl
from jax.experimental.pallas import tpu as pltpu
from jax.sharding import PartitionSpec as P

TILE = 128
BLOCK = 512
COARSE = 2048
K_CAND = 8
D = 768
NY, NX, NZ = 4, 4, 4
TILES = NX * NZ
BIG = 1 << 20
F32 = jnp.float32
BF16 = jnp.bfloat16
MESH = pl.DeviceIdType.MESH
R0, R1, R2 = (0, 32), (32, 48), (80, 48)
ROWS0, ROWS1, ROWS2 = pl.ds(*R0), pl.ds(*R1), pl.ds(*R2)
THIRD = D // 3


def mm(a, b, ca, cb):
    return lax.dot_general(a, b, (((ca,), (cb,)), ((), ())), preferred_element_type=F32)


def delta_of(scores, labels, positives):
    hit = labels == positives[0:1]
    for p in range(1, 4):
        hit = hit | (labels == positives[p : p + 1])
    return (0.125 * jnp.tanh(0.5 * scores) + jnp.where(hit, -0.125, 0.125)).astype(BF16)


class Place:
    def __init__(self):
        grp, mid = lax.axis_index("grp"), lax.axis_index("mid")
        self.y, self.c = grp // 2, lax.rem(grp, 2)
        self.x, self.z = mid // NZ, lax.rem(mid, NZ)
        self.mid = mid
        self.ahead = 1 + 2 * self.c
        self.behind = 3 - 2 * self.c

    def at(self, dy=0, dx=0, dz=0):
        y, x, z = lax.rem(self.y + dy, NY), lax.rem(self.x + dx, NX), lax.rem(self.z + dz, NZ)
        return (2 * y + self.c, NZ * x + z)

    def sibling(self):
        return (2 * self.y + 1 - self.c, self.mid)

    def tile(self, dx, dz):
        return NZ * lax.rem(self.x + dx, NX) + lax.rem(self.z + dz, NZ)

    def greet(self):
        near = [self.sibling()]
        for step in (self.ahead, self.behind):
            near += [self.at(dy=step), self.at(dx=step), self.at(dz=step)]
        barrier = pltpu.get_barrier_semaphore()
        for device in near:
            pl.semaphore_signal(barrier, inc=1, device_id=device, device_id_type=MESH)
        pl.semaphore_wait(barrier, len(near))


class Net:
    def __init__(self, send_sem, recv_sem):
        self.send_sem, self.recv_sem, self.made = send_sem, recv_sem, []

    def send(self, src, dst, device):
        i = len(self.made)
        copy = pltpu.make_async_remote_copy(
            src_ref=src,
            dst_ref=dst,
            send_sem=self.send_sem.at[i],
            recv_sem=self.recv_sem.at[i],
            device_id=device,
            device_id_type=MESH,
        )
        copy.start()
        self.made.append(copy)
        return copy

    def finish(self):
        for copy in self.made:
            copy.wait_send()


GATHER_COPIES = 128
OWN, BACK, FRONT, ACROSS = range(4)


def role_step(color, role):
    return (0, 3 - 2 * color, 1 + 2 * color, 2)[role]


def gather_kernel(
    q, mp, lp, mc, lc, cp, owner, cv,
    sel, meta, plan, tbl, gc, qc,
    q_own, q_b, q_a, q_2, p_own, p_b, p_a, p_2, cvv, cvm, cpall, packo, packs, metao, metas,
    planv, plans, local_sem, send_sem, recv_sem,
):
    me = Place()
    c, a, b = me.c, me.ahead, me.behind
    net = Net(send_sem, recv_sem)
    loads = [
        pltpu.make_async_copy(q, q_own, local_sem.at[0]),
        pltpu.make_async_copy(cv, cvv, local_sem.at[1]),
    ]
    for load in loads:
        load.start()
    for t in range(TILES):
        p_own[t, 0:4, :] = mp[:, t * TILE : (t + 1) * TILE]
        p_own[t, 4:8, :] = lp[:, t * TILE : (t + 1) * TILE]
    p_own[16:18] = jnp.full((2, 8, 128), -1, jnp.int32)
    p_own[16, :, 0:TILES] = mc[...]
    p_own[17, :, 0:TILES] = lc[...]
    cpall[me.x, me.z, 0:4, :] = cp[...]
    cpall[me.x, me.z, 4:8, :] = cp[...]
    me.greet()

    m = me.mid
    small = pl.ds(R1[0], R1[1] + R2[1])
    up, down = me.at(dy=a), me.at(dy=b)
    xa, xb, za, zb = me.at(dx=a), me.at(dx=b), me.at(dz=a), me.at(dz=b)
    sib = me.sibling()
    planes = {BACK: q_b, FRONT: q_a, ACROSS: q_2}

    y_a = net.send(q.at[m, small], q_b.at[m, small], up)
    y_b = net.send(q.at[m, small], q_a.at[m, small], down)
    at_y = {BACK: y_a, FRONT: y_b}
    pos_own = cpall.at[me.x, me.z]
    cz_a = net.send(pos_own, pos_own, za)
    cz_b = net.send(pos_own, pos_own, zb)
    pr_a = net.send(p_own, p_b, up)
    pr_b = net.send(p_own, p_a, down)

    def bulk(i):
        return pl.ds(4 * i, 4)

    t0_a, t0_b, t0_f = [], [], []

    def bulk_own(i):
        t0_a.append(net.send(q.at[bulk(i), ROWS0], q_b.at[bulk(i), ROWS0], up))
        t0_b.append(net.send(q.at[bulk(i), ROWS0], q_a.at[bulk(i), ROWS0], down))

    def bulk_forward(i):
        t0_a[i].wait_recv()
        t0_f.append(net.send(q_b.at[bulk(i), ROWS0], q_2.at[bulk(i), ROWS0], up))

    bulk_own(0)

    axes = ((ROWS1, za, zb, xa, xb), (ROWS2, xa, xb, za, zb))

    def tile_of(h, first, last):
        return me.tile(last, first) if h == 0 else me.tile(first, last)

    second, second_f, last, last_f = {}, {}, {}, {}
    walk = (0, b, a, 2)

    def send_second(role):
        for h, (rows, to_a, to_b, _, _) in enumerate(axes):
            piece = planes[role].at[m, rows]
            second[role, h] = (net.send(piece, piece, to_a), net.send(piece, piece, to_b))

    def send_last(role, key):
        step = walk[key]
        for h, (rows, _, _, to_a, to_b) in enumerate(axes):
            piece = planes[role].at[tile_of(h, step, 0), rows]
            last[role, h, key] = (net.send(piece, piece, to_a), net.send(piece, piece, to_b))

    def second_stage(role):
        for h, (rows, to_a, _, _, _) in enumerate(axes):
            second[role, h][0].wait_recv()
            piece = planes[role].at[tile_of(h, b, 0), rows]
            second_f[role, h] = net.send(piece, piece, to_a)
        send_last(role, BACK)
        for h in range(2):
            second[role, h][1].wait_recv()
        send_last(role, FRONT)

    def across_stage(role):
        for h in range(2):
            second_f[role, h].wait_recv()
        send_last(role, ACROSS)

    def forward_last(role):
        for key, step in enumerate(walk):
            for h, (rows, _, _, to_a, _) in enumerate(axes):
                last[role, h, key][0].wait_recv()
                piece = planes[role].at[tile_of(h, step, b), rows]
                last_f[role, h, key] = net.send(piece, piece, to_a)

    def complete(role):
        for key in range(4):
            for h in range(2):
                last[role, h, key][1].wait_recv()
                last_f[role, h, key].wait_recv()

    y_a.wait_recv()
    y_f = net.send(q_b.at[m, small], q_2.at[m, small], up)
    send_second(BACK)
    y_b.wait_recv()
    send_second(FRONT)
    cz_a.wait_recv()
    pos_b = cpall.at[me.x, lax.rem(me.z + b, NZ)]
    cz_f = net.send(pos_b, pos_b, za)
    pr_a.wait_recv()
    pr_f = net.send(p_b, p_2, up)
    bulk_own(1)
    send_last(BACK, OWN)
    second_stage(BACK)
    y_f.wait_recv()
    send_second(ACROSS)
    bulk_own(2)
    bulk_own(3)
    across_stage(BACK)
    send_last(FRONT, OWN)
    second_stage(FRONT)
    cz_b.wait_recv()
    cz_f.wait_recv()
    pos_row = cpall.at[me.x]
    cx_a = net.send(pos_row, pos_row, xa)
    cx_b = net.send(pos_row, pos_row, xb)
    bulk_forward(0)
    across_stage(FRONT)
    send_last(ACROSS, OWN)
    forward_last(BACK)
    second_stage(ACROSS)
    bulk_forward(1)
    across_stage(ACROSS)
    bulk_forward(2)
    forward_last(FRONT)
    bulk_forward(3)

    pr_b.wait_recv()
    pr_f.wait_recv()
    index = lax.broadcasted_iota(jnp.int32, (2, 128), 0) * 128 + lax.broadcasted_iota(
        jnp.int32, (2, 128), 1
    )
    code = 4 * (
        TILES * lax.broadcasted_iota(jnp.int32, (8, 128), 0)
        + lax.broadcasted_iota(jnp.int32, (8, 128), 1)
    )
    lane = lax.broadcasted_iota(jnp.int32, (1, 128), 1)
    tables = {OWN: p_own, BACK: p_b, FRONT: p_a, ACROSS: p_2}
    for which, core in enumerate((c, 1 - c)):
        device = (2 * me.y + core) * TILES + m
        held = [
            jnp.sum(jnp.where(owner[...] == 2 * device + i, index, 0), axis=(0, 1), keepdims=True)
            for i in range(2)
        ]
        for role, table in tables.items():
            mids, leaves = table[16], table[17]
            entries = []
            for live, block in (
                ((mids >> 2) == device, mids & 3),
                ((leaves == held[0]) | (leaves == held[1]), (leaves == held[1]).astype(jnp.int32)),
            ):
                found = code + block
                first = jnp.min(jnp.where(live, found, BIG), axis=(0, 1), keepdims=True)
                final = jnp.max(jnp.where(live, found, -1), axis=(0, 1), keepdims=True)
                some = first < BIG
                entries.append((some, jnp.where(some, first, 0)))
                two = some & (final != first)
                entries.append((two, jnp.where(two, final, 0)))
            tiles = [(value >> 2) & 15 for _, value in entries]
            spots = jnp.full((1, 128), 4, jnp.int32)
            for e in (3, 2, 1, 0):
                spots = jnp.where(entries[e][0] & (tiles[e] == lane), e, spots)
            tbl[4 * which + role : 4 * which + role + 1, :] = spots
            for e, (valid, value) in enumerate(entries):
                slot = jnp.full((1, 1), e, jnp.int32)
                alone = jnp.full((1, 1), 1, jnp.int32)
                for f in range(3, -1, -1):
                    if f != e:
                        same = valid & entries[f][0] & (tiles[f] == tiles[e])
                        alone = jnp.where(same, 0, alone)
                        if f < e:
                            slot = jnp.where(same, f, slot)
                row = jnp.where(lane == 0, jnp.where(valid, value & 3, -1), slot + 4 * role)
                row = jnp.where(lane == 2, tiles[e], row)
                row = jnp.where(lane == 3, value >> 6, row)
                row = jnp.where(lane == 4, alone, row)
                at = 16 * which + 4 * role + e
                planv[at : at + 1, :] = row
    to_smem = pltpu.make_async_copy(planv, plans, local_sem.at[2])
    to_smem.start()
    for load in loads:
        load.wait()
    to_smem.wait()
    stored = [pltpu.make_async_copy(planv.at[pl.ds(0, 16)], plan.at[c], local_sem.at[3])]
    stored[0].start()
    arrivals = [net.send(planv.at[pl.ds(16, 16)], plan.at[c], sib)]

    def pack(role, rows, table):
        for which, (slots, notes) in enumerate(((packo, metao), (packs, metas))):
            for e in range(4):
                at = 4 * role + e
                tile, cand = plans[16 * which + at, 2], plans[16 * which + at, 3]
                slots[at] = rows[tile]
                level = 4 * (e // 2)
                positives = table[tile][level : level + 4] - BLOCK * cand
                notes[at, 0:4, :] = positives
                notes[at, 4:8, :] = positives
        group = pl.ds(4 * role, 4)
        arrivals.append(net.send(packs.at[group], sel.at[c, group], sib))
        own = pltpu.make_async_copy(packo.at[group], sel.at[c, group], local_sem.at[4 + role])
        own.start()
        stored.append(own)

    pack(OWN, q_own, p_own)
    cx_a.wait_recv()
    pos_row_b = cpall.at[lax.rem(me.x + b, NX)]
    cx_f = net.send(pos_row_b, pos_row_b, xa)
    forward_last(ACROSS)

    for j in range(8):
        color, role = j // 4, j % 4
        row = (2 * lax.rem(me.y + role_step(color, role), NY) + color) * TILES + m
        start = pl.multiple_of(row * 16, 16)
        cvm[pl.ds(16 * j, 16), :] = cvv[pl.ds(start, 16), :]
    place = lax.broadcasted_iota(jnp.int32, (128, 128), 0)
    chunk = place // 16
    color, role = chunk // 4, lax.rem(chunk, 4)
    step = jnp.where(role == ACROSS, 2, jnp.where(role == FRONT, 1 + 2 * color, 3 - 2 * color))
    step = jnp.where(role == OWN, 0, step)
    owner_grp = 2 * lax.rem(me.y + step, NY) + color
    coarse_ids = (owner_grp * TILES + m) * 16 + lax.rem(place, 16)

    def own_coarse():
        qm = q_own[m]
        total = jnp.zeros((TILE, D), F32)
        for i in range(COARSE // BLOCK):
            vectors = cvv[i * BLOCK : (i + 1) * BLOCK, :]
            labels = lax.broadcasted_iota(jnp.int32, (BLOCK, TILE), 0) + i * BLOCK
            delta = delta_of(mm(vectors, qm, 1, 1), labels, cpall[me.x, me.z])
            total += mm(delta, vectors, 0, 0)
        qc[...] = total

    def rows_coarse(lo, hi):
        def body(t, carry):
            qt = q_own[t]
            delta = delta_of(mm(cvm[...], qt, 1, 1), coarse_ids, cpall[t // NZ, lax.rem(t, NZ)])
            gc[...] += mm(delta, qt, 1, 0)
            return carry

        lax.fori_loop(lo, hi, body, 0)

    gc[...] = jnp.zeros_like(gc)
    for i in range(4):
        t0_b[i].wait_recv()
    complete(BACK)
    pack(BACK, q_b, p_b)
    own_coarse()
    complete(FRONT)
    pack(FRONT, q_a, p_a)
    cx_b.wait_recv()
    cx_f.wait_recv()
    rows_coarse(0, 8)
    for i in range(4):
        t0_f[i].wait_recv()
    complete(ACROSS)
    pack(ACROSS, q_2, p_2)
    arrivals.append(net.send(metas, meta.at[c], sib))
    notes = pltpu.make_async_copy(metao, meta.at[c], local_sem.at[8])
    notes.start()
    stored.append(notes)
    rows_coarse(8, 16)
    for copy in stored:
        copy.wait()
    for copy in arrivals:
        copy.wait_recv()
    net.finish()


SLOTS = 32
LIST = 16


def local_kernel(
    plan, meta, midv, leafv, sel,
    gm, gl, qt,
    counts, entries, begun, rows, vectors, acc, terms, row_sem, vec_sem, grad_sem, term_sem,
):
    stores = [(gm, 0), (gm, 1), (gm, 2), (gm, 3), (gl, 0), (gl, 1)]

    def row_copy(e):
        return pltpu.make_async_copy(sel.at[e], rows.at[e], row_sem.at[e])

    def term_copy(e):
        return pltpu.make_async_copy(terms.at[e], qt.at[e], term_sem.at[e])

    for key in range(6):
        counts[key] = 0
    for e in range(SLOTS):
        block = plan[e, 0]
        begun[e] = 0

        @pl.when(block >= 0)
        def _():
            row_copy(e).start()
            key = block + 4 * (e // 2 % 2)
            n = counts[key]
            entries[LIST * key + n] = e
            counts[key] = n + 1

    for key, (src, i) in enumerate([(midv, i) for i in range(4)] + [(leafv, i) for i in range(2)]):
        pltpu.make_async_copy(src.at[i], vectors.at[key], vec_sem.at[key]).start()
    rows[SLOTS] = jnp.zeros((TILE, D), BF16)
    labels = lax.broadcasted_iota(jnp.int32, (BLOCK, TILE), 0)

    def put(e, value):
        slot = (e & 16) + plan[e, 1]

        @pl.when(begun[slot] == 0)
        def _():
            terms[slot] = value.astype(BF16)

        @pl.when(begun[slot] != 0)
        def _():
            terms[slot] = (terms[slot].astype(F32) + value).astype(BF16)

        begun[slot] = 1

        @pl.when(plan[e, 4] == 1)
        def _():
            term_copy(e).start()

    def per_key(key, carry):
        n = counts[key]
        start = LIST * key
        pltpu.make_async_copy(leafv.at[0], vectors.at[key], vec_sem.at[key]).wait()

        @pl.when(n == 0)
        def _():
            acc[key] = jnp.zeros((BLOCK, D), F32)

        def batch(i, inner):
            at = start + 2 * i
            full = 2 * i + 1 < n
            e0 = entries[at]
            e1 = jnp.where(full, entries[at + 1], SLOTS)
            row_copy(e0).wait()

            @pl.when(full)
            def _():
                row_copy(e1).wait()

            block = vectors[key]
            both = jnp.concatenate([rows[e0], rows[e1]], axis=0)
            scores = mm(block, both, 1, 1)
            delta = jnp.concatenate(
                [
                    delta_of(scores[:, 0:TILE], labels, meta[e0]),
                    delta_of(scores[:, TILE : 2 * TILE], labels, meta[jnp.minimum(e1, SLOTS - 1)]),
                ],
                axis=1,
            )

            @pl.when(i == 0)
            def _():
                for n_col in range(3):
                    cols = slice(n_col * THIRD, (n_col + 1) * THIRD)
                    acc[key, :, cols] = mm(delta, both[:, cols], 1, 0)

            @pl.when(i != 0)
            def _():
                for n_col in range(3):
                    cols = slice(n_col * THIRD, (n_col + 1) * THIRD)
                    acc[key, :, cols] += mm(delta, both[:, cols], 1, 0)

            term = mm(delta, block, 0, 0)
            put(e0, term[0:TILE])

            @pl.when(full)
            def _():
                put(e1, term[TILE : 2 * TILE])

            return inner

        lax.fori_loop(0, (n + 1) // 2, batch, 0)
        for i, (out, j) in enumerate(stores):

            @pl.when(key == i)
            def _():
                pltpu.make_async_copy(acc.at[i], out.at[j], grad_sem.at[i]).start()

        return carry

    lax.fori_loop(0, 6, per_key, 0)
    for e in range(SLOTS):

        @pl.when((plan[e, 0] >= 0) & (plan[e, 4] == 0) & (begun[e] != 0))
        def _():
            term_copy(e).start()

    for e in range(SLOTS):

        @pl.when(begun[e] != 0)
        def _():
            term_copy(e).wait()

    for i, (out, j) in enumerate(stores):
        pltpu.make_async_copy(acc.at[i], out.at[j], grad_sem.at[i]).wait()


SCATTER_COPIES = 80


def scatter_kernel(
    tbl, qt, gcp, qc,
    gq, gco,
    own0, own1, own2, own3, sib0, sib1, sib2, sib3, gsib, gbuf,
    s2, sb, r2, rb, ra, u2, ub, ua, w2, wb, wa, local_sem, send_sem, recv_sem,
):
    me = Place()
    c, a, b = me.c, me.ahead, me.behind
    far = 1 - c
    net = Net(send_sem, recv_sem)
    owns, sibs = (own0, own1, own2, own3), (sib0, sib1, sib2, sib3)
    order = (ACROSS, BACK, FRONT, OWN)
    loads = {}
    for role in order:
        loads[role] = pltpu.make_async_copy(
            qt.at[c, pl.ds(4 * role, 4)], owns[role].at[pl.ds(0, 4)], local_sem.at[role]
        )
        loads[role].start()
    for role in order:
        owns[role][4] = jnp.zeros((TILE, D), BF16)
        sibs[role][4] = jnp.zeros((TILE, D), BF16)
    me.greet()
    sib = me.sibling()
    halves = {}
    for role in order:
        halves[role] = net.send(
            qt.at[far, pl.ds(4 * role, 4)], sibs[role].at[pl.ds(0, 4)], sib
        )
    coarse = net.send(gcp.at[far], gsib.at[pl.ds(0, 4)], sib)
    ahead = [me.at(dy=a), me.at(dx=a), me.at(dz=a)]
    behind = [me.at(dy=b), me.at(dx=b), me.at(dz=b)]
    steps = (0, b, a, 2)
    orders = ((0, 1, 2), (1, 2, 0), (2, 0, 1))

    def chunk(k, *units):
        at = [0, 0, 0]
        for axis, unit in zip(orders[k], units):
            at[axis] = unit
        role, tile = at[0], me.tile(steps[at[1]], steps[at[2]])
        cols = slice(k * THIRD, (k + 1) * THIRD)
        return owns[role][tbl[role, tile], :, cols] + sibs[role][tbl[4 + role, tile], :, cols]

    first2, firsta, firstb = {}, {}, {}

    def start2(k, i):
        for j in range(4):
            s2[k, i, j] = chunk(k, ACROSS, i, j)
        first2[k, i] = net.send(s2.at[k, i], r2.at[k, i], ahead[orders[k][0]])

    def startb(k, i):
        for j in range(4):
            sb[k, i, j] = chunk(k, BACK, i, j)
        firstb[k, i] = net.send(sb.at[k, i], rb.at[k, i], behind[orders[k][0]])

    def starta(k, i):
        first2[k, i].wait_recv()
        for j in range(4):
            r2[k, i, j] = r2[k, i, j] + chunk(k, FRONT, i, j)
        firsta[k, i] = net.send(r2.at[k, i], ra.at[k, i], ahead[orders[k][0]])

    def arrive(role):
        loads[role].wait()
        halves[role].wait_recv()

    arrive(ACROSS)
    for i in order:
        start2(0, i)
    arrive(BACK)
    for i in order:
        startb(0, i)
    arrive(FRONT)
    arrive(OWN)
    for i in order:
        for k in (1, 2):
            start2(k, i)
            startb(k, i)

    coarse.wait_recv()
    for role in range(4):
        gbuf[role] = gcp[c, role] + gsib[role]
    coarse2 = net.send(gbuf.at[ACROSS], gsib.at[4], ahead[0])
    coarseb = net.send(gbuf.at[BACK], gsib.at[5], behind[0])
    for i in order:
        for k in range(3):
            starta(k, i)
    coarse2.wait_recv()
    gbuf[4] = gbuf[FRONT] + gsib[4]
    coarsea = net.send(gbuf.at[4], gsib.at[6], ahead[0])

    second2, seconda, secondb = {}, {}, {}
    for i in order:
        for k in range(3):
            firstb[k, i].wait_recv()
            firsta[k, i].wait_recv()
            for j in range(4):
                rb[k, i, j] = chunk(k, OWN, i, j) + rb[k, i, j] + ra[k, i, j]
            if i == ACROSS:
                second2[k] = net.send(rb.at[k, i], u2.at[k], ahead[orders[k][1]])
            if i == BACK:
                secondb[k] = net.send(rb.at[k, i], ub.at[k], behind[orders[k][1]])
            if i == FRONT:
                second2[k].wait_recv()
                u2[k] = u2[k] + rb[k, i]
                seconda[k] = net.send(u2.at[k], ua.at[k], ahead[orders[k][1]])
    coarsea.wait_recv()
    coarseb.wait_recv()
    gco[...] = gbuf[OWN] + gsib[5] + gsib[6]

    third2, thirda, thirdb = [], [], []
    for k in range(3):
        secondb[k].wait_recv()
        seconda[k].wait_recv()
        ub[k] = rb[k, OWN] + ub[k] + ua[k]
        third2.append(net.send(ub.at[k, ACROSS], w2.at[k], ahead[orders[k][2]]))
        thirdb.append(net.send(ub.at[k, BACK], wb.at[k], behind[orders[k][2]]))
    for k in range(3):
        third2[k].wait_recv()
        w2[k] = w2[k] + ub[k, FRONT]
        thirda.append(net.send(w2.at[k], wa.at[k], ahead[orders[k][2]]))
    for k in range(3):
        thirdb[k].wait_recv()
        thirda[k].wait_recv()
        cols = slice(k * THIRD, (k + 1) * THIRD)
        gq[:, cols] = (
            qc[:, cols] + ub[k, OWN].astype(F32) + wb[k].astype(F32) + wa[k].astype(F32)
        )
    net.finish()


def vmem():
    return pl.BlockSpec(memory_space=pltpu.VMEM)


def smem():
    return pl.BlockSpec(memory_space=pltpu.SMEM)


def hbm():
    return pl.BlockSpec(memory_space=pl.ANY)


def shape(dims, dtype):
    return jax.ShapeDtypeStruct(dims, dtype)


def shards(
    queries,
    coarse_vectors,
    mid_vectors,
    leaf_vectors,
    coarse_pos,
    mid_pos,
    leaf_pos,
    mid_cand,
    leaf_cand,
    leaf_owner,
):
    dma = pltpu.SemaphoreType.DMA
    limit = 56 * 1024 * 1024
    group = pltpu.VMEM((TILES, TILE, D), BF16)
    notes = pltpu.VMEM((18, 8, 128), jnp.int32)
    packed = pltpu.VMEM((16, TILE, D), BF16)
    packed_notes = pltpu.VMEM((16, 8, 128), jnp.int32)
    sel, meta, plan, tbl, gc, qc = pl.pallas_call(
        gather_kernel,
        out_shape=(
            shape((2, 16, TILE, D), BF16),
            shape((2, 16, 8, 128), jnp.int32),
            shape((2, 16, 128), jnp.int32),
            shape((8, 128), jnp.int32),
            shape((128, D), F32),
            shape((TILE, D), F32),
        ),
        in_specs=[hbm(), vmem(), vmem(), vmem(), vmem(), vmem(), vmem(), hbm()],
        out_specs=(hbm(), hbm(), hbm(), vmem(), vmem(), vmem()),
        scratch_shapes=[
            group, group, group, group,
            notes, notes, notes, notes,
            pltpu.VMEM((COARSE, D), BF16),
            pltpu.VMEM((128, D), BF16),
            pltpu.VMEM((NX, NZ, 8, TILE), jnp.int32),
            packed, packed, packed_notes, packed_notes,
            pltpu.VMEM((32, 128), jnp.int32),
            pltpu.SMEM((32, 128), jnp.int32),
            dma((9,)),
            dma((GATHER_COPIES,)),
            dma((GATHER_COPIES,)),
        ],
        compiler_params=pltpu.CompilerParams(
            collective_id=0, has_side_effects=True, vmem_limit_bytes=limit
        ),
        name="gather",
    )(
        queries.reshape(TILES, TILE, D),
        mid_pos.T,
        leaf_pos.T,
        mid_cand.T,
        leaf_cand.T,
        coarse_pos.T,
        leaf_owner.reshape(2, 128),
        coarse_vectors,
    )
    gm, gl, qt = pl.pallas_call(
        local_kernel,
        out_shape=(
            shape((4, BLOCK, D), F32),
            shape((2, BLOCK, D), F32),
            shape((SLOTS, TILE, D), BF16),
        ),
        in_specs=[smem(), vmem(), hbm(), hbm(), hbm()],
        out_specs=(hbm(), hbm(), hbm()),
        scratch_shapes=[
            pltpu.SMEM((6,), jnp.int32),
            pltpu.SMEM((6 * LIST + 1,), jnp.int32),
            pltpu.SMEM((SLOTS,), jnp.int32),
            pltpu.VMEM((SLOTS + 1, TILE, D), BF16),
            pltpu.VMEM((6, BLOCK, D), BF16),
            pltpu.VMEM((6, BLOCK, D), F32),
            pltpu.VMEM((SLOTS, TILE, D), BF16),
            dma((SLOTS,)),
            dma((6,)),
            dma((6,)),
            dma((SLOTS,)),
        ],
        compiler_params=pltpu.CompilerParams(vmem_limit_bytes=limit),
        name="pairs",
    )(
        plan.reshape(SLOTS, 128),
        meta.reshape(SLOTS, 8, 128),
        mid_vectors.reshape(4, BLOCK, D),
        leaf_vectors.reshape(2, BLOCK, D),
        sel.reshape(SLOTS, TILE, D),
    )
    slots = pltpu.VMEM((5, TILE, D), BF16)
    first = pltpu.VMEM((3, 4, 4, TILE, THIRD), BF16)
    second = pltpu.VMEM((3, 4, TILE, THIRD), BF16)
    third = pltpu.VMEM((3, TILE, THIRD), BF16)
    gq, gco = pl.pallas_call(
        scatter_kernel,
        out_shape=(shape((TILE, D), F32), shape((16, D), F32)),
        in_specs=[smem(), hbm(), vmem(), vmem()],
        out_specs=(vmem(), vmem()),
        scratch_shapes=[
            slots, slots, slots, slots, slots, slots, slots, slots,
            pltpu.VMEM((7, 16, D), F32),
            pltpu.VMEM((5, 16, D), F32),
            first, first, first, first, first,
            second, second, second,
            third, third, third,
            dma((4,)),
            dma((SCATTER_COPIES,)),
            dma((SCATTER_COPIES,)),
        ],
        compiler_params=pltpu.CompilerParams(
            collective_id=1, has_side_effects=True, vmem_limit_bytes=limit
        ),
        name="scatter",
    )(tbl, qt.reshape(2, 16, TILE, D), gc.reshape(2, NY, 16, D), qc)
    return gq, gco, gm.reshape(4 * BLOCK, D), gl.reshape(2 * BLOCK, D)


def solution(mesh):
    placed = (
        P("grp", None),
        P(),
        P(("grp", "mid"), None),
        P(("grp", "mid"), None),
        P(("grp", "mid"), None),
        P("grp", None),
        P("grp", None),
        P("grp", None),
        P("grp", None),
        P(),
    )
    return jax.shard_map(
        shards,
        mesh=mesh,
        in_specs=placed,
        out_specs=(
            P(("grp", "mid"), None),
            P(("grp", "mid"), None),
            P(("grp", "mid"), None),
            P(("grp", "mid"), None),
        ),
        check_vma=False,
    )
```

```python
import jax
import jax.numpy as jnp
from jax import lax
from jax.experimental import pallas as pl
from jax.experimental.pallas import tpu as pltpu
from jax.sharding import PartitionSpec as P

TILE = 128
BLOCK = 512
COARSE = 2048
K_CAND = 8
D = 768
NY, NX, NZ = 4, 4, 4
TILES = NX * NZ
BIG = 1 << 20
F32 = jnp.float32
BF16 = jnp.bfloat16
MESH = pl.DeviceIdType.MESH
THIRD = D // 3
HALF = D // 2
NEAR = 64
REST = TILE - NEAR


def mm(a, b, ca, cb):
    return lax.dot_general(a, b, (((ca,), (cb,)), ((), ())), preferred_element_type=F32)


def delta_of(scores, labels, positives):
    hit = labels == positives[0:1]
    for p in range(1, 4):
        hit = hit | (labels == positives[p : p + 1])
    return (0.125 * jnp.tanh(0.5 * scores) + jnp.where(hit, -0.125, 0.125)).astype(BF16)


class Place:
    def __init__(self):
        grp, mid = lax.axis_index("grp"), lax.axis_index("mid")
        self.y, self.c = grp // 2, lax.rem(grp, 2)
        self.x, self.z = mid // NZ, lax.rem(mid, NZ)
        self.mid = mid
        self.ahead = 1 + 2 * self.c
        self.behind = 3 - 2 * self.c

    def at(self, dy=0, dx=0, dz=0, other=False):
        y, x, z = lax.rem(self.y + dy, NY), lax.rem(self.x + dx, NX), lax.rem(self.z + dz, NZ)
        return (2 * y + (1 - self.c if other else self.c), NZ * x + z)

    def sibling(self):
        return (2 * self.y + 1 - self.c, self.mid)

    def tile(self, dx, dz):
        return NZ * lax.rem(self.x + dx, NX) + lax.rem(self.z + dz, NZ)

    def greet(self):
        near = [self.sibling(), self.at(dy=2)]
        for step in (self.ahead, self.behind):
            near += [self.at(dy=step), self.at(dy=step, other=True)]
            near += [self.at(dx=step), self.at(dz=step)]
        barrier = pltpu.get_barrier_semaphore()
        for device in near:
            pl.semaphore_signal(barrier, inc=1, device_id=device, device_id_type=MESH)
        pl.semaphore_wait(barrier, len(near))


class Net:
    def __init__(self, send_sem, recv_sem):
        self.send_sem, self.recv_sem, self.made = send_sem, recv_sem, []

    def send(self, src, dst, device):
        i = len(self.made)
        copy = pltpu.make_async_remote_copy(
            src_ref=src,
            dst_ref=dst,
            send_sem=self.send_sem.at[i],
            recv_sem=self.recv_sem.at[i],
            device_id=device,
            device_id_type=MESH,
        )
        copy.start()
        self.made.append(copy)
        return copy

    def finish(self):
        for copy in self.made:
            copy.wait_send()


COPIES = 200
OWN, BACK, FRONT, ACROSS = range(4)
SLOTS = 32
LIST = 16


def role_step(color, role):
    return (0, 3 - 2 * color, 1 + 2 * color, 2)[role]


def main_kernel(
    q, mp, lp, mc, lc, cp, owner, cv, midv, leafv,
    gq, gco, plan, sel, deltas,
    q_own, q_b, q_a, q_2, p_own, cvv, cvm, cpall,
    in00, in01, in02, in03, in10, in11, in12, in13,
    no00, no01, no02, no03, no10, no11, no12, no13,
    sm00, sm01, sm02, sm03, sm10, sm11, sm12, sm13,
    no_a, no_b, no_x, planv, smo, pk_as, pk_ao, pk_bs, pk_bo, pk_own, pk_x, pk_b, pk_f,
    out_own, out_x, out0b, out0f, out1o, out1b, out1f, out1x,
    ret_own, ret_x, a0_0, a0_1, a1_0, a1_1, b0_0, b0_1, b1_0, b1_1,
    vectors, held_delta, gc, qc, gsib, gbuf,
    s2, sb, r2, rb, ra, u2, ub, ua, far, local_sem, send_sem, recv_sem,
):
    me = Place()
    c, a, b = me.c, me.ahead, me.behind
    net = Net(send_sem, recv_sem)
    local, done = [], []

    def start_local(src, dst):
        copy = pltpu.make_async_copy(src, dst, local_sem.at[len(local)])
        copy.start()
        local.append(copy)
        return copy

    def wait_local(copy):
        copy.wait()
        done.append(copy)

    load_q = start_local(q, q_own)
    load_v = [start_local(midv, vectors.at[pl.ds(0, 4)]), start_local(leafv, vectors.at[pl.ds(4, 2)])]
    load_c = start_local(cv, cvv)
    for t in range(TILES):
        p_own[t, 0:4, :] = mp[:, t * TILE : (t + 1) * TILE]
        p_own[t, 4:8, :] = lp[:, t * TILE : (t + 1) * TILE]
    p_own[16:18] = jnp.full((2, 8, 128), -1, jnp.int32)
    p_own[16, :, 0:TILES] = mc[...]
    p_own[17, :, 0:TILES] = lc[...]
    cpall[me.x, me.z, 0:4, :] = cp[...]
    cpall[me.x, me.z, 4:8, :] = cp[...]
    me.greet()

    m = me.mid
    up, down, across = me.at(dy=a), me.at(dy=b), me.at(dy=2)
    up_other, down_other = me.at(dy=a, other=True), me.at(dy=b, other=True)
    xa, xb, za, zb = me.at(dx=a), me.at(dx=b), me.at(dz=a), me.at(dz=b)
    sib = me.sibling()
    planes = {BACK: q_b, FRONT: q_a, ACROSS: q_2}
    slots = ((in00, in01, in02, in03), (in10, in11, in12, in13))
    notes = ((no00, no01, no02, no03), (no10, no11, no12, no13))
    facts = ((sm00, sm01, sm02, sm03), (sm10, sm11, sm12, sm13))
    outs = ((out_own, out0b, out0f, out_x), (out1o, out1b, out1f, out1x))

    rest, near = pl.ds(NEAR, REST), pl.ds(0, NEAR)
    y_in = {
        BACK: net.send(q.at[m, rest], q_b.at[m], up),
        FRONT: net.send(q.at[m, rest], q_a.at[m], down),
        ACROSS: net.send(q.at[m], q_2.at[m], across),
    }
    pos_own = cpall.at[me.x, me.z]
    cz_a = net.send(pos_own, pos_own, za)
    cz_b = net.send(pos_own, pos_own, zb)

    index = lax.broadcasted_iota(jnp.int32, (2, 128), 0) * 128 + lax.broadcasted_iota(
        jnp.int32, (2, 128), 1
    )
    code = 4 * (
        TILES * lax.broadcasted_iota(jnp.int32, (8, 128), 0)
        + lax.broadcasted_iota(jnp.int32, (8, 128), 1)
    )
    lane = lax.broadcasted_iota(jnp.int32, (1, 128), 1)
    mids, leaves = p_own[16], p_own[17]
    for label, step in enumerate((0, a, b, 2)):
        for which, core in enumerate((c, 1 - c)):
            device = (2 * lax.rem(me.y + step, NY) + core) * TILES + m
            held = [
                jnp.sum(
                    jnp.where(owner[...] == 2 * device + i, index, 0), axis=(0, 1), keepdims=True
                )
                for i in range(2)
            ]
            entries = []
            for live, block in (
                ((mids >> 2) == device, mids & 3),
                ((leaves == held[0]) | (leaves == held[1]), (leaves == held[1]).astype(jnp.int32)),
            ):
                found = code + block
                first = jnp.min(jnp.where(live, found, BIG), axis=(0, 1), keepdims=True)
                final = jnp.max(jnp.where(live, found, -1), axis=(0, 1), keepdims=True)
                some = first < BIG
                entries.append((some, jnp.where(some, first, 0)))
                two = some & (final != first)
                entries.append((two, jnp.where(two, final, 0)))
            tiles = [(value >> 2) & 15 for _, value in entries]
            spots = jnp.full((1, 128), 4, jnp.int32)
            for e in (3, 2, 1, 0):
                spots = jnp.where(entries[e][0] & (tiles[e] == lane), e, spots)
            at = 32 + 2 * label + which
            planv[at : at + 1, :] = spots
            for e, (valid, value) in enumerate(entries):
                slot = jnp.full((1, 1), e, jnp.int32)
                for f in range(e - 1, -1, -1):
                    slot = jnp.where(valid & entries[f][0] & (tiles[f] == tiles[e]), f, slot)
                row = jnp.where(lane == 0, jnp.where(valid, value & 3, -1), slot)
                row = jnp.where(lane == 2, tiles[e], row)
                row = jnp.where(lane == 3, value >> 6, row)
                row = jnp.where(lane == 4, (value & 3) + 4 * (e // 2), row)
                at = 8 * label + 4 * which + e
                planv[at : at + 1, :] = row
    to_smem = start_local(planv, smo)
    wait_local(load_q)
    wait_local(to_smem)
    notes_out = (no00, no_a, no_b, no_x)

    def fill_notes(label):
        out = notes_out[label]
        for e in range(8):
            at = 8 * label + e
            level = 4 * (e % 4 // 2)
            positives = p_own[smo[at, 2]][level : level + 4] - BLOCK * smo[at, 3]
            out[e, 0:4, :] = positives
            out[e, 4:5, :] = planv[at : at + 1, :]
            out[e, 5:8, :] = jnp.zeros((3, 128), jnp.int32)
        out[8, 0:2, :] = planv[32 + 2 * label : 34 + 2 * label, :]
        out[8, 2:8, :] = jnp.zeros((6, 128), jnp.int32)

    direct, note_in = {}, {}
    for label, targets in ((BACK, ((pk_as, up), (pk_ao, up_other))), (FRONT, ((pk_bs, down), (pk_bo, down_other)))):
        fill_notes(label)
        for which, (buffer, device) in enumerate(targets):
            for e in range(4):
                buffer[e] = q_own[smo[8 * label + 4 * which + e, 2], 0:NEAR]
            note_in[which, label] = net.send(notes_out[label], notes[which][label], device)
            direct[which, label] = net.send(buffer, slots[which][label].at[:, near], device)
    fill_notes(ACROSS)
    note_in[0, ACROSS] = net.send(no_x, no03, across)
    fill_notes(OWN)
    for e in range(4):
        pk_own[e] = q_own[smo[4 + e, 2]]
    note_in[1, OWN] = net.send(no00, no10, sib)
    beside = {OWN: net.send(pk_own, in10, sib)}
    for e in range(4):
        in00[e] = q_own[smo[e, 2]]

    axes = ((za, zb, xa, xb), (xa, xb, za, zb))
    walk = (0, b, a, 2)

    def rows_of(role, h):
        size = (TILE if role == ACROSS else REST) // 2
        return pl.ds(h * size, size)

    def tile_of(h, first, last):
        return me.tile(last, first) if h == 0 else me.tile(first, last)

    second, second_f, last, last_f = {}, {}, {}, {}

    def send_second(role):
        y_in[role].wait_recv()
        for h, (to_a, to_b, _, _) in enumerate(axes):
            piece = planes[role].at[m, rows_of(role, h)]
            second[role, h] = (net.send(piece, piece, to_a), net.send(piece, piece, to_b))

    def send_last(role, key):
        for h, (_, _, to_a, to_b) in enumerate(axes):
            piece = planes[role].at[tile_of(h, walk[key], 0), rows_of(role, h)]
            last[role, h, key] = (net.send(piece, piece, to_a), net.send(piece, piece, to_b))

    def second_stage(role):
        for h, (to_a, _, _, _) in enumerate(axes):
            second[role, h][0].wait_recv()
            piece = planes[role].at[tile_of(h, b, 0), rows_of(role, h)]
            second_f[role, h] = net.send(piece, piece, to_a)
        send_last(role, BACK)
        for h in range(2):
            second[role, h][1].wait_recv()
        send_last(role, FRONT)

    def across_stage(role):
        for h in range(2):
            second_f[role, h].wait_recv()
        send_last(role, ACROSS)

    def forward_last(role):
        for key, step in enumerate(walk):
            for h, (_, _, to_a, _) in enumerate(axes):
                last[role, h, key][0].wait_recv()
                piece = planes[role].at[tile_of(h, step, b), rows_of(role, h)]
                last_f[role, h, key] = net.send(piece, piece, to_a)

    def complete(role):
        for key in range(4):
            for h in range(2):
                last[role, h, key][1].wait_recv()
                last_f[role, h, key].wait_recv()

    def know(which, role):
        if (which, role) in note_in:
            note_in[which, role].wait_recv()
        wait_local(start_local(notes[which][role], facts[which][role]))

    def pack(role):
        know(0, role)
        rows = planes[role]
        buffer = {BACK: pk_b, FRONT: pk_f, ACROSS: pk_x}[role]
        for e in range(4):
            buffer[e] = rows[facts[0][role][4 + e, 4, 2]]
        if role == ACROSS:
            note_in[1, role] = net.send(no03, no13, sib)
            beside[role] = net.send(buffer, in13, sib)
        else:
            beside[role] = net.send(buffer, slots[1][role].at[:, rest], sib)
        for e in range(4):
            value = rows[facts[0][role][e, 4, 2]]
            if role == ACROSS:
                in03[e] = value
            else:
                slots[0][role][e, NEAR:TILE] = value

    labels = lax.broadcasted_iota(jnp.int32, (BLOCK, TILE), 0)
    returns = {}

    def pairs(which, role):
        if which == 1:
            know(1, role)
            beside[role].wait_recv()
        if (which, role) in direct:
            direct[which, role].wait_recv()
        block_of, rows, info, out = (
            facts[which][role], slots[which][role], notes[which][role], outs[which][role]
        )
        group = pl.ds(4 * role, 4)
        start_local(rows, sel.at[which, group])

        def body(e, carry):
            block = vectors[block_of[4 * which + e, 4, 4]]
            delta = delta_of(mm(block, rows[e], 1, 1), labels, info[4 * which + e])
            held_delta[which, 4 * role + e] = delta
            out[e] = mm(delta, block, 0, 0).astype(BF16)
            return carry

        lax.fori_loop(0, 4, body, 0)
        start_local(held_delta.at[which, group], deltas.at[which, group])
        for e in range(3):
            value = out[e]
            for f in range(e + 1, 4):
                same = block_of[4 * which + f, 4, 1] == e
                value += jnp.where(same, out[f], jnp.zeros((TILE, D), BF16))
            out[e] = value
        for e in range(4):
            at = 16 * which + 4 * role + e
            plan[at : at + 1, :] = info[4 * which + e, 4:5, :]

    row_halves = (pl.ds(0, TILE // 2), pl.ds(TILE // 2, TILE // 2))
    ret_a0, ret_a1, ret_b0, ret_b1 = (a0_0, a0_1), (a1_0, a1_1), (b0_0, b0_1), (b1_0, b1_1)
    four = pl.ds(0, 4)

    def give_back(which, role, r):
        out = outs[which][role]
        back = {
            (0, BACK): (ret_a0, down),
            (0, FRONT): (ret_b0, up),
            (1, BACK): (ret_a1, up_other),
            (1, FRONT): (ret_b1, down_other),
        }[which, role]
        returns[which, role, r] = net.send(
            out.at[four, row_halves[r]], back[0][r].at[four], back[1]
        )

    for ref in (out_own, out_x, ret_own, ret_x):
        ref[4] = jnp.zeros((TILE, D), BF16)
    for ref in ret_a0 + ret_a1 + ret_b0 + ret_b1:
        ref[4] = jnp.zeros((TILE // 2, D), BF16)
    steps = (0, b, a, 2)
    first_axis = ((xa, xb), (za, zb))
    first2, firsta, firstb = {}, {}, {}
    second2, seconda, secondb = {}, {}, {}
    term_in = {}

    def part(h, stream, unit, j):
        tile = me.tile(steps[unit], steps[j]) if h == 0 else me.tile(steps[j], steps[unit])
        cols = slice(h * HALF, (h + 1) * HALF)
        r = stream % 2
        rows = slice(r * TILE // 2, (r + 1) * TILE // 2)
        if stream < 2:
            return out_x[sm03[8, 0, tile], rows, cols] + ret_x[sm03[8, 1, tile], rows, cols]
        value = out_own[smo[32 + 2 * OWN, tile], rows, cols]
        value += ret_own[smo[33 + 2 * OWN, tile], rows, cols]
        value += ret_a0[r][smo[32 + 2 * BACK, tile], :, cols]
        value += ret_a1[r][smo[33 + 2 * BACK, tile], :, cols]
        value += ret_b0[r][smo[32 + 2 * FRONT, tile], :, cols]
        return value + ret_b1[r][smo[33 + 2 * FRONT, tile], :, cols]

    def begin_sum(stream):
        if stream == 0:
            term_in[ACROSS].wait_recv()
        if stream >= 2:
            if stream == 2:
                term_in[OWN].wait_recv()
            for which in range(2):
                for role in (BACK, FRONT):
                    returns[which, role, stream - 2].wait_recv()
        for h in range(2):
            for j in range(4):
                s2[h, stream, j] = part(h, stream, ACROSS, j)
            first2[h, stream] = net.send(s2.at[h, stream], r2.at[h, stream], first_axis[h][0])
            for j in range(4):
                sb[h, stream, j] = part(h, stream, BACK, j)
            firstb[h, stream] = net.send(sb.at[h, stream], rb.at[h, stream], first_axis[h][1])

    def pass_sum(stream):
        for h in range(2):
            first2[h, stream].wait_recv()
            for j in range(4):
                r2[h, stream, j] = r2[h, stream, j] + part(h, stream, FRONT, j)
            firsta[h, stream] = net.send(r2.at[h, stream], ra.at[h, stream], first_axis[h][0])

    def begin_second(stream):
        for h in range(2):
            firstb[h, stream].wait_recv()
            firsta[h, stream].wait_recv()
            to_a, to_b = first_axis[1 - h]
            for j in (ACROSS, BACK, FRONT, OWN):
                rb[h, stream, j] = part(h, stream, OWN, j) + rb[h, stream, j] + ra[h, stream, j]
                if j == ACROSS:
                    second2[h, stream] = net.send(rb.at[h, stream, j], u2.at[h, stream], to_a)
                if j == BACK:
                    secondb[h, stream] = net.send(rb.at[h, stream, j], ub.at[h, stream], to_b)

    def pass_second(stream):
        for h in range(2):
            second2[h, stream].wait_recv()
            u2[h, stream] = u2[h, stream] + rb[h, stream, FRONT]
            seconda[h, stream] = net.send(u2.at[h, stream], ua.at[h, stream], first_axis[1 - h][0])

    def end_second(stream):
        for h in range(2):
            secondb[h, stream].wait_recv()
            seconda[h, stream].wait_recv()
            ub[h, stream] = rb[h, stream, OWN] + ub[h, stream] + ua[h, stream]

    send_second(BACK)
    send_second(FRONT)
    send_last(BACK, OWN)
    send_second(ACROSS)
    know(0, OWN)
    for load in load_v:
        wait_local(load)
    pairs(0, OWN)
    second_stage(BACK)
    cz_a.wait_recv()
    pos_b = cpall.at[me.x, lax.rem(me.z + b, NZ)]
    cz_f = net.send(pos_b, pos_b, za)
    send_last(FRONT, OWN)
    second_stage(FRONT)
    across_stage(BACK)
    pairs(1, OWN)
    term_in[OWN] = net.send(out1o, ret_own.at[four], sib)
    across_stage(FRONT)
    cz_b.wait_recv()
    cz_f.wait_recv()
    pos_row = cpall.at[me.x]
    cx_a = net.send(pos_row, pos_row, xa)
    cx_b = net.send(pos_row, pos_row, xb)
    forward_last(BACK)
    send_last(ACROSS, OWN)
    second_stage(ACROSS)
    complete(BACK)
    pack(BACK)
    across_stage(ACROSS)
    cx_a.wait_recv()
    pos_row_b = cpall.at[lax.rem(me.x + b, NX)]
    cx_f = net.send(pos_row_b, pos_row_b, xa)
    pairs(0, BACK)
    give_back(0, BACK, 0)
    forward_last(FRONT)
    complete(FRONT)
    pack(FRONT)
    pairs(0, FRONT)
    give_back(0, FRONT, 0)
    forward_last(ACROSS)
    pairs(1, BACK)
    give_back(1, BACK, 0)
    pairs(1, FRONT)
    give_back(1, FRONT, 0)
    for role in (BACK, FRONT):
        for which in range(2):
            give_back(which, role, 1)
    wait_local(load_c)
    for j in range(8):
        color, role = j // 4, j % 4
        row = (2 * lax.rem(me.y + role_step(color, role), NY) + color) * TILES + m
        start = pl.multiple_of(row * 16, 16)
        cvm[pl.ds(16 * j, 16), :] = cvv[pl.ds(start, 16), :]
    place = lax.broadcasted_iota(jnp.int32, (128, 128), 0)
    chunk = place // 16
    color, role = chunk // 4, lax.rem(chunk, 4)
    step = jnp.where(role == ACROSS, 2, jnp.where(role == FRONT, 1 + 2 * color, 3 - 2 * color))
    step = jnp.where(role == OWN, 0, step)
    owner_grp = 2 * lax.rem(me.y + step, NY) + color
    coarse_ids = (owner_grp * TILES + m) * 16 + lax.rem(place, 16)

    def own_coarse():
        qm = q_own[m]
        total = jnp.zeros((TILE, D), F32)
        for i in range(COARSE // BLOCK):
            vectors = cvv[i * BLOCK : (i + 1) * BLOCK, :]
            labels = lax.broadcasted_iota(jnp.int32, (BLOCK, TILE), 0) + i * BLOCK
            delta = delta_of(mm(vectors, qm, 1, 1), labels, cpall[me.x, me.z])
            total += mm(delta, vectors, 0, 0)
        qc[...] = total

    def rows_coarse(lo, hi):
        def body(t, carry):
            qt = q_own[t]
            delta = delta_of(mm(cvm[...], qt, 1, 1), coarse_ids, cpall[t // NZ, lax.rem(t, NZ)])
            gc[...] += mm(delta, qt, 1, 0)
            return carry

        lax.fori_loop(lo, hi, body, 0)


    gc[...] = jnp.zeros_like(gc)
    own_coarse()
    complete(ACROSS)
    pack(ACROSS)
    cx_b.wait_recv()
    cx_f.wait_recv()
    pairs(0, ACROSS)
    rows_coarse(0, 8)
    pairs(1, ACROSS)
    term_in[ACROSS] = net.send(out1x, ret_x.at[four], sib)
    rows_coarse(8, 16)
    coarse = net.send(gc.at[pl.ds(64 * (1 - c), 64)], gsib, sib)
    begin_sum(2)
    begin_sum(0)
    begin_sum(1)
    pass_sum(2)
    pass_sum(0)
    pass_sum(1)
    begin_sum(3)
    begin_second(2)
    begin_second(0)
    begin_second(1)
    pass_sum(3)
    pass_second(2)
    pass_second(0)
    pass_second(1)
    coarse.wait_recv()
    for role in range(4):
        gbuf[role] = gc[pl.ds(64 * c + 16 * role, 16)] + gsib[16 * role : 16 * role + 16]
    coarse2 = net.send(gbuf.at[ACROSS], gbuf.at[5], up)
    coarseb = net.send(gbuf.at[BACK], gbuf.at[6], down)
    end_second(0)
    end_second(1)
    home = net.send(ub.at[:, pl.ds(0, 2)], far, across)
    begin_second(3)
    end_second(2)
    coarse2.wait_recv()
    gbuf[4] = gbuf[FRONT] + gbuf[5]
    coarsea = net.send(gbuf.at[4], gbuf.at[7], up)
    pass_second(3)
    coarsea.wait_recv()
    coarseb.wait_recv()
    gco[...] = gbuf[OWN] + gbuf[6] + gbuf[7]
    home.wait_recv()
    end_second(3)
    for h in range(2):
        cols = slice(h * HALF, (h + 1) * HALF)
        for r in range(2):
            rows = slice(r * TILE // 2, (r + 1) * TILE // 2)
            gq[rows, cols] = (
                qc[rows, cols] + ub[h, 2 + r].astype(F32) + far[h, r].astype(F32)
            )
    for copy in local:
        if not any(copy is other for other in done):
            copy.wait()
    net.finish()


def grads_kernel(
    plan, sel, deltas,
    gm, gl,
    counts, entries, rows, held, acc, row_sem, delta_sem, grad_sem,
):
    stores = [(gm, 0), (gm, 1), (gm, 2), (gm, 3), (gl, 0), (gl, 1)]

    def row_copy(e):
        return pltpu.make_async_copy(sel.at[e], rows.at[e], row_sem.at[e])

    def delta_copy(e):
        return pltpu.make_async_copy(deltas.at[e], held.at[e], delta_sem.at[e])

    for key in range(6):
        counts[key] = 0
    for e in range(SLOTS):
        block = plan[e, 0]

        @pl.when(block >= 0)
        def _():
            row_copy(e).start()
            delta_copy(e).start()
            key = block + 4 * (e // 2 % 2)
            n = counts[key]
            entries[LIST * key + n] = e
            counts[key] = n + 1

    rows[SLOTS] = jnp.zeros((TILE, D), BF16)
    held[SLOTS] = jnp.zeros((BLOCK, TILE), BF16)

    def per_key(key, carry):
        n = counts[key]
        start = LIST * key

        @pl.when(n == 0)
        def _():
            acc[key] = jnp.zeros((BLOCK, D), F32)

        def batch(i, inner):
            at = start + 2 * i
            full = 2 * i + 1 < n
            e0 = entries[at]
            e1 = jnp.where(full, entries[at + 1], SLOTS)
            row_copy(e0).wait()
            delta_copy(e0).wait()

            @pl.when(full)
            def _():
                row_copy(e1).wait()
                delta_copy(e1).wait()

            both = jnp.concatenate([rows[e0], rows[e1]], axis=0)
            delta = jnp.concatenate([held[e0], held[e1]], axis=1)

            @pl.when(i == 0)
            def _():
                for n_col in range(3):
                    cols = slice(n_col * THIRD, (n_col + 1) * THIRD)
                    acc[key, :, cols] = mm(delta, both[:, cols], 1, 0)

            @pl.when(i != 0)
            def _():
                for n_col in range(3):
                    cols = slice(n_col * THIRD, (n_col + 1) * THIRD)
                    acc[key, :, cols] += mm(delta, both[:, cols], 1, 0)

            return inner

        lax.fori_loop(0, (n + 1) // 2, batch, 0)
        for i, (out, j) in enumerate(stores):

            @pl.when(key == i)
            def _():
                pltpu.make_async_copy(acc.at[i], out.at[j], grad_sem.at[i]).start()

        return carry

    lax.fori_loop(0, 6, per_key, 0)
    for i, (out, j) in enumerate(stores):
        pltpu.make_async_copy(acc.at[i], out.at[j], grad_sem.at[i]).wait()


def vmem():
    return pl.BlockSpec(memory_space=pltpu.VMEM)


def smem():
    return pl.BlockSpec(memory_space=pltpu.SMEM)


def hbm():
    return pl.BlockSpec(memory_space=pl.ANY)


def shape(dims, dtype):
    return jax.ShapeDtypeStruct(dims, dtype)


def shards(
    queries,
    coarse_vectors,
    mid_vectors,
    leaf_vectors,
    coarse_pos,
    mid_pos,
    leaf_pos,
    mid_cand,
    leaf_cand,
    leaf_owner,
):
    dma = pltpu.SemaphoreType.DMA
    mib = 1024 * 1024
    group = pltpu.VMEM((TILES, TILE, D), BF16)
    part = pltpu.VMEM((TILES, REST, D), BF16)
    four = pltpu.VMEM((4, TILE, D), BF16)
    five = pltpu.VMEM((5, TILE, D), BF16)
    half = pltpu.VMEM((5, TILE // 2, D), BF16)
    near = pltpu.VMEM((4, NEAR, D), BF16)
    rest = pltpu.VMEM((4, REST, D), BF16)
    notes = pltpu.VMEM((9, 8, 128), jnp.int32)
    facts = pltpu.SMEM((9, 8, 128), jnp.int32)
    first = pltpu.VMEM((2, 4, 4, TILE // 2, HALF), BF16)
    second = pltpu.VMEM((2, 4, TILE // 2, HALF), BF16)
    gq, gco, plan, sel, deltas = pl.pallas_call(
        main_kernel,
        out_shape=(
            shape((TILE, D), F32),
            shape((16, D), F32),
            shape((SLOTS, 128), jnp.int32),
            shape((2, 16, TILE, D), BF16),
            shape((2, 16, BLOCK, TILE), BF16),
        ),
        in_specs=[hbm(), vmem(), vmem(), vmem(), vmem(), vmem(), vmem(), hbm(), hbm(), hbm()],
        out_specs=(vmem(), vmem(), vmem(), hbm(), hbm()),
        scratch_shapes=[
            group, part, part, group,
            pltpu.VMEM((18, 8, 128), jnp.int32),
            pltpu.VMEM((COARSE, D), BF16),
            pltpu.VMEM((128, D), BF16),
            pltpu.VMEM((NX, NZ, 8, TILE), jnp.int32),
            four, four, four, four, four, four, four, four,
            notes, notes, notes, notes, notes, notes, notes, notes,
            facts, facts, facts, facts, facts, facts, facts, facts,
            notes, notes, notes,
            pltpu.VMEM((40, 128), jnp.int32),
            pltpu.SMEM((40, 128), jnp.int32),
            near, near, near, near, four, four, rest, rest,
            five, five, four, four, four, four, four, four,
            five, five,
            half, half, half, half, half, half, half, half,
            pltpu.VMEM((6, BLOCK, D), BF16),
            pltpu.VMEM((2, 16, BLOCK, TILE), BF16),
            pltpu.VMEM((128, D), F32),
            pltpu.VMEM((TILE, D), F32),
            pltpu.VMEM((64, D), F32),
            pltpu.VMEM((8, 16, D), F32),
            first, first, first, first, first,
            second, second, second,
            pltpu.VMEM((2, 2, TILE // 2, HALF), BF16),
            dma((40,)),
            dma((COPIES,)),
            dma((COPIES,)),
        ],
        compiler_params=pltpu.CompilerParams(
            collective_id=0, has_side_effects=True, vmem_limit_bytes=62 * mib
        ),
        name="main",
    )(
        queries.reshape(TILES, TILE, D),
        mid_pos.T,
        leaf_pos.T,
        mid_cand.T,
        leaf_cand.T,
        coarse_pos.T,
        leaf_owner.reshape(2, 128),
        coarse_vectors,
        mid_vectors.reshape(4, BLOCK, D),
        leaf_vectors.reshape(2, BLOCK, D),
    )
    gm, gl = pl.pallas_call(
        grads_kernel,
        out_shape=(shape((4, BLOCK, D), F32), shape((2, BLOCK, D), F32)),
        in_specs=[smem(), hbm(), hbm()],
        out_specs=(hbm(), hbm()),
        scratch_shapes=[
            pltpu.SMEM((6,), jnp.int32),
            pltpu.SMEM((6 * LIST + 1,), jnp.int32),
            pltpu.VMEM((SLOTS + 1, TILE, D), BF16),
            pltpu.VMEM((SLOTS + 1, BLOCK, TILE), BF16),
            pltpu.VMEM((6, BLOCK, D), F32),
            dma((SLOTS,)),
            dma((SLOTS,)),
            dma((6,)),
        ],
        compiler_params=pltpu.CompilerParams(vmem_limit_bytes=60 * mib),
        name="grads",
    )(plan, sel.reshape(SLOTS, TILE, D), deltas.reshape(SLOTS, BLOCK, TILE))
    return gq, gco, gm.reshape(4 * BLOCK, D), gl.reshape(2 * BLOCK, D)


def solution(mesh):
    placed = (
        P("grp", None),
        P(),
        P(("grp", "mid"), None),
        P(("grp", "mid"), None),
        P(("grp", "mid"), None),
        P("grp", None),
        P("grp", None),
        P("grp", None),
        P("grp", None),
        P(),
    )
    return jax.shard_map(
        shards,
        mesh=mesh,
        in_specs=placed,
        out_specs=(
            P(("grp", "mid"), None),
            P(("grp", "mid"), None),
            P(("grp", "mid"), None),
            P(("grp", "mid"), None),
        ),
        check_vma=False,
    )
```

```python
import jax
import jax.numpy as jnp
from jax import lax
from jax.experimental import pallas as pl
from jax.experimental.pallas import tpu as pltpu
from jax.sharding import PartitionSpec as P

TILE = 128
BLOCK = 512
COARSE = 2048
K_CAND = 8
D = 768
NY, NX, NZ = 4, 4, 4
TILES = NX * NZ
BIG = 1 << 20
F32 = jnp.float32
BF16 = jnp.bfloat16
MESH = pl.DeviceIdType.MESH
THIRD = D // 3
HALF = D // 2
NEAR = 64
REST = TILE - NEAR


def mm(a, b, ca, cb):
    return lax.dot_general(a, b, (((ca,), (cb,)), ((), ())), preferred_element_type=F32)


def delta_of(scores, labels, positives):
    hit = labels == positives[0:1]
    for p in range(1, 4):
        hit = hit | (labels == positives[p : p + 1])
    return (0.125 * jnp.tanh(0.5 * scores) + jnp.where(hit, -0.125, 0.125)).astype(BF16)


class Place:
    def __init__(self):
        grp, mid = lax.axis_index("grp"), lax.axis_index("mid")
        self.y, self.c = grp // 2, lax.rem(grp, 2)
        self.x, self.z = mid // NZ, lax.rem(mid, NZ)
        self.mid = mid
        self.ahead = 1 + 2 * self.c
        self.behind = 3 - 2 * self.c

    def at(self, dy=0, dx=0, dz=0, other=False):
        y, x, z = lax.rem(self.y + dy, NY), lax.rem(self.x + dx, NX), lax.rem(self.z + dz, NZ)
        return (2 * y + (1 - self.c if other else self.c), NZ * x + z)

    def sibling(self):
        return (2 * self.y + 1 - self.c, self.mid)

    def tile(self, dx, dz):
        return NZ * lax.rem(self.x + dx, NX) + lax.rem(self.z + dz, NZ)

    def greet(self):
        near = [self.sibling(), self.at(dy=2)]
        for step in (self.ahead, self.behind):
            near += [self.at(dy=step), self.at(dy=step, other=True)]
            near += [self.at(dx=step), self.at(dz=step)]
        barrier = pltpu.get_barrier_semaphore()
        for device in near:
            pl.semaphore_signal(barrier, inc=1, device_id=device, device_id_type=MESH)
        pl.semaphore_wait(barrier, len(near))


class Net:
    def __init__(self, send_sem, recv_sem):
        self.send_sem, self.recv_sem, self.made = send_sem, recv_sem, []

    def send(self, src, dst, device):
        i = len(self.made)
        copy = pltpu.make_async_remote_copy(
            src_ref=src,
            dst_ref=dst,
            send_sem=self.send_sem.at[i],
            recv_sem=self.recv_sem.at[i],
            device_id=device,
            device_id_type=MESH,
        )
        copy.start()
        self.made.append(copy)
        return copy

    def finish(self):
        for copy in self.made:
            copy.wait_send()


COPIES = 200
OWN, BACK, FRONT, ACROSS = range(4)
SLOTS = 32
LIST = 16


def role_step(color, role):
    return (0, 3 - 2 * color, 1 + 2 * color, 2)[role]


def main_kernel(
    q, mp, lp, mc, lc, cp, owner, cv, midv, leafv,
    gq, gco, plan, sel, deltas,
    q_own, q_b, q_a, q_2, p_own, cvv, cvm, cpall,
    in00, in01, in02, in03, in10, in11, in12, in13,
    no00, no01, no02, no03, no10, no11, no12, no13,
    sm00, sm01, sm02, sm03, sm10, sm11, sm12, sm13,
    no_a, no_b, no_x, planv, smo, pk_as, pk_ao, pk_bs, pk_bo, pk_own, pk_x, pk_b, pk_f,
    out_own, out_x, out0b, out0f, out1o, out1b, out1f, out1x,
    ret_own, ret_x, a0_0, a0_1, a1_0, a1_1, b0_0, b0_1, b1_0, b1_1,
    vectors, held_delta, gc, qc, gsib, gbuf,
    s2, sb, r2, rb, ra, u2, ub, ua, far, local_sem, send_sem, recv_sem,
):
    me = Place()
    c, a, b = me.c, me.ahead, me.behind
    net = Net(send_sem, recv_sem)
    local, done = [], []

    def start_local(src, dst):
        copy = pltpu.make_async_copy(src, dst, local_sem.at[len(local)])
        copy.start()
        local.append(copy)
        return copy

    def wait_local(copy):
        copy.wait()
        done.append(copy)

    load_q = start_local(q, q_own)
    load_v = [start_local(midv, vectors.at[pl.ds(0, 4)]), start_local(leafv, vectors.at[pl.ds(4, 2)])]
    load_c = start_local(cv, cvv)
    for t in range(TILES):
        p_own[t, 0:4, :] = mp[:, t * TILE : (t + 1) * TILE]
        p_own[t, 4:8, :] = lp[:, t * TILE : (t + 1) * TILE]
    p_own[16:18] = jnp.full((2, 8, 128), -1, jnp.int32)
    p_own[16, :, 0:TILES] = mc[...]
    p_own[17, :, 0:TILES] = lc[...]
    cpall[me.x, me.z, 0:4, :] = cp[...]
    cpall[me.x, me.z, 4:8, :] = cp[...]
    me.greet()

    m = me.mid
    up, down, across = me.at(dy=a), me.at(dy=b), me.at(dy=2)
    up_other, down_other = me.at(dy=a, other=True), me.at(dy=b, other=True)
    xa, xb, za, zb = me.at(dx=a), me.at(dx=b), me.at(dz=a), me.at(dz=b)
    sib = me.sibling()
    planes = {BACK: q_b, FRONT: q_a, ACROSS: q_2}
    slots = ((in00, in01, in02, in03), (in10, in11, in12, in13))
    notes = ((no00, no01, no02, no03), (no10, no11, no12, no13))
    facts = ((sm00, sm01, sm02, sm03), (sm10, sm11, sm12, sm13))
    outs = ((out_own, out0b, out0f, out_x), (out1o, out1b, out1f, out1x))

    rest, near = pl.ds(NEAR, REST), pl.ds(0, NEAR)
    y_in = {
        BACK: net.send(q.at[m, rest], q_b.at[m], up),
        FRONT: net.send(q.at[m, rest], q_a.at[m], down),
        ACROSS: net.send(q.at[m], q_2.at[m], across),
    }
    pos_own = cpall.at[me.x, me.z]
    cz_a = net.send(pos_own, pos_own, za)
    cz_b = net.send(pos_own, pos_own, zb)

    index = lax.broadcasted_iota(jnp.int32, (2, 128), 0) * 128 + lax.broadcasted_iota(
        jnp.int32, (2, 128), 1
    )
    code = 4 * (
        TILES * lax.broadcasted_iota(jnp.int32, (8, 128), 0)
        + lax.broadcasted_iota(jnp.int32, (8, 128), 1)
    )
    lane = lax.broadcasted_iota(jnp.int32, (1, 128), 1)
    mids, leaves = p_own[16], p_own[17]

    def whole(value):
        return jnp.broadcast_to(value, (1, 128))

    for label, step in enumerate((0, a, b, 2)):
        for which, core in enumerate((c, 1 - c)):
            device = (2 * lax.rem(me.y + step, NY) + core) * TILES + m
            held = [
                whole(
                    jnp.sum(
                        jnp.where(owner[...] == 2 * device + i, index, 0), axis=(0, 1), keepdims=True
                    )
                )
                for i in range(2)
            ]
            entries = []
            for live, block in (
                ((mids >> 2) == device, mids & 3),
                ((leaves == held[0]) | (leaves == held[1]), (leaves == held[1]).astype(jnp.int32)),
            ):
                found = code + block
                first = whole(jnp.min(jnp.where(live, found, BIG), axis=(0, 1), keepdims=True))
                final = whole(jnp.max(jnp.where(live, found, -1), axis=(0, 1), keepdims=True))
                some = first < BIG
                entries.append((some, jnp.where(some, first, 0)))
                two = some & (final != first)
                entries.append((two, jnp.where(two, final, 0)))
            tiles = [(value >> 2) & 15 for _, value in entries]
            spots = jnp.full((1, 128), 4, jnp.int32)
            for e in (3, 2, 1, 0):
                spots = jnp.where(entries[e][0] & (tiles[e] == lane), e, spots)
            at = 32 + 2 * label + which
            planv[at : at + 1, :] = spots
            for e, (valid, value) in enumerate(entries):
                follow = jnp.full((1, 128), 4, jnp.int32)
                for f in range(3, e, -1):
                    follow = jnp.where(valid & entries[f][0] & (tiles[f] == tiles[e]), f, follow)
                row = jnp.where(lane == 0, jnp.where(valid, value & 3, -1), follow)
                row = jnp.where(lane == 2, tiles[e], row)
                row = jnp.where(lane == 3, value >> 6, row)
                row = jnp.where(lane == 4, (value & 3) + 4 * (e // 2), row)
                at = 8 * label + 4 * which + e
                planv[at : at + 1, :] = row
    to_smem = start_local(planv, smo)
    wait_local(load_q)
    wait_local(to_smem)
    notes_out = (no00, no_a, no_b, no_x)

    def fill_notes(label):
        out = notes_out[label]
        for e in range(8):
            at = 8 * label + e
            level = 4 * (e % 4 // 2)
            positives = p_own[smo[at, 2]][level : level + 4] - BLOCK * smo[at, 3]
            out[e, 0:4, :] = positives
            out[e, 4:5, :] = planv[at : at + 1, :]
            out[e, 5:8, :] = jnp.zeros((3, 128), jnp.int32)
        out[8, 0:2, :] = planv[32 + 2 * label : 34 + 2 * label, :]
        out[8, 2:8, :] = jnp.zeros((6, 128), jnp.int32)

    direct, note_in = {}, {}
    for label, targets in ((BACK, ((pk_as, up), (pk_ao, up_other))), (FRONT, ((pk_bs, down), (pk_bo, down_other)))):
        fill_notes(label)
        for which, (buffer, device) in enumerate(targets):
            for e in range(4):
                buffer[e] = q_own[smo[8 * label + 4 * which + e, 2], 0:NEAR]
            note_in[which, label] = net.send(notes_out[label], notes[which][label], device)
            direct[which, label] = net.send(buffer, slots[which][label].at[:, near], device)
    fill_notes(ACROSS)
    note_in[0, ACROSS] = net.send(no_x, no03, across)
    fill_notes(OWN)
    for e in range(4):
        pk_own[e] = q_own[smo[4 + e, 2]]
    note_in[1, OWN] = net.send(no00, no10, sib)
    beside = {OWN: net.send(pk_own, in10, sib)}
    for e in range(4):
        in00[e] = q_own[smo[e, 2]]

    axes = ((za, zb, xa, xb), (xa, xb, za, zb))
    walk = (0, b, a, 2)

    def rows_of(role, h):
        size = (TILE if role == ACROSS else REST) // 2
        return pl.ds(h * size, size)

    def tile_of(h, first, last):
        return me.tile(last, first) if h == 0 else me.tile(first, last)

    second, second_f, last, last_f = {}, {}, {}, {}

    def send_second(role):
        y_in[role].wait_recv()
        for h, (to_a, to_b, _, _) in enumerate(axes):
            piece = planes[role].at[m, rows_of(role, h)]
            second[role, h] = (net.send(piece, piece, to_a), net.send(piece, piece, to_b))

    def send_last(role, key):
        for h, (_, _, to_a, to_b) in enumerate(axes):
            piece = planes[role].at[tile_of(h, walk[key], 0), rows_of(role, h)]
            last[role, h, key] = (net.send(piece, piece, to_a), net.send(piece, piece, to_b))

    def second_stage(role):
        for h, (to_a, _, _, _) in enumerate(axes):
            second[role, h][0].wait_recv()
            piece = planes[role].at[tile_of(h, b, 0), rows_of(role, h)]
            second_f[role, h] = net.send(piece, piece, to_a)
        send_last(role, BACK)
        for h in range(2):
            second[role, h][1].wait_recv()
        send_last(role, FRONT)

    def across_stage(role):
        for h in range(2):
            second_f[role, h].wait_recv()
        send_last(role, ACROSS)

    def forward_last(role):
        for key, step in enumerate(walk):
            for h, (_, _, to_a, _) in enumerate(axes):
                last[role, h, key][0].wait_recv()
                piece = planes[role].at[tile_of(h, step, b), rows_of(role, h)]
                last_f[role, h, key] = net.send(piece, piece, to_a)

    def complete(role):
        for key in range(4):
            for h in range(2):
                last[role, h, key][1].wait_recv()
                last_f[role, h, key].wait_recv()

    fetches = {}

    def fetch(which, role):
        if (which, role) in note_in:
            note_in[which, role].wait_recv()
        fetches[which, role] = start_local(notes[which][role], facts[which][role])

    def know(which, role):
        wait_local(fetches[which, role])

    def pack(role):
        know(0, role)
        rows = planes[role]
        buffer = {BACK: pk_b, FRONT: pk_f, ACROSS: pk_x}[role]
        for e in range(4):
            buffer[e] = rows[facts[0][role][4 + e, 4, 2]]
            if role == ACROSS and e % 2:
                duo = pl.ds(e - 1, 2)
                beside[role, e // 2] = net.send(buffer.at[duo], in13.at[duo], sib)
        if role != ACROSS:
            beside[role] = net.send(buffer, slots[1][role].at[:, rest], sib)
        for e in range(4):
            value = rows[facts[0][role][e, 4, 2]]
            if role == ACROSS:
                in03[e] = value
            else:
                slots[0][role][e, NEAR:TILE] = value

    labels = lax.broadcasted_iota(jnp.int32, (BLOCK, TILE), 0)
    returns = {}

    def pairs(which, role, half):
        block_of, rows, info, out = (
            facts[which][role], slots[which][role], notes[which][role], outs[which][role]
        )
        group = pl.ds(4 * role, 4)
        if half == 0:
            if which == 1 or role == OWN:
                know(which, role)
            if (which, role) in direct:
                direct[which, role].wait_recv()
            if which == 1 and role != ACROSS:
                beside[role].wait_recv()
        if which == 1 and role == ACROSS:
            beside[role, half].wait_recv()
        both = (2 * half, 2 * half + 1)
        blocks = [vectors[block_of[4 * which + e, 4, 4]] for e in both]
        scores = [mm(block, rows[e], 1, 1) for e, block in zip(both, blocks)]
        for e, block, score in zip(both, blocks, scores):
            delta = delta_of(score, labels, info[4 * which + e])
            held_delta[which, 4 * role + e] = delta
            out[e] = mm(delta, block, 0, 0).astype(BF16)
            at = 16 * which + 4 * role + e
            plan[at : at + 1, :] = info[4 * which + e, 4:5, :]
        if half == 1:
            start_local(rows, sel.at[which, group])
            start_local(held_delta.at[which, group], deltas.at[which, group])
            for e in (2, 1, 0):
                out[e] = out[e] + out[block_of[4 * which + e, 4, 1]]

    row_halves = (pl.ds(0, TILE // 2), pl.ds(TILE // 2, TILE // 2))
    ret_a0, ret_a1, ret_b0, ret_b1 = (a0_0, a0_1), (a1_0, a1_1), (b0_0, b0_1), (b1_0, b1_1)
    four = pl.ds(0, 4)

    def give_back(which, role, r):
        out = outs[which][role]
        back = {
            (0, BACK): (ret_a0, down),
            (0, FRONT): (ret_b0, up),
            (1, BACK): (ret_a1, up_other),
            (1, FRONT): (ret_b1, down_other),
        }[which, role]
        returns[which, role, r] = net.send(
            out.at[four, row_halves[r]], back[0][r].at[four], back[1]
        )

    for ref in outs[0] + outs[1] + (ret_own, ret_x):
        ref[4] = jnp.zeros((TILE, D), BF16)
    for ref in ret_a0 + ret_a1 + ret_b0 + ret_b1:
        ref[4] = jnp.zeros((TILE // 2, D), BF16)
    steps = (0, b, a, 2)
    first_axis = ((xa, xb), (za, zb))
    first2, firsta, firstb = {}, {}, {}
    second2, seconda, secondb = {}, {}, {}
    term_in = {}

    def part(h, stream, unit, j):
        tile = me.tile(steps[unit], steps[j]) if h == 0 else me.tile(steps[j], steps[unit])
        cols = slice(h * HALF, (h + 1) * HALF)
        r = stream % 2
        rows = slice(r * TILE // 2, (r + 1) * TILE // 2)
        if stream < 2:
            return out_x[sm03[8, 0, tile], rows, cols] + ret_x[sm03[8, 1, tile], rows, cols]
        value = out_own[smo[32 + 2 * OWN, tile], rows, cols]
        value += ret_own[smo[33 + 2 * OWN, tile], rows, cols]
        value += ret_a0[r][smo[32 + 2 * BACK, tile], :, cols]
        value += ret_a1[r][smo[33 + 2 * BACK, tile], :, cols]
        value += ret_b0[r][smo[32 + 2 * FRONT, tile], :, cols]
        return value + ret_b1[r][smo[33 + 2 * FRONT, tile], :, cols]

    def begin_sum(stream):
        if stream == 0:
            term_in[ACROSS].wait_recv()
        if stream >= 2:
            if stream == 2:
                term_in[OWN].wait_recv()
            for which in range(2):
                for role in (BACK, FRONT):
                    returns[which, role, stream - 2].wait_recv()
        for h in range(2):
            for j in range(4):
                s2[h, stream, j] = part(h, stream, ACROSS, j)
            first2[h, stream] = net.send(s2.at[h, stream], r2.at[h, stream], first_axis[h][0])
            for j in range(4):
                sb[h, stream, j] = part(h, stream, BACK, j)
            firstb[h, stream] = net.send(sb.at[h, stream], rb.at[h, stream], first_axis[h][1])

    def pass_sum(stream):
        for h in range(2):
            first2[h, stream].wait_recv()
            for j in range(4):
                r2[h, stream, j] = r2[h, stream, j] + part(h, stream, FRONT, j)
            firsta[h, stream] = net.send(r2.at[h, stream], ra.at[h, stream], first_axis[h][0])

    def begin_second(stream):
        for h in range(2):
            firstb[h, stream].wait_recv()
            firsta[h, stream].wait_recv()
            to_a, to_b = first_axis[1 - h]
            for j in (ACROSS, BACK, FRONT, OWN):
                rb[h, stream, j] = part(h, stream, OWN, j) + rb[h, stream, j] + ra[h, stream, j]
                if j == ACROSS:
                    second2[h, stream] = net.send(rb.at[h, stream, j], u2.at[h, stream], to_a)
                if j == BACK:
                    secondb[h, stream] = net.send(rb.at[h, stream, j], ub.at[h, stream], to_b)

    def pass_second(stream):
        for h in range(2):
            second2[h, stream].wait_recv()
            u2[h, stream] = u2[h, stream] + rb[h, stream, FRONT]
            seconda[h, stream] = net.send(u2.at[h, stream], ua.at[h, stream], first_axis[1 - h][0])

    def end_second(stream):
        for h in range(2):
            secondb[h, stream].wait_recv()
            seconda[h, stream].wait_recv()
            ub[h, stream] = rb[h, stream, OWN] + ub[h, stream] + ua[h, stream]

    fetch(0, OWN)
    send_second(BACK)
    send_second(FRONT)
    send_last(BACK, OWN)
    send_second(ACROSS)
    for load in load_v:
        wait_local(load)
    pairs(0, OWN, 0)
    second_stage(BACK)
    cz_a.wait_recv()
    pos_b = cpall.at[me.x, lax.rem(me.z + b, NZ)]
    cz_f = net.send(pos_b, pos_b, za)
    send_last(FRONT, OWN)
    pairs(0, OWN, 1)
    second_stage(FRONT)
    across_stage(BACK)
    fetch(1, OWN)
    fetch(0, BACK)
    fetch(0, FRONT)
    cz_b.wait_recv()
    cz_f.wait_recv()
    pos_row = cpall.at[me.x]
    cx_a = net.send(pos_row, pos_row, xa)
    cx_b = net.send(pos_row, pos_row, xb)
    forward_last(BACK)
    pairs(1, OWN, 0)
    across_stage(FRONT)
    send_last(ACROSS, OWN)
    second_stage(ACROSS)
    pairs(1, OWN, 1)
    term_in[OWN] = net.send(out1o.at[four], ret_own.at[four], sib)
    complete(BACK)
    pack(BACK)
    across_stage(ACROSS)
    forward_last(FRONT)
    cx_a.wait_recv()
    pos_row_b = cpall.at[lax.rem(me.x + b, NX)]
    cx_f = net.send(pos_row_b, pos_row_b, xa)
    pairs(0, BACK, 0)
    pairs(0, BACK, 1)
    give_back(0, BACK, 0)
    fetch(1, BACK)
    fetch(1, FRONT)
    fetch(0, ACROSS)
    note_in[1, ACROSS] = net.send(no03, no13, sib)
    complete(FRONT)
    pack(FRONT)
    pairs(0, FRONT, 0)
    pairs(0, FRONT, 1)
    give_back(0, FRONT, 0)
    forward_last(ACROSS)
    pairs(1, BACK, 0)
    pairs(1, BACK, 1)
    give_back(1, BACK, 0)
    fetch(1, ACROSS)
    pairs(1, FRONT, 0)
    pairs(1, FRONT, 1)
    give_back(1, FRONT, 0)
    for role in (BACK, FRONT):
        for which in range(2):
            give_back(which, role, 1)
    complete(ACROSS)
    pack(ACROSS)
    pairs(0, ACROSS, 0)
    pairs(1, ACROSS, 0)
    pairs(1, ACROSS, 1)
    term_in[ACROSS] = net.send(out1x.at[four], ret_x.at[four], sib)
    pairs(0, ACROSS, 1)
    begin_sum(2)
    wait_local(load_c)
    for j in range(8):
        color, role = j // 4, j % 4
        row = (2 * lax.rem(me.y + role_step(color, role), NY) + color) * TILES + m
        start = pl.multiple_of(row * 16, 16)
        cvm[pl.ds(16 * j, 16), :] = cvv[pl.ds(start, 16), :]
    place = lax.broadcasted_iota(jnp.int32, (128, 128), 0)
    chunk = place // 16
    color, role = chunk // 4, lax.rem(chunk, 4)
    step = jnp.where(role == ACROSS, 2, jnp.where(role == FRONT, 1 + 2 * color, 3 - 2 * color))
    step = jnp.where(role == OWN, 0, step)
    owner_grp = 2 * lax.rem(me.y + step, NY) + color
    coarse_ids = (owner_grp * TILES + m) * 16 + lax.rem(place, 16)

    def own_coarse():
        qm = q_own[m]
        total = jnp.zeros((TILE, D), F32)
        for i in range(COARSE // BLOCK):
            vectors = cvv[i * BLOCK : (i + 1) * BLOCK, :]
            labels = lax.broadcasted_iota(jnp.int32, (BLOCK, TILE), 0) + i * BLOCK
            delta = delta_of(mm(vectors, qm, 1, 1), labels, cpall[me.x, me.z])
            total += mm(delta, vectors, 0, 0)
        qc[...] = total

    def rows_coarse(lo, hi):
        def body(t, carry):
            qt = q_own[pl.ds(2 * t, 2)].reshape(2 * TILE, D)
            scores = mm(cvm[...], qt, 1, 1)
            delta = jnp.concatenate(
                [
                    delta_of(
                        scores[:, h * TILE : (h + 1) * TILE],
                        coarse_ids,
                        cpall[t // 2, 2 * lax.rem(t, 2) + h],
                    )
                    for h in range(2)
                ],
                axis=1,
            )
            gc[...] += mm(delta, qt, 1, 0)
            return carry

        lax.fori_loop(lo, hi, body, 0)


    gc[...] = jnp.zeros_like(gc)
    cx_b.wait_recv()
    cx_f.wait_recv()
    rows_coarse(0, 4)
    begin_sum(0)
    begin_sum(1)
    pass_sum(2)
    rows_coarse(4, 8)
    coarse = net.send(gc.at[pl.ds(64 * (1 - c), 64)], gsib, sib)
    pass_sum(0)
    pass_sum(1)
    begin_sum(3)
    begin_second(2)
    own_coarse()
    begin_second(0)
    begin_second(1)
    pass_sum(3)
    pass_second(2)
    pass_second(0)
    pass_second(1)
    coarse.wait_recv()
    for role in range(4):
        gbuf[role] = gc[pl.ds(64 * c + 16 * role, 16)] + gsib[16 * role : 16 * role + 16]
    coarse2 = net.send(gbuf.at[ACROSS], gbuf.at[5], up)
    coarseb = net.send(gbuf.at[BACK], gbuf.at[6], down)
    end_second(0)
    end_second(1)
    home = net.send(ub.at[:, pl.ds(0, 2)], far, across)
    begin_second(3)
    end_second(2)
    coarse2.wait_recv()
    gbuf[4] = gbuf[FRONT] + gbuf[5]
    coarsea = net.send(gbuf.at[4], gbuf.at[7], up)
    pass_second(3)
    coarsea.wait_recv()
    coarseb.wait_recv()
    gco[...] = gbuf[OWN] + gbuf[6] + gbuf[7]
    home.wait_recv()
    end_second(3)
    for h in range(2):
        cols = slice(h * HALF, (h + 1) * HALF)
        for r in range(2):
            rows = slice(r * TILE // 2, (r + 1) * TILE // 2)
            gq[rows, cols] = (
                qc[rows, cols] + ub[h, 2 + r].astype(F32) + far[h, r].astype(F32)
            )
    for copy in local:
        if not any(copy is other for other in done):
            copy.wait()
    net.finish()


def grads_kernel(
    plan, sel, deltas,
    gm, gl,
    counts, entries, rows, held, acc, row_sem, delta_sem, grad_sem,
):
    stores = [(gm, 0), (gm, 1), (gm, 2), (gm, 3), (gl, 0), (gl, 1)]

    def row_copy(e):
        return pltpu.make_async_copy(sel.at[e], rows.at[e], row_sem.at[e])

    def delta_copy(e):
        return pltpu.make_async_copy(deltas.at[e], held.at[e], delta_sem.at[e])

    for key in range(6):
        counts[key] = 0
    for e in range(SLOTS):
        block = plan[e, 0]

        @pl.when(block >= 0)
        def _():
            row_copy(e).start()
            delta_copy(e).start()
            key = block + 4 * (e // 2 % 2)
            n = counts[key]
            entries[LIST * key + n] = e
            counts[key] = n + 1

    rows[SLOTS] = jnp.zeros((TILE, D), BF16)
    held[SLOTS] = jnp.zeros((BLOCK, TILE), BF16)

    def per_key(key, carry):
        n = counts[key]
        start = LIST * key

        @pl.when(n == 0)
        def _():
            acc[key] = jnp.zeros((BLOCK, D), F32)

        def batch(i, inner):
            at = start + 2 * i
            full = 2 * i + 1 < n
            e0 = entries[at]
            e1 = jnp.where(full, entries[at + 1], SLOTS)
            row_copy(e0).wait()
            delta_copy(e0).wait()

            @pl.when(full)
            def _():
                row_copy(e1).wait()
                delta_copy(e1).wait()

            both = jnp.concatenate([rows[e0], rows[e1]], axis=0)
            delta = jnp.concatenate([held[e0], held[e1]], axis=1)

            @pl.when(i == 0)
            def _():
                for n_col in range(3):
                    cols = slice(n_col * THIRD, (n_col + 1) * THIRD)
                    acc[key, :, cols] = mm(delta, both[:, cols], 1, 0)

            @pl.when(i != 0)
            def _():
                for n_col in range(3):
                    cols = slice(n_col * THIRD, (n_col + 1) * THIRD)
                    acc[key, :, cols] += mm(delta, both[:, cols], 1, 0)

            return inner

        lax.fori_loop(0, (n + 1) // 2, batch, 0)
        for i, (out, j) in enumerate(stores):

            @pl.when(key == i)
            def _():
                pltpu.make_async_copy(acc.at[i], out.at[j], grad_sem.at[i]).start()

        return carry

    lax.fori_loop(0, 6, per_key, 0)
    for i, (out, j) in enumerate(stores):
        pltpu.make_async_copy(acc.at[i], out.at[j], grad_sem.at[i]).wait()


def vmem():
    return pl.BlockSpec(memory_space=pltpu.VMEM)


def smem():
    return pl.BlockSpec(memory_space=pltpu.SMEM)


def hbm():
    return pl.BlockSpec(memory_space=pl.ANY)


def shape(dims, dtype):
    return jax.ShapeDtypeStruct(dims, dtype)


def shards(
    queries,
    coarse_vectors,
    mid_vectors,
    leaf_vectors,
    coarse_pos,
    mid_pos,
    leaf_pos,
    mid_cand,
    leaf_cand,
    leaf_owner,
):
    dma = pltpu.SemaphoreType.DMA
    mib = 1024 * 1024
    group = pltpu.VMEM((TILES, TILE, D), BF16)
    part = pltpu.VMEM((TILES, REST, D), BF16)
    four = pltpu.VMEM((4, TILE, D), BF16)
    five = pltpu.VMEM((5, TILE, D), BF16)
    half = pltpu.VMEM((5, TILE // 2, D), BF16)
    near = pltpu.VMEM((4, NEAR, D), BF16)
    rest = pltpu.VMEM((4, REST, D), BF16)
    notes = pltpu.VMEM((9, 8, 128), jnp.int32)
    facts = pltpu.SMEM((9, 8, 128), jnp.int32)
    first = pltpu.VMEM((2, 4, 4, TILE // 2, HALF), BF16)
    second = pltpu.VMEM((2, 4, TILE // 2, HALF), BF16)
    gq, gco, plan, sel, deltas = pl.pallas_call(
        main_kernel,
        out_shape=(
            shape((TILE, D), F32),
            shape((16, D), F32),
            shape((SLOTS, 128), jnp.int32),
            shape((2, 16, TILE, D), BF16),
            shape((2, 16, BLOCK, TILE), BF16),
        ),
        in_specs=[hbm(), vmem(), vmem(), vmem(), vmem(), vmem(), vmem(), hbm(), hbm(), hbm()],
        out_specs=(vmem(), vmem(), vmem(), hbm(), hbm()),
        scratch_shapes=[
            group, part, part, group,
            pltpu.VMEM((18, 8, 128), jnp.int32),
            pltpu.VMEM((COARSE, D), BF16),
            pltpu.VMEM((128, D), BF16),
            pltpu.VMEM((NX, NZ, 8, TILE), jnp.int32),
            four, four, four, four, four, four, four, four,
            notes, notes, notes, notes, notes, notes, notes, notes,
            facts, facts, facts, facts, facts, facts, facts, facts,
            notes, notes, notes,
            pltpu.VMEM((40, 128), jnp.int32),
            pltpu.SMEM((40, 128), jnp.int32),
            near, near, near, near, four, four, rest, rest,
            five, five, five, five, five, five, five, five,
            five, five,
            half, half, half, half, half, half, half, half,
            pltpu.VMEM((6, BLOCK, D), BF16),
            pltpu.VMEM((2, 16, BLOCK, TILE), BF16),
            pltpu.VMEM((128, D), F32),
            pltpu.VMEM((TILE, D), F32),
            pltpu.VMEM((64, D), F32),
            pltpu.VMEM((8, 16, D), F32),
            first, first, first, first, first,
            second, second, second,
            pltpu.VMEM((2, 2, TILE // 2, HALF), BF16),
            dma((40,)),
            dma((COPIES,)),
            dma((COPIES,)),
        ],
        compiler_params=pltpu.CompilerParams(
            collective_id=0, has_side_effects=True, vmem_limit_bytes=62 * mib
        ),
        name="main",
    )(
        queries.reshape(TILES, TILE, D),
        mid_pos.T,
        leaf_pos.T,
        mid_cand.T,
        leaf_cand.T,
        coarse_pos.T,
        leaf_owner.reshape(2, 128),
        coarse_vectors,
        mid_vectors.reshape(4, BLOCK, D),
        leaf_vectors.reshape(2, BLOCK, D),
    )
    gm, gl = pl.pallas_call(
        grads_kernel,
        out_shape=(shape((4, BLOCK, D), F32), shape((2, BLOCK, D), F32)),
        in_specs=[smem(), hbm(), hbm()],
        out_specs=(hbm(), hbm()),
        scratch_shapes=[
            pltpu.SMEM((6,), jnp.int32),
            pltpu.SMEM((6 * LIST + 1,), jnp.int32),
            pltpu.VMEM((SLOTS + 1, TILE, D), BF16),
            pltpu.VMEM((SLOTS + 1, BLOCK, TILE), BF16),
            pltpu.VMEM((6, BLOCK, D), F32),
            dma((SLOTS,)),
            dma((SLOTS,)),
            dma((6,)),
        ],
        compiler_params=pltpu.CompilerParams(vmem_limit_bytes=60 * mib),
        name="grads",
    )(plan, sel.reshape(SLOTS, TILE, D), deltas.reshape(SLOTS, BLOCK, TILE))
    return gq, gco, gm.reshape(4 * BLOCK, D), gl.reshape(2 * BLOCK, D)


def solution(mesh):
    placed = (
        P("grp", None),
        P(),
        P(("grp", "mid"), None),
        P(("grp", "mid"), None),
        P(("grp", "mid"), None),
        P("grp", None),
        P("grp", None),
        P("grp", None),
        P("grp", None),
        P(),
    )
    return jax.shard_map(
        shards,
        mesh=mesh,
        in_specs=placed,
        out_specs=(
            P(("grp", "mid"), None),
            P(("grp", "mid"), None),
            P(("grp", "mid"), None),
            P(("grp", "mid"), None),
        ),
        check_vma=False,
    )
```

```python
import jax
import jax.numpy as jnp
from jax import lax
from jax.experimental import pallas as pl
from jax.experimental.pallas import tpu as pltpu
from jax.sharding import PartitionSpec as P

TILE = 128
BLOCK = 512
COARSE = 2048
K_CAND = 8
D = 768
NY, NX, NZ = 4, 4, 4
TILES = NX * NZ
BIG = 1 << 20
F32 = jnp.float32
BF16 = jnp.bfloat16
MESH = pl.DeviceIdType.MESH
THIRD = D // 3
HALF = D // 2
NEAR = 96
REST = TILE - NEAR


def mm(a, b, ca, cb):
    return lax.dot_general(a, b, (((ca,), (cb,)), ((), ())), preferred_element_type=F32)


def delta_of(scores, labels, positives):
    hit = labels == positives[0:1]
    for p in range(1, 4):
        hit = hit | (labels == positives[p : p + 1])
    return (0.125 * jnp.tanh(0.5 * scores) + jnp.where(hit, -0.125, 0.125)).astype(BF16)


class Place:
    def __init__(self):
        grp, mid = lax.axis_index("grp"), lax.axis_index("mid")
        self.y, self.c = grp // 2, lax.rem(grp, 2)
        self.x, self.z = mid // NZ, lax.rem(mid, NZ)
        self.mid = mid
        self.ahead = 1 + 2 * self.c
        self.behind = 3 - 2 * self.c

    def at(self, dy=0, dx=0, dz=0, other=False):
        y, x, z = lax.rem(self.y + dy, NY), lax.rem(self.x + dx, NX), lax.rem(self.z + dz, NZ)
        return (2 * y + (1 - self.c if other else self.c), NZ * x + z)

    def sibling(self):
        return (2 * self.y + 1 - self.c, self.mid)

    def tile(self, dx, dz):
        return NZ * lax.rem(self.x + dx, NX) + lax.rem(self.z + dz, NZ)

    def greet(self):
        near = [self.sibling(), self.at(dy=2)]
        for step in (self.ahead, self.behind):
            near += [self.at(dy=step), self.at(dy=step, other=True)]
            near += [self.at(dx=step), self.at(dz=step)]
        barrier = pltpu.get_barrier_semaphore()
        for device in near:
            pl.semaphore_signal(barrier, inc=1, device_id=device, device_id_type=MESH)
        pl.semaphore_wait(barrier, len(near))


class Net:
    def __init__(self, send_sem, recv_sem):
        self.send_sem, self.recv_sem, self.made = send_sem, recv_sem, []

    def send(self, src, dst, device):
        i = len(self.made)
        copy = pltpu.make_async_remote_copy(
            src_ref=src,
            dst_ref=dst,
            send_sem=self.send_sem.at[i],
            recv_sem=self.recv_sem.at[i],
            device_id=device,
            device_id_type=MESH,
        )
        copy.start()
        self.made.append(copy)
        return copy

    def finish(self):
        for copy in self.made:
            copy.wait_send()


COPIES = 200
OWN, BACK, FRONT, ACROSS = range(4)
SLOTS = 32
LIST = 16


def role_step(color, role):
    return (0, 3 - 2 * color, 1 + 2 * color, 2)[role]


def main_kernel(
    q, mp, lp, mc, lc, cp, owner, cv, midv, leafv,
    gq, gco, plan, sel, deltas,
    q_own, q_b, q_a, q_2, p_own, cvv, cvm, cpall,
    in00, in01, in02, in03, in10, in11, in12, in13,
    no00, no01, no02, no03, no10, no11, no12, no13,
    sm00, sm01, sm02, sm03, sm10, sm11, sm12, sm13,
    no_a, no_b, no_x, planv, smo, pk_as, pk_ao, pk_bs, pk_bo, pk_own, pk_x, pk_b, pk_f,
    out_own, out_x, out0b, out0f, out1o, out1b, out1f, out1x,
    ret_own, x_0, x_1, a0_0, a0_1, a1_0, a1_1, b0_0, b0_1, b1_0, b1_1,
    vectors, held_delta, gc, qc, gsib, gbuf,
    s2, sb, r2, rb, ra, u2, ub, ua, far, local_sem, send_sem, recv_sem,
):
    me = Place()
    c, a, b = me.c, me.ahead, me.behind
    net = Net(send_sem, recv_sem)
    local, done = [], []

    def start_local(src, dst):
        copy = pltpu.make_async_copy(src, dst, local_sem.at[len(local)])
        copy.start()
        local.append(copy)
        return copy

    def wait_local(copy):
        copy.wait()
        done.append(copy)

    load_q = start_local(q, q_own)
    load_v = [start_local(midv, vectors.at[pl.ds(0, 4)]), start_local(leafv, vectors.at[pl.ds(4, 2)])]
    load_c = start_local(cv, cvv)
    for t in range(TILES):
        p_own[t, 0:4, :] = mp[:, t * TILE : (t + 1) * TILE]
        p_own[t, 4:8, :] = lp[:, t * TILE : (t + 1) * TILE]
    p_own[16:18] = jnp.full((2, 8, 128), -1, jnp.int32)
    p_own[16, :, 0:TILES] = mc[...]
    p_own[17, :, 0:TILES] = lc[...]
    cpall[me.x, me.z, 0:4, :] = cp[...]
    cpall[me.x, me.z, 4:8, :] = cp[...]
    me.greet()

    m = me.mid
    up, down, across = me.at(dy=a), me.at(dy=b), me.at(dy=2)
    up_other, down_other = me.at(dy=a, other=True), me.at(dy=b, other=True)
    xa, xb, za, zb = me.at(dx=a), me.at(dx=b), me.at(dz=a), me.at(dz=b)
    sib = me.sibling()
    planes = {BACK: q_b, FRONT: q_a, ACROSS: q_2}
    slots = ((in00, in01, in02, in03), (in10, in11, in12, in13))
    notes = ((no00, no01, no02, no03), (no10, no11, no12, no13))
    facts = ((sm00, sm01, sm02, sm03), (sm10, sm11, sm12, sm13))
    outs = ((out_own, out0b, out0f, out_x), (out1o, out1b, out1f, out1x))

    rest, near = pl.ds(NEAR, REST), pl.ds(0, NEAR)
    y_in = {
        BACK: net.send(q.at[m, rest], q_b.at[m], up),
        FRONT: net.send(q.at[m, rest], q_a.at[m], down),
        ACROSS: net.send(q.at[m], q_2.at[m], across),
    }
    pos_own = cpall.at[me.x, me.z]
    cz_a = net.send(pos_own, pos_own, za)
    cz_b = net.send(pos_own, pos_own, zb)

    index = lax.broadcasted_iota(jnp.int32, (2, 128), 0) * 128 + lax.broadcasted_iota(
        jnp.int32, (2, 128), 1
    )
    code = 4 * (
        TILES * lax.broadcasted_iota(jnp.int32, (8, 128), 0)
        + lax.broadcasted_iota(jnp.int32, (8, 128), 1)
    )
    lane = lax.broadcasted_iota(jnp.int32, (1, 128), 1)
    mids, leaves = p_own[16], p_own[17]

    def whole(value):
        return jnp.broadcast_to(value, (1, 128))

    for label, step in enumerate((0, a, b, 2)):
        for which, core in enumerate((c, 1 - c)):
            device = (2 * lax.rem(me.y + step, NY) + core) * TILES + m
            held = [
                whole(
                    jnp.sum(
                        jnp.where(owner[...] == 2 * device + i, index, 0), axis=(0, 1), keepdims=True
                    )
                )
                for i in range(2)
            ]
            entries = []
            for live, block in (
                ((mids >> 2) == device, mids & 3),
                ((leaves == held[0]) | (leaves == held[1]), (leaves == held[1]).astype(jnp.int32)),
            ):
                found = code + block
                first = whole(jnp.min(jnp.where(live, found, BIG), axis=(0, 1), keepdims=True))
                final = whole(jnp.max(jnp.where(live, found, -1), axis=(0, 1), keepdims=True))
                some = first < BIG
                entries.append((some, jnp.where(some, first, 0)))
                two = some & (final != first)
                entries.append((two, jnp.where(two, final, 0)))
            tiles = [(value >> 2) & 15 for _, value in entries]
            spots = jnp.full((1, 128), 4, jnp.int32)
            for e in (3, 2, 1, 0):
                spots = jnp.where(entries[e][0] & (tiles[e] == lane), e, spots)
            at = 32 + 2 * label + which
            planv[at : at + 1, :] = spots
            for e, (valid, value) in enumerate(entries):
                follow = jnp.full((1, 128), 4, jnp.int32)
                for f in range(3, e, -1):
                    follow = jnp.where(valid & entries[f][0] & (tiles[f] == tiles[e]), f, follow)
                row = jnp.where(lane == 0, jnp.where(valid, value & 3, -1), follow)
                row = jnp.where(lane == 2, tiles[e], row)
                row = jnp.where(lane == 3, value >> 6, row)
                row = jnp.where(lane == 4, (value & 3) + 4 * (e // 2), row)
                at = 8 * label + 4 * which + e
                planv[at : at + 1, :] = row
    to_smem = start_local(planv, smo)
    wait_local(load_q)
    wait_local(to_smem)
    notes_out = (no00, no_a, no_b, no_x)

    def fill_notes(label):
        out = notes_out[label]
        for e in range(8):
            at = 8 * label + e
            level = 4 * (e % 4 // 2)
            positives = p_own[smo[at, 2]][level : level + 4] - BLOCK * smo[at, 3]
            out[e, 0:4, :] = positives
            out[e, 4:5, :] = planv[at : at + 1, :]
            out[e, 5:8, :] = jnp.zeros((3, 128), jnp.int32)
        out[8, 0:2, :] = planv[32 + 2 * label : 34 + 2 * label, :]
        out[8, 2:8, :] = jnp.zeros((6, 128), jnp.int32)

    direct, note_in = {}, {}
    for label, targets in ((BACK, ((pk_as, up), (pk_ao, up_other))), (FRONT, ((pk_bs, down), (pk_bo, down_other)))):
        fill_notes(label)
        for which, (buffer, device) in enumerate(targets):
            for e in range(4):
                buffer[e] = q_own[smo[8 * label + 4 * which + e, 2], 0:NEAR]
            note_in[which, label] = net.send(notes_out[label], notes[which][label], device)
            direct[which, label] = net.send(buffer, slots[which][label].at[:, near], device)
    fill_notes(ACROSS)
    note_in[0, ACROSS] = net.send(no_x, no03, across)
    fill_notes(OWN)
    for e in range(4):
        pk_own[e] = q_own[smo[4 + e, 2]]
    note_in[1, OWN] = net.send(no00, no10, sib)
    beside = {OWN: net.send(pk_own, in10, sib)}
    for e in range(4):
        in00[e] = q_own[smo[e, 2]]

    axes = ((za, zb, xa, xb), (xa, xb, za, zb))
    walk = (0, b, a, 2)

    def rows_of(role, h):
        size = (TILE if role == ACROSS else REST) // 2
        return pl.ds(h * size, size)

    def tile_of(h, first, last):
        return me.tile(last, first) if h == 0 else me.tile(first, last)

    second, second_f, last, last_f = {}, {}, {}, {}

    def send_second(role):
        y_in[role].wait_recv()
        for h, (to_a, to_b, _, _) in enumerate(axes):
            piece = planes[role].at[m, rows_of(role, h)]
            second[role, h] = (net.send(piece, piece, to_a), net.send(piece, piece, to_b))

    def send_last(role, key):
        for h, (_, _, to_a, to_b) in enumerate(axes):
            piece = planes[role].at[tile_of(h, walk[key], 0), rows_of(role, h)]
            last[role, h, key] = (net.send(piece, piece, to_a), net.send(piece, piece, to_b))

    def second_stage(role):
        for h, (to_a, _, _, _) in enumerate(axes):
            second[role, h][0].wait_recv()
            piece = planes[role].at[tile_of(h, b, 0), rows_of(role, h)]
            second_f[role, h] = net.send(piece, piece, to_a)
        send_last(role, BACK)
        for h in range(2):
            second[role, h][1].wait_recv()
        send_last(role, FRONT)

    def across_stage(role):
        for h in range(2):
            second_f[role, h].wait_recv()
        send_last(role, ACROSS)

    def forward_last(role):
        for key, step in enumerate(walk):
            for h, (_, _, to_a, _) in enumerate(axes):
                last[role, h, key][0].wait_recv()
                piece = planes[role].at[tile_of(h, step, b), rows_of(role, h)]
                last_f[role, h, key] = net.send(piece, piece, to_a)

    def complete(role):
        for key in range(4):
            for h in range(2):
                last[role, h, key][1].wait_recv()
                last_f[role, h, key].wait_recv()

    fetches = {}

    def fetch(which, role):
        if (which, role) in note_in:
            note_in[which, role].wait_recv()
        fetches[which, role] = start_local(notes[which][role], facts[which][role])

    def know(which, role):
        wait_local(fetches[which, role])

    def pack(role):
        know(0, role)
        rows = planes[role]
        buffer = {BACK: pk_b, FRONT: pk_f, ACROSS: pk_x}[role]
        for e in range(4):
            buffer[e] = rows[facts[0][role][4 + e, 4, 2]]
            if role == ACROSS and e % 2:
                duo = pl.ds(e - 1, 2)
                beside[role, e // 2] = net.send(buffer.at[duo], in13.at[duo], sib)
        if role != ACROSS:
            beside[role] = net.send(buffer, slots[1][role].at[:, rest], sib)
        for e in range(4):
            value = rows[facts[0][role][e, 4, 2]]
            if role == ACROSS:
                in03[e] = value
            else:
                slots[0][role][e, NEAR:TILE] = value

    labels = lax.broadcasted_iota(jnp.int32, (BLOCK, TILE), 0)
    returns = {}

    def pairs(which, role, half):
        block_of, rows, info, out = (
            facts[which][role], slots[which][role], notes[which][role], outs[which][role]
        )
        group = pl.ds(4 * role, 4)
        if half == 0:
            if which == 1 or role == OWN:
                know(which, role)
            if (which, role) in direct:
                direct[which, role].wait_recv()
            if which == 1 and role != ACROSS:
                beside[role].wait_recv()
        if which == 1 and role == ACROSS:
            beside[role, half].wait_recv()
        both = (2 * half, 2 * half + 1)
        blocks = [vectors[block_of[4 * which + e, 4, 4]] for e in both]
        scores = [mm(block, rows[e], 1, 1) for e, block in zip(both, blocks)]
        for e, block, score in zip(both, blocks, scores):
            delta = delta_of(score, labels, info[4 * which + e])
            held_delta[which, 4 * role + e] = delta
            out[e] = mm(delta, block, 0, 0).astype(BF16)
            at = 16 * which + 4 * role + e
            plan[at : at + 1, :] = info[4 * which + e, 4:5, :]
        if half == 1:
            start_local(rows, sel.at[which, group])
            start_local(held_delta.at[which, group], deltas.at[which, group])
            for e in (2, 1, 0):
                out[e] = out[e] + out[block_of[4 * which + e, 4, 1]]

    row_halves = (pl.ds(0, TILE // 2), pl.ds(TILE // 2, TILE // 2))
    ret_a0, ret_a1, ret_b0, ret_b1 = (a0_0, a0_1), (a1_0, a1_1), (b0_0, b0_1), (b1_0, b1_1)
    ret_x = (x_0, x_1)
    four = pl.ds(0, 4)

    def give_back(which, role, r):
        out = outs[which][role]
        back = {
            (0, BACK): (ret_a0, down),
            (0, FRONT): (ret_b0, up),
            (1, BACK): (ret_a1, up_other),
            (1, FRONT): (ret_b1, down_other),
        }[which, role]
        returns[which, role, r] = net.send(
            out.at[four, row_halves[r]], back[0][r].at[four], back[1]
        )

    for ref in outs[0] + outs[1] + (ret_own,):
        ref[4] = jnp.zeros((TILE, D), BF16)
    for ref in ret_x + ret_a0 + ret_a1 + ret_b0 + ret_b1:
        ref[4] = jnp.zeros((TILE // 2, D), BF16)
    steps = (0, b, a, 2)
    first_axis = ((xa, xb), (za, zb))
    first2, firsta, firstb = {}, {}, {}
    second2, seconda, secondb = {}, {}, {}
    term_in = {}

    def part(h, stream, unit, j):
        tile = me.tile(steps[unit], steps[j]) if h == 0 else me.tile(steps[j], steps[unit])
        cols = slice(h * HALF, (h + 1) * HALF)
        r = stream % 2
        rows = slice(r * TILE // 2, (r + 1) * TILE // 2)
        if stream < 2:
            return out_x[sm03[8, 0, tile], rows, cols] + ret_x[r][sm03[8, 1, tile], :, cols]
        value = out_own[smo[32 + 2 * OWN, tile], rows, cols]
        value += ret_own[smo[33 + 2 * OWN, tile], rows, cols]
        value += ret_a0[r][smo[32 + 2 * BACK, tile], :, cols]
        value += ret_a1[r][smo[33 + 2 * BACK, tile], :, cols]
        value += ret_b0[r][smo[32 + 2 * FRONT, tile], :, cols]
        return value + ret_b1[r][smo[33 + 2 * FRONT, tile], :, cols]

    def begin_sum(stream):
        if stream < 2:
            term_in[ACROSS, stream].wait_recv()
        if stream >= 2:
            if stream == 2:
                term_in[OWN].wait_recv()
            for which in range(2):
                for role in (BACK, FRONT):
                    returns[which, role, stream - 2].wait_recv()
        for h in range(2):
            for j in range(4):
                s2[h, stream, j] = part(h, stream, ACROSS, j)
            first2[h, stream] = net.send(s2.at[h, stream], r2.at[h, stream], first_axis[h][0])
            for j in range(4):
                sb[h, stream, j] = part(h, stream, BACK, j)
            firstb[h, stream] = net.send(sb.at[h, stream], rb.at[h, stream], first_axis[h][1])

    def pass_sum(stream):
        for h in range(2):
            first2[h, stream].wait_recv()
            for j in range(4):
                r2[h, stream, j] = r2[h, stream, j] + part(h, stream, FRONT, j)
            firsta[h, stream] = net.send(r2.at[h, stream], ra.at[h, stream], first_axis[h][0])

    def begin_second(stream):
        for h in range(2):
            firstb[h, stream].wait_recv()
            firsta[h, stream].wait_recv()
            to_a, to_b = first_axis[1 - h]
            for j in (ACROSS, BACK, FRONT, OWN):
                rb[h, stream, j] = part(h, stream, OWN, j) + rb[h, stream, j] + ra[h, stream, j]
                if j == ACROSS:
                    second2[h, stream] = net.send(rb.at[h, stream, j], u2.at[h, stream], to_a)
                if j == BACK:
                    secondb[h, stream] = net.send(rb.at[h, stream, j], ub.at[h, stream], to_b)

    def pass_second(stream):
        for h in range(2):
            second2[h, stream].wait_recv()
            u2[h, stream] = u2[h, stream] + rb[h, stream, FRONT]
            seconda[h, stream] = net.send(u2.at[h, stream], ua.at[h, stream], first_axis[1 - h][0])

    def end_second(stream):
        for h in range(2):
            secondb[h, stream].wait_recv()
            seconda[h, stream].wait_recv()
            ub[h, stream] = rb[h, stream, OWN] + ub[h, stream] + ua[h, stream]

    fetch(0, OWN)
    send_second(BACK)
    send_second(FRONT)
    send_last(BACK, OWN)
    send_second(ACROSS)
    for load in load_v:
        wait_local(load)
    pairs(0, OWN, 0)
    second_stage(BACK)
    cz_a.wait_recv()
    pos_b = cpall.at[me.x, lax.rem(me.z + b, NZ)]
    cz_f = net.send(pos_b, pos_b, za)
    send_last(FRONT, OWN)
    pairs(0, OWN, 1)
    second_stage(FRONT)
    across_stage(BACK)
    fetch(1, OWN)
    fetch(0, BACK)
    fetch(0, FRONT)
    cz_b.wait_recv()
    cz_f.wait_recv()
    pos_row = cpall.at[me.x]
    cx_a = net.send(pos_row, pos_row, xa)
    cx_b = net.send(pos_row, pos_row, xb)
    forward_last(BACK)
    pairs(1, OWN, 0)
    across_stage(FRONT)
    send_last(ACROSS, OWN)
    second_stage(ACROSS)
    pairs(1, OWN, 1)
    term_in[OWN] = net.send(out1o.at[four], ret_own.at[four], sib)
    complete(BACK)
    pack(BACK)
    across_stage(ACROSS)
    forward_last(FRONT)
    cx_a.wait_recv()
    pos_row_b = cpall.at[lax.rem(me.x + b, NX)]
    cx_f = net.send(pos_row_b, pos_row_b, xa)
    pairs(0, BACK, 0)
    pairs(0, BACK, 1)
    give_back(0, BACK, 0)
    fetch(1, BACK)
    fetch(1, FRONT)
    fetch(0, ACROSS)
    note_in[1, ACROSS] = net.send(no03, no13, sib)
    complete(FRONT)
    pack(FRONT)
    pairs(0, FRONT, 0)
    pairs(0, FRONT, 1)
    give_back(0, FRONT, 0)
    forward_last(ACROSS)
    pairs(1, BACK, 0)
    pairs(1, BACK, 1)
    give_back(1, BACK, 0)
    fetch(1, ACROSS)
    pairs(1, FRONT, 0)
    pairs(1, FRONT, 1)
    give_back(1, FRONT, 0)
    for role in (BACK, FRONT):
        for which in range(2):
            give_back(which, role, 1)
    complete(ACROSS)
    pack(ACROSS)
    pairs(0, ACROSS, 0)
    pairs(1, ACROSS, 0)
    pairs(1, ACROSS, 1)
    for r in range(2):
        term_in[ACROSS, r] = net.send(out1x.at[four, row_halves[r]], ret_x[r].at[four], sib)
    pairs(0, ACROSS, 1)
    begin_sum(2)
    wait_local(load_c)
    for j in range(8):
        color, role = j // 4, j % 4
        row = (2 * lax.rem(me.y + role_step(color, role), NY) + color) * TILES + m
        start = pl.multiple_of(row * 16, 16)
        cvm[pl.ds(16 * j, 16), :] = cvv[pl.ds(start, 16), :]
    place = lax.broadcasted_iota(jnp.int32, (128, 128), 0)
    chunk = place // 16
    color, role = chunk // 4, lax.rem(chunk, 4)
    step = jnp.where(role == ACROSS, 2, jnp.where(role == FRONT, 1 + 2 * color, 3 - 2 * color))
    step = jnp.where(role == OWN, 0, step)
    owner_grp = 2 * lax.rem(me.y + step, NY) + color
    coarse_ids = (owner_grp * TILES + m) * 16 + lax.rem(place, 16)

    def own_coarse():
        qm = q_own[m]
        total = jnp.zeros((TILE, D), F32)
        for i in range(COARSE // BLOCK):
            vectors = cvv[i * BLOCK : (i + 1) * BLOCK, :]
            labels = lax.broadcasted_iota(jnp.int32, (BLOCK, TILE), 0) + i * BLOCK
            delta = delta_of(mm(vectors, qm, 1, 1), labels, cpall[me.x, me.z])
            total += mm(delta, vectors, 0, 0)
        qc[...] = total

    def rows_coarse(lo, hi):
        def body(t, carry):
            qt = q_own[pl.ds(2 * t, 2)].reshape(2 * TILE, D)
            scores = mm(cvm[...], qt, 1, 1)
            delta = jnp.concatenate(
                [
                    delta_of(
                        scores[:, h * TILE : (h + 1) * TILE],
                        coarse_ids,
                        cpall[t // 2, 2 * lax.rem(t, 2) + h],
                    )
                    for h in range(2)
                ],
                axis=1,
            )
            gc[...] += mm(delta, qt, 1, 0)
            return carry

        lax.fori_loop(lo, hi, body, 0)


    gc[...] = jnp.zeros_like(gc)
    cx_b.wait_recv()
    cx_f.wait_recv()
    rows_coarse(0, 4)
    begin_sum(0)
    begin_sum(1)
    pass_sum(2)
    rows_coarse(4, 8)
    coarse = net.send(gc.at[pl.ds(64 * (1 - c), 64)], gsib, sib)
    pass_sum(0)
    pass_sum(1)
    begin_sum(3)
    begin_second(2)
    own_coarse()
    begin_second(0)
    begin_second(1)
    pass_sum(3)
    pass_second(2)
    pass_second(0)
    pass_second(1)
    coarse.wait_recv()
    for role in range(4):
        gbuf[role] = gc[pl.ds(64 * c + 16 * role, 16)] + gsib[16 * role : 16 * role + 16]
    coarse2 = net.send(gbuf.at[ACROSS], gbuf.at[5], up)
    coarseb = net.send(gbuf.at[BACK], gbuf.at[6], down)
    end_second(0)
    end_second(1)
    home = net.send(ub.at[:, pl.ds(0, 2)], far, across)
    begin_second(3)
    end_second(2)
    coarse2.wait_recv()
    gbuf[4] = gbuf[FRONT] + gbuf[5]
    coarsea = net.send(gbuf.at[4], gbuf.at[7], up)
    pass_second(3)
    coarsea.wait_recv()
    coarseb.wait_recv()
    gco[...] = gbuf[OWN] + gbuf[6] + gbuf[7]
    home.wait_recv()
    end_second(3)
    for h in range(2):
        cols = slice(h * HALF, (h + 1) * HALF)
        for r in range(2):
            rows = slice(r * TILE // 2, (r + 1) * TILE // 2)
            gq[rows, cols] = (
                qc[rows, cols] + ub[h, 2 + r].astype(F32) + far[h, r].astype(F32)
            )
    for copy in local:
        if not any(copy is other for other in done):
            copy.wait()
    net.finish()


def grads_kernel(
    plan, sel, deltas, gq_in, gco_in,
    gm, gl, gq, gco,
    counts, entries, rows, held, acc, row_sem, delta_sem, grad_sem, out_sem,
):
    results = [
        pltpu.make_async_copy(gq_in, gq, out_sem.at[0]),
        pltpu.make_async_copy(gco_in, gco, out_sem.at[1]),
    ]
    for copy in results:
        copy.start()
    stores = [(gm, 0), (gm, 1), (gm, 2), (gm, 3), (gl, 0), (gl, 1)]

    def row_copy(e):
        return pltpu.make_async_copy(sel.at[e], rows.at[e], row_sem.at[e])

    def delta_copy(e):
        return pltpu.make_async_copy(deltas.at[e], held.at[e], delta_sem.at[e])

    for key in range(6):
        counts[key] = 0
    for e in range(SLOTS):
        block = plan[e, 0]

        @pl.when(block >= 0)
        def _():
            row_copy(e).start()
            delta_copy(e).start()
            key = block + 4 * (e // 2 % 2)
            n = counts[key]
            entries[LIST * key + n] = e
            counts[key] = n + 1

    rows[SLOTS] = jnp.zeros((TILE, D), BF16)
    held[SLOTS] = jnp.zeros((BLOCK, TILE), BF16)

    def per_key(key, carry):
        n = counts[key]
        start = LIST * key

        @pl.when(n == 0)
        def _():
            acc[key] = jnp.zeros((BLOCK, D), F32)

        def batch(i, inner):
            at = start + 2 * i
            full = 2 * i + 1 < n
            e0 = entries[at]
            e1 = jnp.where(full, entries[at + 1], SLOTS)
            row_copy(e0).wait()
            delta_copy(e0).wait()

            @pl.when(full)
            def _():
                row_copy(e1).wait()
                delta_copy(e1).wait()

            both = jnp.concatenate([rows[e0], rows[e1]], axis=0)
            delta = jnp.concatenate([held[e0], held[e1]], axis=1)

            @pl.when(i == 0)
            def _():
                for n_col in range(3):
                    cols = slice(n_col * THIRD, (n_col + 1) * THIRD)
                    acc[key, :, cols] = mm(delta, both[:, cols], 1, 0)

            @pl.when(i != 0)
            def _():
                for n_col in range(3):
                    cols = slice(n_col * THIRD, (n_col + 1) * THIRD)
                    acc[key, :, cols] += mm(delta, both[:, cols], 1, 0)

            return inner

        lax.fori_loop(0, (n + 1) // 2, batch, 0)
        for i, (out, j) in enumerate(stores):

            @pl.when(key == i)
            def _():
                pltpu.make_async_copy(acc.at[i], out.at[j], grad_sem.at[i]).start()

        return carry

    lax.fori_loop(0, 6, per_key, 0)
    for i, (out, j) in enumerate(stores):
        pltpu.make_async_copy(acc.at[i], out.at[j], grad_sem.at[i]).wait()
    for copy in results:
        copy.wait()


def vmem():
    return pl.BlockSpec(memory_space=pltpu.VMEM)


def smem():
    return pl.BlockSpec(memory_space=pltpu.SMEM)


def hbm():
    return pl.BlockSpec(memory_space=pl.ANY)


def shape(dims, dtype):
    return jax.ShapeDtypeStruct(dims, dtype)


def shards(
    queries,
    coarse_vectors,
    mid_vectors,
    leaf_vectors,
    coarse_pos,
    mid_pos,
    leaf_pos,
    mid_cand,
    leaf_cand,
    leaf_owner,
):
    dma = pltpu.SemaphoreType.DMA
    mib = 1024 * 1024
    group = pltpu.VMEM((TILES, TILE, D), BF16)
    part = pltpu.VMEM((TILES, REST, D), BF16)
    four = pltpu.VMEM((4, TILE, D), BF16)
    five = pltpu.VMEM((5, TILE, D), BF16)
    half = pltpu.VMEM((5, TILE // 2, D), BF16)
    near = pltpu.VMEM((4, NEAR, D), BF16)
    rest = pltpu.VMEM((4, REST, D), BF16)
    notes = pltpu.VMEM((9, 8, 128), jnp.int32)
    facts = pltpu.SMEM((9, 8, 128), jnp.int32)
    first = pltpu.VMEM((2, 4, 4, TILE // 2, HALF), BF16)
    second = pltpu.VMEM((2, 4, TILE // 2, HALF), BF16)
    gq, gco, plan, sel, deltas = pl.pallas_call(
        main_kernel,
        out_shape=(
            shape((TILE, D), F32),
            shape((16, D), F32),
            shape((SLOTS, 128), jnp.int32),
            shape((2, 16, TILE, D), BF16),
            shape((2, 16, BLOCK, TILE), BF16),
        ),
        in_specs=[hbm(), vmem(), vmem(), vmem(), vmem(), vmem(), vmem(), hbm(), hbm(), hbm()],
        out_specs=(vmem(), vmem(), vmem(), hbm(), hbm()),
        scratch_shapes=[
            group, part, part, group,
            pltpu.VMEM((18, 8, 128), jnp.int32),
            pltpu.VMEM((COARSE, D), BF16),
            pltpu.VMEM((128, D), BF16),
            pltpu.VMEM((NX, NZ, 8, TILE), jnp.int32),
            four, four, four, four, four, four, four, four,
            notes, notes, notes, notes, notes, notes, notes, notes,
            facts, facts, facts, facts, facts, facts, facts, facts,
            notes, notes, notes,
            pltpu.VMEM((40, 128), jnp.int32),
            pltpu.SMEM((40, 128), jnp.int32),
            near, near, near, near, four, four, rest, rest,
            five, five, five, five, five, five, five, five,
            five,
            half, half, half, half, half, half, half, half, half, half,
            pltpu.VMEM((6, BLOCK, D), BF16),
            pltpu.VMEM((2, 16, BLOCK, TILE), BF16),
            pltpu.VMEM((128, D), F32),
            pltpu.VMEM((TILE, D), F32),
            pltpu.VMEM((64, D), F32),
            pltpu.VMEM((8, 16, D), F32),
            first, first, first, first, first,
            second, second, second,
            pltpu.VMEM((2, 2, TILE // 2, HALF), BF16),
            dma((40,)),
            dma((COPIES,)),
            dma((COPIES,)),
        ],
        compiler_params=pltpu.CompilerParams(
            collective_id=0, has_side_effects=True, vmem_limit_bytes=62 * mib
        ),
        name="main",
    )(
        queries.reshape(TILES, TILE, D),
        mid_pos.T,
        leaf_pos.T,
        mid_cand.T,
        leaf_cand.T,
        coarse_pos.T,
        leaf_owner.reshape(2, 128),
        coarse_vectors,
        mid_vectors.reshape(4, BLOCK, D),
        leaf_vectors.reshape(2, BLOCK, D),
    )
    gm, gl, gq, gco = pl.pallas_call(
        grads_kernel,
        out_shape=(
            shape((4, BLOCK, D), F32),
            shape((2, BLOCK, D), F32),
            shape((TILE, D), F32),
            shape((16, D), F32),
        ),
        in_specs=[smem(), hbm(), hbm(), hbm(), hbm()],
        out_specs=(hbm(), hbm(), hbm(), hbm()),
        scratch_shapes=[
            pltpu.SMEM((6,), jnp.int32),
            pltpu.SMEM((6 * LIST + 1,), jnp.int32),
            pltpu.VMEM((SLOTS + 1, TILE, D), BF16),
            pltpu.VMEM((SLOTS + 1, BLOCK, TILE), BF16),
            pltpu.VMEM((6, BLOCK, D), F32),
            dma((SLOTS,)),
            dma((SLOTS,)),
            dma((6,)),
            dma((2,)),
        ],
        compiler_params=pltpu.CompilerParams(vmem_limit_bytes=60 * mib),
        name="grads",
    )(plan, sel.reshape(SLOTS, TILE, D), deltas.reshape(SLOTS, BLOCK, TILE), gq, gco)
    return gq, gco, gm.reshape(4 * BLOCK, D), gl.reshape(2 * BLOCK, D)


def solution(mesh):
    placed = (
        P("grp", None),
        P(),
        P(("grp", "mid"), None),
        P(("grp", "mid"), None),
        P(("grp", "mid"), None),
        P("grp", None),
        P("grp", None),
        P("grp", None),
        P("grp", None),
        P(),
    )
    return jax.shard_map(
        shards,
        mesh=mesh,
        in_specs=placed,
        out_specs=(
            P(("grp", "mid"), None),
            P(("grp", "mid"), None),
            P(("grp", "mid"), None),
            P(("grp", "mid"), None),
        ),
        check_vma=False,
    )
```

```python
import jax
import jax.numpy as jnp
from jax import lax
from jax.experimental import pallas as pl
from jax.experimental.pallas import tpu as pltpu
from jax.sharding import PartitionSpec as P

TILE = 128
BLOCK = 512
COARSE = 2048
K_CAND = 8
D = 768
NY, NX, NZ = 4, 4, 4
TILES = NX * NZ
BIG = 1 << 20
F32 = jnp.float32
BF16 = jnp.bfloat16
MESH = pl.DeviceIdType.MESH
THIRD = D // 3
HALF = D // 2
NEAR = 96
REST = TILE - NEAR


def mm(a, b, ca, cb):
    return lax.dot_general(a, b, (((ca,), (cb,)), ((), ())), preferred_element_type=F32)


def delta_of(scores, labels, positives):
    hit = labels == positives[0:1]
    for p in range(1, 4):
        hit = hit | (labels == positives[p : p + 1])
    return (0.125 * jnp.tanh(0.5 * scores) + jnp.where(hit, -0.125, 0.125)).astype(BF16)


class Place:
    def __init__(self):
        grp, mid = lax.axis_index("grp"), lax.axis_index("mid")
        self.y, self.c = grp // 2, lax.rem(grp, 2)
        self.x, self.z = mid // NZ, lax.rem(mid, NZ)
        self.mid = mid
        self.ahead = 1 + 2 * self.c
        self.behind = 3 - 2 * self.c

    def at(self, dy=0, dx=0, dz=0, other=False):
        y, x, z = lax.rem(self.y + dy, NY), lax.rem(self.x + dx, NX), lax.rem(self.z + dz, NZ)
        return (2 * y + (1 - self.c if other else self.c), NZ * x + z)

    def sibling(self):
        return (2 * self.y + 1 - self.c, self.mid)

    def tile(self, dx, dz):
        return NZ * lax.rem(self.x + dx, NX) + lax.rem(self.z + dz, NZ)

    def greet(self):
        near = [self.sibling(), self.at(dy=2)]
        for step in (self.ahead, self.behind):
            near += [self.at(dy=step), self.at(dy=step, other=True)]
            near += [self.at(dx=step), self.at(dz=step)]
        barrier = pltpu.get_barrier_semaphore()
        for device in near:
            pl.semaphore_signal(barrier, inc=1, device_id=device, device_id_type=MESH)
        pl.semaphore_wait(barrier, len(near))


class Net:
    def __init__(self, send_sem, recv_sem):
        self.send_sem, self.recv_sem, self.made, self.drained = send_sem, recv_sem, [], 0

    def send(self, src, dst, device):
        i = len(self.made)
        copy = pltpu.make_async_remote_copy(
            src_ref=src,
            dst_ref=dst,
            send_sem=self.send_sem.at[i],
            recv_sem=self.recv_sem.at[i],
            device_id=device,
            device_id_type=MESH,
        )
        copy.start()
        self.made.append(copy)
        return copy

    def drain(self, count):
        for copy in self.made[self.drained : count]:
            copy.wait_send()
        self.drained = count


COPIES = 200
OWN, BACK, FRONT, ACROSS = range(4)
SLOTS = 32
LIST = 16


def role_step(color, role):
    return (0, 3 - 2 * color, 1 + 2 * color, 2)[role]


def main_kernel(
    q, mp, lp, mc, lc, cp, owner, cv, midv, leafv,
    gq, gco, plan, sel, deltas,
    q_own, q_b, q_a, q_2, p_own, cvv, cvm, cpall,
    in00, in01, in02, in03, in10, in11, in12, in13,
    no00, no01, no02, no03, no10, no11, no12, no13,
    sm00, sm01, sm02, sm03, sm10, sm11, sm12, sm13,
    no_a, no_b, no_x, planv, smo, pk_as, pk_ao, pk_bs, pk_bo, pk_own, pk_x, pk_b, pk_f,
    out_own, out_x, out0b, out0f, out1o, out1b, out1f, out1x,
    ret_own, x_0, x_1, a0_0, a0_1, a1_0, a1_1, b0_0, b0_1, b1_0, b1_1,
    vectors, held_delta, gc, qc, gsib, gbuf,
    s2, sb, r2, rb, ra, u2, ub, ua, far, local_sem, send_sem, recv_sem,
):
    me = Place()
    c, a, b = me.c, me.ahead, me.behind
    net = Net(send_sem, recv_sem)
    local, done = [], []

    def start_local(src, dst):
        copy = pltpu.make_async_copy(src, dst, local_sem.at[len(local)])
        copy.start()
        local.append(copy)
        return copy

    def wait_local(copy):
        copy.wait()
        done.append(copy)

    load_q = start_local(q, q_own)
    load_v = [start_local(midv, vectors.at[pl.ds(0, 4)]), start_local(leafv, vectors.at[pl.ds(4, 2)])]
    load_c = start_local(cv, cvv)
    for t in range(TILES):
        p_own[t, 0:4, :] = mp[:, t * TILE : (t + 1) * TILE]
        p_own[t, 4:8, :] = lp[:, t * TILE : (t + 1) * TILE]
    p_own[16:18] = jnp.full((2, 8, 128), -1, jnp.int32)
    p_own[16, :, 0:TILES] = mc[...]
    p_own[17, :, 0:TILES] = lc[...]
    cpall[me.x, me.z, 0:4, :] = cp[...]
    cpall[me.x, me.z, 4:8, :] = cp[...]
    me.greet()

    m = me.mid
    up, down, across = me.at(dy=a), me.at(dy=b), me.at(dy=2)
    up_other, down_other = me.at(dy=a, other=True), me.at(dy=b, other=True)
    xa, xb, za, zb = me.at(dx=a), me.at(dx=b), me.at(dz=a), me.at(dz=b)
    sib = me.sibling()
    planes = {BACK: q_b, FRONT: q_a, ACROSS: q_2}
    slots = ((in00, in01, in02, in03), (in10, in11, in12, in13))
    notes = ((no00, no01, no02, no03), (no10, no11, no12, no13))
    facts = ((sm00, sm01, sm02, sm03), (sm10, sm11, sm12, sm13))
    outs = ((out_own, out0b, out0f, out_x), (out1o, out1b, out1f, out1x))

    rest, near = pl.ds(NEAR, REST), pl.ds(0, NEAR)
    y_in = {
        BACK: net.send(q.at[m, rest], q_b.at[m], up),
        FRONT: net.send(q.at[m, rest], q_a.at[m], down),
        ACROSS: net.send(q.at[m], q_2.at[m], across),
    }
    pos_own = cpall.at[me.x, me.z]
    cz_a = net.send(pos_own, pos_own, za)
    cz_b = net.send(pos_own, pos_own, zb)

    index = lax.broadcasted_iota(jnp.int32, (2, 128), 0) * 128 + lax.broadcasted_iota(
        jnp.int32, (2, 128), 1
    )
    code = 4 * (
        TILES * lax.broadcasted_iota(jnp.int32, (8, 128), 0)
        + lax.broadcasted_iota(jnp.int32, (8, 128), 1)
    )
    lane = lax.broadcasted_iota(jnp.int32, (1, 128), 1)
    mids, leaves = p_own[16], p_own[17]

    def whole(value):
        return jnp.broadcast_to(value, (1, 128))

    def plan_slots(label):
        step = (0, a, b, 2)[label]
        for which, core in enumerate((c, 1 - c)):
            device = (2 * lax.rem(me.y + step, NY) + core) * TILES + m
            held = [
                whole(
                    jnp.sum(
                        jnp.where(owner[...] == 2 * device + i, index, 0), axis=(0, 1), keepdims=True
                    )
                )
                for i in range(2)
            ]
            entries = []
            for live, block in (
                ((mids >> 2) == device, mids & 3),
                ((leaves == held[0]) | (leaves == held[1]), (leaves == held[1]).astype(jnp.int32)),
            ):
                found = code + block
                first = whole(jnp.min(jnp.where(live, found, BIG), axis=(0, 1), keepdims=True))
                final = whole(jnp.max(jnp.where(live, found, -1), axis=(0, 1), keepdims=True))
                some = first < BIG
                entries.append((some, jnp.where(some, first, 0)))
                two = some & (final != first)
                entries.append((two, jnp.where(two, final, 0)))
            tiles = [(value >> 2) & 15 for _, value in entries]
            spots = jnp.full((1, 128), 4, jnp.int32)
            for e in (3, 2, 1, 0):
                spots = jnp.where(entries[e][0] & (tiles[e] == lane), e, spots)
            at = 32 + 2 * label + which
            planv[at : at + 1, :] = spots
            for e, (valid, value) in enumerate(entries):
                follow = jnp.full((1, 128), 4, jnp.int32)
                for f in range(3, e, -1):
                    follow = jnp.where(valid & entries[f][0] & (tiles[f] == tiles[e]), f, follow)
                row = jnp.where(lane == 0, jnp.where(valid, value & 3, -1), follow)
                row = jnp.where(lane == 2, tiles[e], row)
                row = jnp.where(lane == 3, value >> 6, row)
                row = jnp.where(lane == 4, (value & 3) + 4 * (e // 2), row)
                at = 8 * label + 4 * which + e
                planv[at : at + 1, :] = row
    planv[...] = jnp.zeros((40, 128), jnp.int32)
    plan_slots(BACK)
    plan_slots(FRONT)
    to_smem = start_local(planv, smo)
    wait_local(load_q)
    wait_local(to_smem)
    notes_out = (no00, no_a, no_b, no_x)

    def fill_notes(label):
        out = notes_out[label]
        for e in range(8):
            at = 8 * label + e
            level = 4 * (e % 4 // 2)
            positives = p_own[smo[at, 2]][level : level + 4] - BLOCK * smo[at, 3]
            out[e, 0:4, :] = positives
            out[e, 4:5, :] = planv[at : at + 1, :]
            out[e, 5:8, :] = jnp.zeros((3, 128), jnp.int32)
        out[8, 0:2, :] = planv[32 + 2 * label : 34 + 2 * label, :]
        out[8, 2:8, :] = jnp.zeros((6, 128), jnp.int32)

    direct, note_in = {}, {}
    for label, targets in ((BACK, ((pk_as, up), (pk_ao, up_other))), (FRONT, ((pk_bs, down), (pk_bo, down_other)))):
        fill_notes(label)
        for which, (buffer, device) in enumerate(targets):
            for e in range(4):
                buffer[e] = q_own[smo[8 * label + 4 * which + e, 2], 0:NEAR]
            note_in[which, label] = net.send(notes_out[label], notes[which][label], device)
            direct[which, label] = net.send(buffer, slots[which][label].at[:, near], device)
    plan_slots(ACROSS)
    plan_slots(OWN)
    to_smem = start_local(planv, smo)
    wait_local(to_smem)
    fill_notes(ACROSS)
    note_in[0, ACROSS] = net.send(no_x, no03, across)
    fill_notes(OWN)
    for e in range(4):
        pk_own[e] = q_own[smo[4 + e, 2]]
    note_in[1, OWN] = net.send(no00, no10, sib)
    beside = {OWN: net.send(pk_own, in10, sib)}
    for e in range(4):
        in00[e] = q_own[smo[e, 2]]

    axes = ((za, zb, xa, xb), (xa, xb, za, zb))
    walk = (0, b, a, 2)

    def rows_of(role, h):
        size = (TILE if role == ACROSS else REST) // 2
        return pl.ds(h * size, size)

    def tile_of(h, first, last):
        return me.tile(last, first) if h == 0 else me.tile(first, last)

    second, second_f, last, last_f = {}, {}, {}, {}

    def send_second(role):
        y_in[role].wait_recv()
        for h, (to_a, to_b, _, _) in enumerate(axes):
            piece = planes[role].at[m, rows_of(role, h)]
            second[role, h] = (net.send(piece, piece, to_a), net.send(piece, piece, to_b))

    def send_last(role, key):
        for h, (_, _, to_a, to_b) in enumerate(axes):
            piece = planes[role].at[tile_of(h, walk[key], 0), rows_of(role, h)]
            last[role, h, key] = (net.send(piece, piece, to_a), net.send(piece, piece, to_b))

    def second_stage(role):
        for h, (to_a, _, _, _) in enumerate(axes):
            second[role, h][0].wait_recv()
            piece = planes[role].at[tile_of(h, b, 0), rows_of(role, h)]
            second_f[role, h] = net.send(piece, piece, to_a)
        send_last(role, BACK)
        for h in range(2):
            second[role, h][1].wait_recv()
        send_last(role, FRONT)

    def across_stage(role):
        for h in range(2):
            second_f[role, h].wait_recv()
        send_last(role, ACROSS)

    def forward_last(role):
        for key, step in enumerate(walk):
            for h, (_, _, to_a, _) in enumerate(axes):
                last[role, h, key][0].wait_recv()
                piece = planes[role].at[tile_of(h, step, b), rows_of(role, h)]
                last_f[role, h, key] = net.send(piece, piece, to_a)

    def complete(role):
        for key in range(4):
            for h in range(2):
                last[role, h, key][1].wait_recv()
                last_f[role, h, key].wait_recv()

    fetches = {}

    def fetch(which, role):
        if (which, role) in note_in:
            note_in[which, role].wait_recv()
        fetches[which, role] = start_local(notes[which][role], facts[which][role])

    def know(which, role):
        wait_local(fetches[which, role])

    def pack(role):
        know(0, role)
        rows = planes[role]
        buffer = {BACK: pk_b, FRONT: pk_f, ACROSS: pk_x}[role]
        for e in range(4):
            buffer[e] = rows[facts[0][role][4 + e, 4, 2]]
            if role == ACROSS and e % 2:
                duo = pl.ds(e - 1, 2)
                beside[role, e // 2] = net.send(buffer.at[duo], in13.at[duo], sib)
        if role != ACROSS:
            beside[role] = net.send(buffer, slots[1][role].at[:, rest], sib)
        for e in range(4):
            value = rows[facts[0][role][e, 4, 2]]
            if role == ACROSS:
                in03[e] = value
            else:
                slots[0][role][e, NEAR:TILE] = value

    labels = lax.broadcasted_iota(jnp.int32, (BLOCK, TILE), 0)
    returns = {}

    def pairs(which, role, half):
        block_of, rows, info, out = (
            facts[which][role], slots[which][role], notes[which][role], outs[which][role]
        )
        group = pl.ds(4 * role, 4)
        if half == 0:
            if which == 1 or role == OWN:
                know(which, role)
            if (which, role) in direct:
                direct[which, role].wait_recv()
            if which == 1 and role != ACROSS:
                beside[role].wait_recv()
        if which == 1 and role == ACROSS:
            beside[role, half].wait_recv()
        both = (2 * half, 2 * half + 1)
        blocks = [vectors[block_of[4 * which + e, 4, 4]] for e in both]
        scores = [mm(block, rows[e], 1, 1) for e, block in zip(both, blocks)]
        for e, block, score in zip(both, blocks, scores):
            delta = delta_of(score, labels, info[4 * which + e])
            held_delta[which, 4 * role + e] = delta
            out[e] = mm(delta, block, 0, 0).astype(BF16)
            at = 16 * which + 4 * role + e
            plan[at : at + 1, :] = info[4 * which + e, 4:5, :]
        if half == 1:
            start_local(rows, sel.at[which, group])
            start_local(held_delta.at[which, group], deltas.at[which, group])
            for e in (2, 1, 0):
                out[e] = out[e] + out[block_of[4 * which + e, 4, 1]]

    row_halves = (pl.ds(0, TILE // 2), pl.ds(TILE // 2, TILE // 2))
    ret_a0, ret_a1, ret_b0, ret_b1 = (a0_0, a0_1), (a1_0, a1_1), (b0_0, b0_1), (b1_0, b1_1)
    ret_x = (x_0, x_1)
    four = pl.ds(0, 4)

    def give_back(which, role, r):
        out = outs[which][role]
        back = {
            (0, BACK): (ret_a0, down),
            (0, FRONT): (ret_b0, up),
            (1, BACK): (ret_a1, up_other),
            (1, FRONT): (ret_b1, down_other),
        }[which, role]
        returns[which, role, r] = net.send(
            out.at[four, row_halves[r]], back[0][r].at[four], back[1]
        )

    for ref in outs[0] + outs[1] + (ret_own,):
        ref[4] = jnp.zeros((TILE, D), BF16)
    for ref in ret_x + ret_a0 + ret_a1 + ret_b0 + ret_b1:
        ref[4] = jnp.zeros((TILE // 2, D), BF16)
    steps = (0, b, a, 2)
    first_axis = ((xa, xb), (za, zb))
    first2, firsta, firstb = {}, {}, {}
    second2, seconda, secondb = {}, {}, {}
    term_in = {}

    def part(h, stream, unit, j):
        tile = me.tile(steps[unit], steps[j]) if h == 0 else me.tile(steps[j], steps[unit])
        cols = slice(h * HALF, (h + 1) * HALF)
        r = stream % 2
        rows = slice(r * TILE // 2, (r + 1) * TILE // 2)
        if stream < 2:
            return out_x[sm03[8, 0, tile], rows, cols] + ret_x[r][sm03[8, 1, tile], :, cols]
        value = out_own[smo[32 + 2 * OWN, tile], rows, cols]
        value += ret_own[smo[33 + 2 * OWN, tile], rows, cols]
        value += ret_a0[r][smo[32 + 2 * BACK, tile], :, cols]
        value += ret_a1[r][smo[33 + 2 * BACK, tile], :, cols]
        value += ret_b0[r][smo[32 + 2 * FRONT, tile], :, cols]
        return value + ret_b1[r][smo[33 + 2 * FRONT, tile], :, cols]

    def begin_sum(stream):
        if stream < 2:
            term_in[ACROSS, stream].wait_recv()
        if stream >= 2:
            if stream == 2:
                term_in[OWN].wait_recv()
            for which in range(2):
                for role in (BACK, FRONT):
                    returns[which, role, stream - 2].wait_recv()
        for h in range(2):
            for j in range(4):
                s2[h, stream, j] = part(h, stream, ACROSS, j)
            first2[h, stream] = net.send(s2.at[h, stream], r2.at[h, stream], first_axis[h][0])
            for j in range(4):
                sb[h, stream, j] = part(h, stream, BACK, j)
            firstb[h, stream] = net.send(sb.at[h, stream], rb.at[h, stream], first_axis[h][1])

    def pass_sum(stream):
        for h in range(2):
            first2[h, stream].wait_recv()
            for j in range(4):
                r2[h, stream, j] = r2[h, stream, j] + part(h, stream, FRONT, j)
            firsta[h, stream] = net.send(r2.at[h, stream], ra.at[h, stream], first_axis[h][0])

    def begin_second(stream):
        for h in range(2):
            firstb[h, stream].wait_recv()
            firsta[h, stream].wait_recv()
            to_a, to_b = first_axis[1 - h]
            for j in (ACROSS, BACK, FRONT, OWN):
                rb[h, stream, j] = part(h, stream, OWN, j) + rb[h, stream, j] + ra[h, stream, j]
                if j == ACROSS:
                    second2[h, stream] = net.send(rb.at[h, stream, j], u2.at[h, stream], to_a)
                if j == BACK:
                    secondb[h, stream] = net.send(rb.at[h, stream, j], ub.at[h, stream], to_b)

    def pass_second(stream):
        for h in range(2):
            second2[h, stream].wait_recv()
            u2[h, stream] = u2[h, stream] + rb[h, stream, FRONT]
            seconda[h, stream] = net.send(u2.at[h, stream], ua.at[h, stream], first_axis[1 - h][0])

    def end_second(stream):
        for h in range(2):
            secondb[h, stream].wait_recv()
            seconda[h, stream].wait_recv()
            ub[h, stream] = rb[h, stream, OWN] + ub[h, stream] + ua[h, stream]

    fetch(0, OWN)
    send_second(BACK)
    send_second(FRONT)
    send_last(BACK, OWN)
    send_second(ACROSS)
    for load in load_v:
        wait_local(load)
    pairs(0, OWN, 0)
    second_stage(BACK)
    cz_a.wait_recv()
    pos_b = cpall.at[me.x, lax.rem(me.z + b, NZ)]
    cz_f = net.send(pos_b, pos_b, za)
    send_last(FRONT, OWN)
    pairs(0, OWN, 1)
    second_stage(FRONT)
    across_stage(BACK)
    fetch(1, OWN)
    fetch(0, BACK)
    fetch(0, FRONT)
    cz_b.wait_recv()
    cz_f.wait_recv()
    pos_row = cpall.at[me.x]
    cx_a = net.send(pos_row, pos_row, xa)
    cx_b = net.send(pos_row, pos_row, xb)
    forward_last(BACK)
    pairs(1, OWN, 0)
    across_stage(FRONT)
    send_last(ACROSS, OWN)
    second_stage(ACROSS)
    pairs(1, OWN, 1)
    term_in[OWN] = net.send(out1o.at[four], ret_own.at[four], sib)
    complete(BACK)
    pack(BACK)
    across_stage(ACROSS)
    forward_last(FRONT)
    cx_a.wait_recv()
    pos_row_b = cpall.at[lax.rem(me.x + b, NX)]
    cx_f = net.send(pos_row_b, pos_row_b, xa)
    pairs(0, BACK, 0)
    pairs(0, BACK, 1)
    give_back(0, BACK, 0)
    fetch(1, BACK)
    fetch(1, FRONT)
    fetch(0, ACROSS)
    note_in[1, ACROSS] = net.send(no03, no13, sib)
    complete(FRONT)
    pack(FRONT)
    pairs(0, FRONT, 0)
    forward_last(ACROSS)
    pairs(0, FRONT, 1)
    give_back(0, FRONT, 0)
    complete(ACROSS)
    pack(ACROSS)
    pairs(1, BACK, 0)
    pairs(1, BACK, 1)
    give_back(1, BACK, 0)
    fetch(1, ACROSS)
    pairs(1, FRONT, 0)
    pairs(1, FRONT, 1)
    give_back(1, FRONT, 0)
    for role in (BACK, FRONT):
        for which in range(2):
            give_back(which, role, 1)
    pairs(1, ACROSS, 0)
    pairs(1, ACROSS, 1)
    for r in range(2):
        term_in[ACROSS, r] = net.send(out1x.at[four, row_halves[r]], ret_x[r].at[four], sib)
    pairs(0, ACROSS, 0)
    pairs(0, ACROSS, 1)
    begin_sum(2)
    early = len(net.made)
    wait_local(load_c)
    for j in range(8):
        color, role = j // 4, j % 4
        row = (2 * lax.rem(me.y + role_step(color, role), NY) + color) * TILES + m
        start = pl.multiple_of(row * 16, 16)
        cvm[pl.ds(16 * j, 16), :] = cvv[pl.ds(start, 16), :]
    place = lax.broadcasted_iota(jnp.int32, (128, 128), 0)
    chunk = place // 16
    color, role = chunk // 4, lax.rem(chunk, 4)
    step = jnp.where(role == ACROSS, 2, jnp.where(role == FRONT, 1 + 2 * color, 3 - 2 * color))
    step = jnp.where(role == OWN, 0, step)
    owner_grp = 2 * lax.rem(me.y + step, NY) + color
    coarse_ids = (owner_grp * TILES + m) * 16 + lax.rem(place, 16)

    def own_coarse():
        qm = q_own[m]
        total = jnp.zeros((TILE, D), F32)
        for i in range(COARSE // BLOCK):
            vectors = cvv[i * BLOCK : (i + 1) * BLOCK, :]
            labels = lax.broadcasted_iota(jnp.int32, (BLOCK, TILE), 0) + i * BLOCK
            delta = delta_of(mm(vectors, qm, 1, 1), labels, cpall[me.x, me.z])
            total += mm(delta, vectors, 0, 0)
        qc[...] = total

    def rows_coarse(lo, hi):
        def body(t, carry):
            qt = q_own[pl.ds(2 * t, 2)].reshape(2 * TILE, D)
            scores = mm(cvm[...], qt, 1, 1)
            delta = jnp.concatenate(
                [
                    delta_of(
                        scores[:, h * TILE : (h + 1) * TILE],
                        coarse_ids,
                        cpall[t // 2, 2 * lax.rem(t, 2) + h],
                    )
                    for h in range(2)
                ],
                axis=1,
            )
            gc[...] += mm(delta, qt, 1, 0)
            return carry

        lax.fori_loop(lo, hi, body, 0)


    gc[...] = jnp.zeros_like(gc)
    cx_b.wait_recv()
    cx_f.wait_recv()
    rows_coarse(0, 4)
    begin_sum(0)
    begin_sum(1)
    pass_sum(2)
    rows_coarse(4, 8)
    coarse = net.send(gc.at[pl.ds(64 * (1 - c), 64)], gsib, sib)
    pass_sum(0)
    pass_sum(1)
    begin_sum(3)
    begin_second(2)
    own_coarse()
    begin_second(0)
    begin_second(1)
    pass_sum(3)
    net.drain(early)
    for copy in local:
        if not any(copy is other for other in done):
            wait_local(copy)
    pass_second(2)
    pass_second(0)
    pass_second(1)
    coarse.wait_recv()
    for role in range(4):
        gbuf[role] = gc[pl.ds(64 * c + 16 * role, 16)] + gsib[16 * role : 16 * role + 16]
    coarse2 = net.send(gbuf.at[ACROSS], gbuf.at[5], up)
    coarseb = net.send(gbuf.at[BACK], gbuf.at[6], down)
    end_second(0)
    end_second(1)
    home = net.send(ub.at[:, pl.ds(0, 2)], far, across)
    begin_second(3)
    end_second(2)
    coarse2.wait_recv()
    gbuf[4] = gbuf[FRONT] + gbuf[5]
    coarsea = net.send(gbuf.at[4], gbuf.at[7], up)
    pass_second(3)
    coarsea.wait_recv()
    coarseb.wait_recv()
    gco[...] = gbuf[OWN] + gbuf[6] + gbuf[7]
    home.wait_recv()
    end_second(3)
    for h in range(2):
        cols = slice(h * HALF, (h + 1) * HALF)
        for r in range(2):
            rows = slice(r * TILE // 2, (r + 1) * TILE // 2)
            gq[rows, cols] = (
                qc[rows, cols] + ub[h, 2 + r].astype(F32) + far[h, r].astype(F32)
            )
    for copy in local:
        if not any(copy is other for other in done):
            copy.wait()
    net.drain(len(net.made))


def grads_kernel(
    plan, sel, deltas, gq_in, gco_in,
    gm, gl, gq, gco,
    counts, entries, rows, held, acc, row_sem, delta_sem, grad_sem, out_sem,
):
    results = [
        pltpu.make_async_copy(gq_in, gq, out_sem.at[0]),
        pltpu.make_async_copy(gco_in, gco, out_sem.at[1]),
    ]
    for copy in results:
        copy.start()
    stores = [(gm, 0), (gm, 1), (gm, 2), (gm, 3), (gl, 0), (gl, 1)]

    def row_copy(e):
        return pltpu.make_async_copy(sel.at[e], rows.at[e], row_sem.at[e])

    def delta_copy(e):
        return pltpu.make_async_copy(deltas.at[e], held.at[e], delta_sem.at[e])

    for key in range(6):
        counts[key] = 0
    for e in range(SLOTS):
        block = plan[e, 0]

        @pl.when(block >= 0)
        def _():
            row_copy(e).start()
            delta_copy(e).start()
            key = block + 4 * (e // 2 % 2)
            n = counts[key]
            entries[LIST * key + n] = e
            counts[key] = n + 1

    rows[SLOTS] = jnp.zeros((TILE, D), BF16)
    held[SLOTS] = jnp.zeros((BLOCK, TILE), BF16)

    def per_key(key, carry):
        n = counts[key]
        start = LIST * key

        @pl.when(n == 0)
        def _():
            acc[key] = jnp.zeros((BLOCK, D), F32)

        def batch(i, inner):
            at = start + 2 * i
            full = 2 * i + 1 < n
            e0 = entries[at]
            e1 = jnp.where(full, entries[at + 1], SLOTS)
            row_copy(e0).wait()
            delta_copy(e0).wait()

            @pl.when(full)
            def _():
                row_copy(e1).wait()
                delta_copy(e1).wait()

            both = jnp.concatenate([rows[e0], rows[e1]], axis=0)
            delta = jnp.concatenate([held[e0], held[e1]], axis=1)

            @pl.when(i == 0)
            def _():
                for n_col in range(3):
                    cols = slice(n_col * THIRD, (n_col + 1) * THIRD)
                    acc[key, :, cols] = mm(delta, both[:, cols], 1, 0)

            @pl.when(i != 0)
            def _():
                for n_col in range(3):
                    cols = slice(n_col * THIRD, (n_col + 1) * THIRD)
                    acc[key, :, cols] += mm(delta, both[:, cols], 1, 0)

            return inner

        lax.fori_loop(0, (n + 1) // 2, batch, 0)
        for i, (out, j) in enumerate(stores):

            @pl.when(key == i)
            def _():
                pltpu.make_async_copy(acc.at[i], out.at[j], grad_sem.at[i]).start()

        return carry

    lax.fori_loop(0, 6, per_key, 0)
    for i, (out, j) in enumerate(stores):
        pltpu.make_async_copy(acc.at[i], out.at[j], grad_sem.at[i]).wait()
    for copy in results:
        copy.wait()


def vmem():
    return pl.BlockSpec(memory_space=pltpu.VMEM)


def smem():
    return pl.BlockSpec(memory_space=pltpu.SMEM)


def hbm():
    return pl.BlockSpec(memory_space=pl.ANY)


def shape(dims, dtype):
    return jax.ShapeDtypeStruct(dims, dtype)


def shards(
    queries,
    coarse_vectors,
    mid_vectors,
    leaf_vectors,
    coarse_pos,
    mid_pos,
    leaf_pos,
    mid_cand,
    leaf_cand,
    leaf_owner,
):
    dma = pltpu.SemaphoreType.DMA
    mib = 1024 * 1024
    group = pltpu.VMEM((TILES, TILE, D), BF16)
    part = pltpu.VMEM((TILES, REST, D), BF16)
    four = pltpu.VMEM((4, TILE, D), BF16)
    five = pltpu.VMEM((5, TILE, D), BF16)
    half = pltpu.VMEM((5, TILE // 2, D), BF16)
    near = pltpu.VMEM((4, NEAR, D), BF16)
    rest = pltpu.VMEM((4, REST, D), BF16)
    notes = pltpu.VMEM((9, 8, 128), jnp.int32)
    facts = pltpu.SMEM((9, 8, 128), jnp.int32)
    first = pltpu.VMEM((2, 4, 4, TILE // 2, HALF), BF16)
    second = pltpu.VMEM((2, 4, TILE // 2, HALF), BF16)
    gq, gco, plan, sel, deltas = pl.pallas_call(
        main_kernel,
        out_shape=(
            shape((TILE, D), F32),
            shape((16, D), F32),
            shape((SLOTS, 128), jnp.int32),
            shape((2, 16, TILE, D), BF16),
            shape((2, 16, BLOCK, TILE), BF16),
        ),
        in_specs=[hbm(), vmem(), vmem(), vmem(), vmem(), vmem(), vmem(), hbm(), hbm(), hbm()],
        out_specs=(vmem(), vmem(), vmem(), hbm(), hbm()),
        scratch_shapes=[
            group, part, part, group,
            pltpu.VMEM((18, 8, 128), jnp.int32),
            pltpu.VMEM((COARSE, D), BF16),
            pltpu.VMEM((128, D), BF16),
            pltpu.VMEM((NX, NZ, 8, TILE), jnp.int32),
            four, four, four, four, four, four, four, four,
            notes, notes, notes, notes, notes, notes, notes, notes,
            facts, facts, facts, facts, facts, facts, facts, facts,
            notes, notes, notes,
            pltpu.VMEM((40, 128), jnp.int32),
            pltpu.SMEM((40, 128), jnp.int32),
            near, near, near, near, four, four, rest, rest,
            five, five, five, five, five, five, five, five,
            five,
            half, half, half, half, half, half, half, half, half, half,
            pltpu.VMEM((6, BLOCK, D), BF16),
            pltpu.VMEM((2, 16, BLOCK, TILE), BF16),
            pltpu.VMEM((128, D), F32),
            pltpu.VMEM((TILE, D), F32),
            pltpu.VMEM((64, D), F32),
            pltpu.VMEM((8, 16, D), F32),
            first, first, first, first, first,
            second, second, second,
            pltpu.VMEM((2, 2, TILE // 2, HALF), BF16),
            dma((40,)),
            dma((COPIES,)),
            dma((COPIES,)),
        ],
        compiler_params=pltpu.CompilerParams(
            collective_id=0, has_side_effects=True, vmem_limit_bytes=62 * mib
        ),
        name="main",
    )(
        queries.reshape(TILES, TILE, D),
        mid_pos.T,
        leaf_pos.T,
        mid_cand.T,
        leaf_cand.T,
        coarse_pos.T,
        leaf_owner.reshape(2, 128),
        coarse_vectors,
        mid_vectors.reshape(4, BLOCK, D),
        leaf_vectors.reshape(2, BLOCK, D),
    )
    gm, gl, gq, gco = pl.pallas_call(
        grads_kernel,
        out_shape=(
            shape((4, BLOCK, D), F32),
            shape((2, BLOCK, D), F32),
            shape((TILE, D), F32),
            shape((16, D), F32),
        ),
        in_specs=[smem(), hbm(), hbm(), vmem(), vmem()],
        out_specs=(hbm(), hbm(), hbm(), hbm()),
        scratch_shapes=[
            pltpu.SMEM((6,), jnp.int32),
            pltpu.SMEM((6 * LIST + 1,), jnp.int32),
            pltpu.VMEM((SLOTS + 1, TILE, D), BF16),
            pltpu.VMEM((SLOTS + 1, BLOCK, TILE), BF16),
            pltpu.VMEM((6, BLOCK, D), F32),
            dma((SLOTS,)),
            dma((SLOTS,)),
            dma((6,)),
            dma((2,)),
        ],
        compiler_params=pltpu.CompilerParams(vmem_limit_bytes=60 * mib),
        name="grads",
    )(plan, sel.reshape(SLOTS, TILE, D), deltas.reshape(SLOTS, BLOCK, TILE), gq, gco)
    return gq, gco, gm.reshape(4 * BLOCK, D), gl.reshape(2 * BLOCK, D)


def solution(mesh):
    placed = (
        P("grp", None),
        P(),
        P(("grp", "mid"), None),
        P(("grp", "mid"), None),
        P(("grp", "mid"), None),
        P("grp", None),
        P("grp", None),
        P("grp", None),
        P("grp", None),
        P(),
    )
    return jax.shard_map(
        shards,
        mesh=mesh,
        in_specs=placed,
        out_specs=(
            P(("grp", "mid"), None),
            P(("grp", "mid"), None),
            P(("grp", "mid"), None),
            P(("grp", "mid"), None),
        ),
        check_vma=False,
    )
```

```python
import jax
import jax.numpy as jnp
from jax import lax
from jax.experimental import pallas as pl
from jax.experimental.pallas import tpu as pltpu
from jax.sharding import PartitionSpec as P

TILE = 128
BLOCK = 512
COARSE = 2048
K_CAND = 8
D = 768
NY, NX, NZ = 4, 4, 4
TILES = NX * NZ
BIG = 1 << 20
F32 = jnp.float32
BF16 = jnp.bfloat16
MESH = pl.DeviceIdType.MESH
THIRD = D // 3
HALF = D // 2
NEAR = 96
REST = TILE - NEAR


def mm(a, b, ca, cb):
    return lax.dot_general(a, b, (((ca,), (cb,)), ((), ())), preferred_element_type=F32)


def delta_of(scores, labels, positives):
    hit = labels == positives[0:1]
    for p in range(1, 4):
        hit = hit | (labels == positives[p : p + 1])
    return (0.125 * jnp.tanh(0.5 * scores) + jnp.where(hit, -0.125, 0.125)).astype(BF16)


class Place:
    def __init__(self):
        grp, mid = lax.axis_index("grp"), lax.axis_index("mid")
        self.y, self.c = grp // 2, lax.rem(grp, 2)
        self.x, self.z = mid // NZ, lax.rem(mid, NZ)
        self.mid = mid
        self.ahead = 1 + 2 * self.c
        self.behind = 3 - 2 * self.c

    def at(self, dy=0, dx=0, dz=0, other=False):
        y, x, z = lax.rem(self.y + dy, NY), lax.rem(self.x + dx, NX), lax.rem(self.z + dz, NZ)
        return (2 * y + (1 - self.c if other else self.c), NZ * x + z)

    def sibling(self):
        return (2 * self.y + 1 - self.c, self.mid)

    def tile(self, dx, dz):
        return NZ * lax.rem(self.x + dx, NX) + lax.rem(self.z + dz, NZ)

    def greet(self):
        near = [self.sibling(), self.at(dy=2)]
        for step in (self.ahead, self.behind):
            near += [self.at(dy=step), self.at(dy=step, other=True)]
            near += [self.at(dx=step), self.at(dz=step)]
        barrier = pltpu.get_barrier_semaphore()
        for device in near:
            pl.semaphore_signal(barrier, inc=1, device_id=device, device_id_type=MESH)
        pl.semaphore_wait(barrier, len(near))


class Net:
    def __init__(self, send_sem, recv_sem):
        self.send_sem, self.recv_sem, self.made, self.drained = send_sem, recv_sem, [], 0

    def send(self, src, dst, device):
        i = len(self.made)
        copy = pltpu.make_async_remote_copy(
            src_ref=src,
            dst_ref=dst,
            send_sem=self.send_sem.at[i],
            recv_sem=self.recv_sem.at[i],
            device_id=device,
            device_id_type=MESH,
        )
        copy.start()
        self.made.append(copy)
        return copy

    def drain(self, count):
        for copy in self.made[self.drained : count]:
            copy.wait_send()
        self.drained = count


COPIES = 200
OWN, BACK, FRONT, ACROSS = range(4)
SLOTS = 32
LIST = 16


def role_step(color, role):
    return (0, 3 - 2 * color, 1 + 2 * color, 2)[role]


def main_kernel(
    q, mp, lp, mc, lc, cp, owner, cv, midv, leafv,
    gq, gco, plan, sel, deltas,
    q_own, q_b, q_a, q_2, p_own, cvv, cvm, cpall,
    in00, in01, in02, in03, in10, in11, in12, in13,
    no00, no01, no02, no03, no10, no11, no12, no13,
    sm00, sm01, sm02, sm03, sm10, sm11, sm12, sm13,
    no_a, no_b, no_x, planv, smo, pk_as, pk_ao, pk_bs, pk_bo, pk_own, pk_x, pk_b, pk_f,
    out_own, out_x, out0b, out0f, out1o, out1b, out1f, out1x,
    ret_own, x_0, x_1, a0_0, a0_1, a1_0, a1_1, b0_0, b0_1, b1_0, b1_1,
    vectors, held_delta, gc, qc, gsib, gbuf,
    s2, sb, r2, rb, ra, u2, ub, ua, far, local_sem, send_sem, recv_sem,
):
    me = Place()
    c, a, b = me.c, me.ahead, me.behind
    net = Net(send_sem, recv_sem)
    local, done = [], []

    def start_local(src, dst):
        copy = pltpu.make_async_copy(src, dst, local_sem.at[len(local)])
        copy.start()
        local.append(copy)
        return copy

    def wait_local(copy):
        copy.wait()
        done.append(copy)

    load_q = start_local(q, q_own)
    load_v = [start_local(midv, vectors.at[pl.ds(0, 4)]), start_local(leafv, vectors.at[pl.ds(4, 2)])]
    load_c = start_local(cv, cvv)
    for t in range(TILES):
        p_own[t, 0:4, :] = mp[:, t * TILE : (t + 1) * TILE]
        p_own[t, 4:8, :] = lp[:, t * TILE : (t + 1) * TILE]
    p_own[16:18] = jnp.full((2, 8, 128), -1, jnp.int32)
    p_own[16, :, 0:TILES] = mc[...]
    p_own[17, :, 0:TILES] = lc[...]
    cpall[me.x, me.z, 0:4, :] = cp[...]
    cpall[me.x, me.z, 4:8, :] = cp[...]
    me.greet()

    m = me.mid
    up, down, across = me.at(dy=a), me.at(dy=b), me.at(dy=2)
    up_other, down_other = me.at(dy=a, other=True), me.at(dy=b, other=True)
    xa, xb, za, zb = me.at(dx=a), me.at(dx=b), me.at(dz=a), me.at(dz=b)
    sib = me.sibling()
    planes = {BACK: q_b, FRONT: q_a, ACROSS: q_2}
    slots = ((in00, in01, in02, in03), (in10, in11, in12, in13))
    notes = ((no00, no01, no02, no03), (no10, no11, no12, no13))
    facts = ((sm00, sm01, sm02, sm03), (sm10, sm11, sm12, sm13))
    outs = ((out_own, out0b, out0f, out_x), (out1o, out1b, out1f, out1x))

    rest, near = pl.ds(NEAR, REST), pl.ds(0, NEAR)
    y_in = {
        BACK: net.send(q.at[m, rest], q_b.at[m], up),
        FRONT: net.send(q.at[m, rest], q_a.at[m], down),
        ACROSS: net.send(q.at[m], q_2.at[m], across),
    }
    pos_own = cpall.at[me.x, me.z]
    cz_a = net.send(pos_own, pos_own, za)
    cz_b = net.send(pos_own, pos_own, zb)

    index = lax.broadcasted_iota(jnp.int32, (2, 128), 0) * 128 + lax.broadcasted_iota(
        jnp.int32, (2, 128), 1
    )
    code = 4 * (
        TILES * lax.broadcasted_iota(jnp.int32, (8, 128), 0)
        + lax.broadcasted_iota(jnp.int32, (8, 128), 1)
    )
    lane = lax.broadcasted_iota(jnp.int32, (1, 128), 1)
    mids, leaves = p_own[16], p_own[17]

    def whole(value):
        return jnp.broadcast_to(value, (1, 128))

    def plan_slots(label):
        step = (0, a, b, 2)[label]
        for which, core in enumerate((c, 1 - c)):
            device = (2 * lax.rem(me.y + step, NY) + core) * TILES + m
            held = [
                whole(
                    jnp.sum(
                        jnp.where(owner[...] == 2 * device + i, index, 0), axis=(0, 1), keepdims=True
                    )
                )
                for i in range(2)
            ]
            entries = []
            for live, block in (
                ((mids >> 2) == device, mids & 3),
                ((leaves == held[0]) | (leaves == held[1]), (leaves == held[1]).astype(jnp.int32)),
            ):
                found = code + block
                first = whole(jnp.min(jnp.where(live, found, BIG), axis=(0, 1), keepdims=True))
                final = whole(jnp.max(jnp.where(live, found, -1), axis=(0, 1), keepdims=True))
                some = first < BIG
                entries.append((some, jnp.where(some, first, 0)))
                two = some & (final != first)
                entries.append((two, jnp.where(two, final, 0)))
            tiles = [(value >> 2) & 15 for _, value in entries]
            spots = jnp.full((1, 128), 4, jnp.int32)
            for e in (3, 2, 1, 0):
                spots = jnp.where(entries[e][0] & (tiles[e] == lane), e, spots)
            at = 32 + 2 * label + which
            planv[at : at + 1, :] = spots
            for e, (valid, value) in enumerate(entries):
                follow = jnp.full((1, 128), 4, jnp.int32)
                for f in range(3, e, -1):
                    follow = jnp.where(valid & entries[f][0] & (tiles[f] == tiles[e]), f, follow)
                row = jnp.where(lane == 0, jnp.where(valid, value & 3, -1), follow)
                row = jnp.where(lane == 2, tiles[e], row)
                row = jnp.where(lane == 3, value >> 6, row)
                row = jnp.where(lane == 4, (value & 3) + 4 * (e // 2), row)
                at = 8 * label + 4 * which + e
                planv[at : at + 1, :] = row
    planv[...] = jnp.zeros((40, 128), jnp.int32)
    plan_slots(BACK)
    plan_slots(FRONT)
    to_smem = start_local(planv, smo)
    wait_local(load_q)
    wait_local(to_smem)
    notes_out = (no00, no_a, no_b, no_x)

    def fill_notes(label):
        out = notes_out[label]
        for e in range(8):
            at = 8 * label + e
            level = 4 * (e % 4 // 2)
            positives = p_own[smo[at, 2]][level : level + 4] - BLOCK * smo[at, 3]
            out[e, 0:4, :] = positives
            out[e, 4:5, :] = planv[at : at + 1, :]
            out[e, 5:8, :] = jnp.zeros((3, 128), jnp.int32)
        out[8, 0:2, :] = planv[32 + 2 * label : 34 + 2 * label, :]
        out[8, 2:8, :] = jnp.zeros((6, 128), jnp.int32)

    direct, note_in = {}, {}
    for label, targets in ((BACK, ((pk_as, up), (pk_ao, up_other))), (FRONT, ((pk_bs, down), (pk_bo, down_other)))):
        fill_notes(label)
        for which, (buffer, device) in enumerate(targets):
            for e in range(4):
                buffer[e] = q_own[smo[8 * label + 4 * which + e, 2], 0:NEAR]
            note_in[which, label] = net.send(notes_out[label], notes[which][label], device)
            direct[which, label] = net.send(buffer, slots[which][label].at[:, near], device)
    plan_slots(ACROSS)
    plan_slots(OWN)
    to_smem = start_local(planv, smo)
    wait_local(to_smem)
    fill_notes(ACROSS)
    note_in[0, ACROSS] = net.send(no_x, no03, across)
    fill_notes(OWN)
    for e in range(4):
        pk_own[e] = q_own[smo[4 + e, 2]]
    note_in[1, OWN] = net.send(no00, no10, sib)
    beside = {OWN: net.send(pk_own, in10, sib)}
    for e in range(4):
        in00[e] = q_own[smo[e, 2]]

    axes = ((za, zb, xa, xb), (xa, xb, za, zb))
    walk = (0, b, a, 2)

    def rows_of(role, h):
        size = (TILE if role == ACROSS else REST) // 2
        return pl.ds(h * size, size)

    def tile_of(h, first, last):
        return me.tile(last, first) if h == 0 else me.tile(first, last)

    second, second_f, last, last_f = {}, {}, {}, {}

    def send_second(role):
        y_in[role].wait_recv()
        for h, (to_a, to_b, _, _) in enumerate(axes):
            piece = planes[role].at[m, rows_of(role, h)]
            second[role, h] = (net.send(piece, piece, to_a), net.send(piece, piece, to_b))

    def send_last(role, key):
        for h, (_, _, to_a, to_b) in enumerate(axes):
            piece = planes[role].at[tile_of(h, walk[key], 0), rows_of(role, h)]
            last[role, h, key] = (net.send(piece, piece, to_a), net.send(piece, piece, to_b))

    def second_stage(role):
        for h, (to_a, _, _, _) in enumerate(axes):
            second[role, h][0].wait_recv()
            piece = planes[role].at[tile_of(h, b, 0), rows_of(role, h)]
            second_f[role, h] = net.send(piece, piece, to_a)
        send_last(role, BACK)
        for h in range(2):
            second[role, h][1].wait_recv()
        send_last(role, FRONT)

    def across_stage(role):
        for h in range(2):
            second_f[role, h].wait_recv()
        send_last(role, ACROSS)

    def forward_last(role):
        for key, step in enumerate(walk):
            for h, (_, _, to_a, _) in enumerate(axes):
                last[role, h, key][0].wait_recv()
                piece = planes[role].at[tile_of(h, step, b), rows_of(role, h)]
                last_f[role, h, key] = net.send(piece, piece, to_a)

    def complete(role):
        for key in range(4):
            for h in range(2):
                last[role, h, key][1].wait_recv()
                last_f[role, h, key].wait_recv()

    fetches = {}

    def fetch(which, role):
        if (which, role) in note_in:
            note_in[which, role].wait_recv()
        fetches[which, role] = start_local(notes[which][role], facts[which][role])

    def know(which, role):
        wait_local(fetches[which, role])

    def pack(role):
        know(0, role)
        rows = planes[role]
        buffer = {BACK: pk_b, FRONT: pk_f, ACROSS: pk_x}[role]
        for e in range(4):
            buffer[e] = rows[facts[0][role][4 + e, 4, 2]]
            if role == ACROSS and e % 2:
                duo = pl.ds(e - 1, 2)
                beside[role, e // 2] = net.send(buffer.at[duo], in13.at[duo], sib)
        if role != ACROSS:
            beside[role] = net.send(buffer, slots[1][role].at[:, rest], sib)
        for e in range(4):
            value = rows[facts[0][role][e, 4, 2]]
            if role == ACROSS:
                in03[e] = value
            else:
                slots[0][role][e, NEAR:TILE] = value

    labels = lax.broadcasted_iota(jnp.int32, (BLOCK, TILE), 0)
    returns = {}

    def pairs(which, role, half):
        block_of, rows, info, out = (
            facts[which][role], slots[which][role], notes[which][role], outs[which][role]
        )
        group = pl.ds(4 * role, 4)
        if half == 0:
            if which == 1 or role == OWN:
                know(which, role)
            if (which, role) in direct:
                direct[which, role].wait_recv()
            if which == 1 and role != ACROSS:
                beside[role].wait_recv()
        if which == 1 and role == ACROSS:
            beside[role, half].wait_recv()
        both = (2 * half, 2 * half + 1)
        blocks = [vectors[block_of[4 * which + e, 4, 4]] for e in both]
        scores = [mm(block, rows[e], 1, 1) for e, block in zip(both, blocks)]
        for e, block, score in zip(both, blocks, scores):
            delta = delta_of(score, labels, info[4 * which + e])
            held_delta[which, 4 * role + e] = delta
            out[e] = mm(delta, block, 0, 0).astype(BF16)
            at = 16 * which + 4 * role + e
            plan[at : at + 1, :] = info[4 * which + e, 4:5, :]
        if half == 1:
            start_local(rows, sel.at[which, group])
            start_local(held_delta.at[which, group], deltas.at[which, group])
            for e in (2, 1, 0):
                out[e] = out[e] + out[block_of[4 * which + e, 4, 1]]

    row_halves = (pl.ds(0, TILE // 2), pl.ds(TILE // 2, TILE // 2))
    ret_a0, ret_a1, ret_b0, ret_b1 = (a0_0, a0_1), (a1_0, a1_1), (b0_0, b0_1), (b1_0, b1_1)
    ret_x = (x_0, x_1)
    four = pl.ds(0, 4)

    def give_back(which, role, r):
        out = outs[which][role]
        back = {
            (0, BACK): (ret_a0, down),
            (0, FRONT): (ret_b0, up),
            (1, BACK): (ret_a1, up_other),
            (1, FRONT): (ret_b1, down_other),
        }[which, role]
        returns[which, role, r] = net.send(
            out.at[four, row_halves[r]], back[0][r].at[four], back[1]
        )

    for ref in outs[0] + outs[1] + (ret_own,):
        ref[4] = jnp.zeros((TILE, D), BF16)
    for ref in ret_x + ret_a0 + ret_a1 + ret_b0 + ret_b1:
        ref[4] = jnp.zeros((TILE // 2, D), BF16)
    steps = (0, b, a, 2)
    first_axis = ((xa, xb), (za, zb))
    first2, firsta, firstb = {}, {}, {}
    second2, seconda, secondb = {}, {}, {}
    term_in = {}

    def part(h, stream, unit, j):
        tile = me.tile(steps[unit], steps[j]) if h == 0 else me.tile(steps[j], steps[unit])
        cols = slice(h * HALF, (h + 1) * HALF)
        r = stream % 2
        rows = slice(r * TILE // 2, (r + 1) * TILE // 2)
        if stream < 2:
            return out_x[sm03[8, 0, tile], rows, cols] + ret_x[r][sm03[8, 1, tile], :, cols]
        value = out_own[smo[32 + 2 * OWN, tile], rows, cols]
        value += ret_own[smo[33 + 2 * OWN, tile], rows, cols]
        value += ret_a0[r][smo[32 + 2 * BACK, tile], :, cols]
        value += ret_a1[r][smo[33 + 2 * BACK, tile], :, cols]
        value += ret_b0[r][smo[32 + 2 * FRONT, tile], :, cols]
        return value + ret_b1[r][smo[33 + 2 * FRONT, tile], :, cols]

    def begin_sum(stream):
        if stream < 2:
            term_in[ACROSS, stream].wait_recv()
        if stream >= 2:
            if stream == 2:
                term_in[OWN].wait_recv()
            for which in range(2):
                for role in (BACK, FRONT):
                    returns[which, role, stream - 2].wait_recv()
        for h in range(2):
            for j in range(4):
                s2[h, stream, j] = part(h, stream, ACROSS, j)
            first2[h, stream] = net.send(s2.at[h, stream], r2.at[h, stream], first_axis[h][0])
            for j in range(4):
                sb[h, stream, j] = part(h, stream, BACK, j)
            firstb[h, stream] = net.send(sb.at[h, stream], rb.at[h, stream], first_axis[h][1])

    def pass_sum(stream):
        for h in range(2):
            first2[h, stream].wait_recv()
            for j in range(4):
                r2[h, stream, j] = r2[h, stream, j] + part(h, stream, FRONT, j)
            firsta[h, stream] = net.send(r2.at[h, stream], ra.at[h, stream], first_axis[h][0])

    def begin_second(stream):
        for h in range(2):
            firstb[h, stream].wait_recv()
            firsta[h, stream].wait_recv()
            to_a, to_b = first_axis[1 - h]
            for j in (ACROSS, BACK, FRONT, OWN):
                rb[h, stream, j] = part(h, stream, OWN, j) + rb[h, stream, j] + ra[h, stream, j]
                if j == ACROSS:
                    second2[h, stream] = net.send(rb.at[h, stream, j], u2.at[h, stream], to_a)
                if j == BACK:
                    secondb[h, stream] = net.send(rb.at[h, stream, j], ub.at[h, stream], to_b)

    def pass_second(stream):
        for h in range(2):
            second2[h, stream].wait_recv()
            u2[h, stream] = u2[h, stream] + rb[h, stream, FRONT]
            seconda[h, stream] = net.send(u2.at[h, stream], ua.at[h, stream], first_axis[1 - h][0])

    def end_second(stream):
        for h in range(2):
            secondb[h, stream].wait_recv()
            seconda[h, stream].wait_recv()
            ub[h, stream] = rb[h, stream, OWN] + ub[h, stream] + ua[h, stream]

    fetch(0, OWN)
    send_second(BACK)
    send_second(FRONT)
    send_last(BACK, OWN)
    send_second(ACROSS)
    for load in load_v:
        wait_local(load)
    pairs(0, OWN, 0)
    second_stage(BACK)
    cz_a.wait_recv()
    pos_b = cpall.at[me.x, lax.rem(me.z + b, NZ)]
    cz_f = net.send(pos_b, pos_b, za)
    send_last(FRONT, OWN)
    pairs(0, OWN, 1)
    second_stage(FRONT)
    across_stage(BACK)
    fetch(1, OWN)
    fetch(0, BACK)
    fetch(0, FRONT)
    cz_b.wait_recv()
    cz_f.wait_recv()
    pos_row = cpall.at[me.x]
    cx_a = net.send(pos_row, pos_row, xa)
    cx_b = net.send(pos_row, pos_row, xb)
    forward_last(BACK)
    pairs(1, OWN, 0)
    across_stage(FRONT)
    send_last(ACROSS, OWN)
    second_stage(ACROSS)
    pairs(1, OWN, 1)
    term_in[OWN] = net.send(out1o.at[four], ret_own.at[four], sib)
    complete(BACK)
    pack(BACK)
    across_stage(ACROSS)
    forward_last(FRONT)
    cx_a.wait_recv()
    pos_row_b = cpall.at[lax.rem(me.x + b, NX)]
    cx_f = net.send(pos_row_b, pos_row_b, xa)
    pairs(0, BACK, 0)
    pairs(0, BACK, 1)
    give_back(0, BACK, 0)
    fetch(1, BACK)
    fetch(1, FRONT)
    fetch(0, ACROSS)
    note_in[1, ACROSS] = net.send(no03, no13, sib)
    complete(FRONT)
    pack(FRONT)
    pairs(0, FRONT, 0)
    pairs(0, FRONT, 1)
    give_back(0, FRONT, 0)
    forward_last(ACROSS)
    pairs(1, BACK, 0)
    pairs(1, BACK, 1)
    give_back(1, BACK, 0)
    fetch(1, ACROSS)
    pairs(1, FRONT, 0)
    pairs(1, FRONT, 1)
    give_back(1, FRONT, 0)
    for role in (BACK, FRONT):
        for which in range(2):
            give_back(which, role, 1)
    complete(ACROSS)
    pack(ACROSS)
    pairs(0, ACROSS, 0)
    pairs(1, ACROSS, 0)
    pairs(1, ACROSS, 1)
    for r in range(2):
        term_in[ACROSS, r] = net.send(out1x.at[four, row_halves[r]], ret_x[r].at[four], sib)
    pairs(0, ACROSS, 1)
    begin_sum(2)
    early = len(net.made)
    wait_local(load_c)
    for j in range(8):
        color, role = j // 4, j % 4
        row = (2 * lax.rem(me.y + role_step(color, role), NY) + color) * TILES + m
        start = pl.multiple_of(row * 16, 16)
        cvm[pl.ds(16 * j, 16), :] = cvv[pl.ds(start, 16), :]
    place = lax.broadcasted_iota(jnp.int32, (128, 128), 0)
    chunk = place // 16
    color, role = chunk // 4, lax.rem(chunk, 4)
    step = jnp.where(role == ACROSS, 2, jnp.where(role == FRONT, 1 + 2 * color, 3 - 2 * color))
    step = jnp.where(role == OWN, 0, step)
    owner_grp = 2 * lax.rem(me.y + step, NY) + color
    coarse_ids = (owner_grp * TILES + m) * 16 + lax.rem(place, 16)

    def own_coarse():
        qm = q_own[m]
        total = jnp.zeros((TILE, D), F32)
        for i in range(COARSE // BLOCK):
            vectors = cvv[i * BLOCK : (i + 1) * BLOCK, :]
            labels = lax.broadcasted_iota(jnp.int32, (BLOCK, TILE), 0) + i * BLOCK
            delta = delta_of(mm(vectors, qm, 1, 1), labels, cpall[me.x, me.z])
            total += mm(delta, vectors, 0, 0)
        qc[...] = total

    def rows_coarse(lo, hi):
        def body(t, carry):
            qt = q_own[pl.ds(2 * t, 2)].reshape(2 * TILE, D)
            scores = mm(cvm[...], qt, 1, 1)
            delta = jnp.concatenate(
                [
                    delta_of(
                        scores[:, h * TILE : (h + 1) * TILE],
                        coarse_ids,
                        cpall[t // 2, 2 * lax.rem(t, 2) + h],
                    )
                    for h in range(2)
                ],
                axis=1,
            )
            gc[...] += mm(delta, qt, 1, 0)
            return carry

        lax.fori_loop(lo, hi, body, 0)


    gc[...] = jnp.zeros_like(gc)
    cx_b.wait_recv()
    cx_f.wait_recv()
    rows_coarse(0, 4)
    begin_sum(0)
    begin_sum(1)
    pass_sum(2)
    rows_coarse(4, 8)
    coarse = net.send(gc.at[pl.ds(64 * (1 - c), 64)], gsib, sib)
    pass_sum(0)
    pass_sum(1)
    begin_sum(3)
    begin_second(2)
    own_coarse()
    begin_second(0)
    begin_second(1)
    pass_sum(3)
    pass_second(2)
    pass_second(0)
    pass_second(1)
    coarse.wait_recv()
    for role in range(4):
        gbuf[role] = gc[pl.ds(64 * c + 16 * role, 16)] + gsib[16 * role : 16 * role + 16]
    coarse2 = net.send(gbuf.at[ACROSS], gbuf.at[5], up)
    coarseb = net.send(gbuf.at[BACK], gbuf.at[6], down)
    end_second(0)
    end_second(1)
    home = net.send(ub.at[:, pl.ds(0, 2)], far, across)
    begin_second(3)
    end_second(2)
    coarse2.wait_recv()
    gbuf[4] = gbuf[FRONT] + gbuf[5]
    coarsea = net.send(gbuf.at[4], gbuf.at[7], up)
    pass_second(3)
    net.drain(early)
    for copy in local:
        if not any(copy is other for other in done):
            wait_local(copy)
    coarsea.wait_recv()
    coarseb.wait_recv()
    gco[...] = gbuf[OWN] + gbuf[6] + gbuf[7]
    home.wait_recv()
    end_second(3)
    for h in range(2):
        cols = slice(h * HALF, (h + 1) * HALF)
        for r in range(2):
            rows = slice(r * TILE // 2, (r + 1) * TILE // 2)
            gq[rows, cols] = (
                qc[rows, cols] + ub[h, 2 + r].astype(F32) + far[h, r].astype(F32)
            )
    for copy in local:
        if not any(copy is other for other in done):
            copy.wait()
    net.drain(len(net.made))


def grads_kernel(
    plan, sel, deltas, gq_in, gco_in,
    gm, gl, gq, gco,
    counts, entries, rows, held, acc, row_sem, delta_sem, grad_sem, out_sem,
):
    results = [
        pltpu.make_async_copy(gq_in, gq, out_sem.at[0]),
        pltpu.make_async_copy(gco_in, gco, out_sem.at[1]),
    ]
    for copy in results:
        copy.start()
    stores = [(gm, 0), (gm, 1), (gm, 2), (gm, 3), (gl, 0), (gl, 1)]

    def row_copy(e):
        return pltpu.make_async_copy(sel.at[e], rows.at[e], row_sem.at[e])

    def delta_copy(e):
        return pltpu.make_async_copy(deltas.at[e], held.at[e], delta_sem.at[e])

    for key in range(6):
        counts[key] = 0
    for e in range(SLOTS):
        block = plan[e, 0]

        @pl.when(block >= 0)
        def _():
            row_copy(e).start()
            delta_copy(e).start()
            key = block + 4 * (e // 2 % 2)
            n = counts[key]
            entries[LIST * key + n] = e
            counts[key] = n + 1

    rows[SLOTS] = jnp.zeros((TILE, D), BF16)
    held[SLOTS] = jnp.zeros((BLOCK, TILE), BF16)

    def per_key(key, carry):
        n = counts[key]
        start = LIST * key

        @pl.when(n == 0)
        def _():
            acc[key] = jnp.zeros((BLOCK, D), F32)

        def batch(i, inner):
            at = start + 2 * i
            full = 2 * i + 1 < n
            e0 = entries[at]
            e1 = jnp.where(full, entries[at + 1], SLOTS)
            row_copy(e0).wait()
            delta_copy(e0).wait()

            @pl.when(full)
            def _():
                row_copy(e1).wait()
                delta_copy(e1).wait()

            both = jnp.concatenate([rows[e0], rows[e1]], axis=0)
            delta = jnp.concatenate([held[e0], held[e1]], axis=1)

            @pl.when(i == 0)
            def _():
                for n_col in range(3):
                    cols = slice(n_col * THIRD, (n_col + 1) * THIRD)
                    acc[key, :, cols] = mm(delta, both[:, cols], 1, 0)

            @pl.when(i != 0)
            def _():
                for n_col in range(3):
                    cols = slice(n_col * THIRD, (n_col + 1) * THIRD)
                    acc[key, :, cols] += mm(delta, both[:, cols], 1, 0)

            return inner

        lax.fori_loop(0, (n + 1) // 2, batch, 0)
        for i, (out, j) in enumerate(stores):

            @pl.when(key == i)
            def _():
                pltpu.make_async_copy(acc.at[i], out.at[j], grad_sem.at[i]).start()

        return carry

    lax.fori_loop(0, 6, per_key, 0)
    for i, (out, j) in enumerate(stores):
        pltpu.make_async_copy(acc.at[i], out.at[j], grad_sem.at[i]).wait()
    for copy in results:
        copy.wait()


def vmem():
    return pl.BlockSpec(memory_space=pltpu.VMEM)


def smem():
    return pl.BlockSpec(memory_space=pltpu.SMEM)


def hbm():
    return pl.BlockSpec(memory_space=pl.ANY)


def shape(dims, dtype):
    return jax.ShapeDtypeStruct(dims, dtype)


def shards(
    queries,
    coarse_vectors,
    mid_vectors,
    leaf_vectors,
    coarse_pos,
    mid_pos,
    leaf_pos,
    mid_cand,
    leaf_cand,
    leaf_owner,
):
    dma = pltpu.SemaphoreType.DMA
    mib = 1024 * 1024
    group = pltpu.VMEM((TILES, TILE, D), BF16)
    part = pltpu.VMEM((TILES, REST, D), BF16)
    four = pltpu.VMEM((4, TILE, D), BF16)
    five = pltpu.VMEM((5, TILE, D), BF16)
    half = pltpu.VMEM((5, TILE // 2, D), BF16)
    near = pltpu.VMEM((4, NEAR, D), BF16)
    rest = pltpu.VMEM((4, REST, D), BF16)
    notes = pltpu.VMEM((9, 8, 128), jnp.int32)
    facts = pltpu.SMEM((9, 8, 128), jnp.int32)
    first = pltpu.VMEM((2, 4, 4, TILE // 2, HALF), BF16)
    second = pltpu.VMEM((2, 4, TILE // 2, HALF), BF16)
    gq, gco, plan, sel, deltas = pl.pallas_call(
        main_kernel,
        out_shape=(
            shape((TILE, D), F32),
            shape((16, D), F32),
            shape((SLOTS, 128), jnp.int32),
            shape((2, 16, TILE, D), BF16),
            shape((2, 16, BLOCK, TILE), BF16),
        ),
        in_specs=[hbm(), vmem(), vmem(), vmem(), vmem(), vmem(), vmem(), hbm(), hbm(), hbm()],
        out_specs=(vmem(), vmem(), vmem(), hbm(), hbm()),
        scratch_shapes=[
            group, part, part, group,
            pltpu.VMEM((18, 8, 128), jnp.int32),
            pltpu.VMEM((COARSE, D), BF16),
            pltpu.VMEM((128, D), BF16),
            pltpu.VMEM((NX, NZ, 8, TILE), jnp.int32),
            four, four, four, four, four, four, four, four,
            notes, notes, notes, notes, notes, notes, notes, notes,
            facts, facts, facts, facts, facts, facts, facts, facts,
            notes, notes, notes,
            pltpu.VMEM((40, 128), jnp.int32),
            pltpu.SMEM((40, 128), jnp.int32),
            near, near, near, near, four, four, rest, rest,
            five, five, five, five, five, five, five, five,
            five,
            half, half, half, half, half, half, half, half, half, half,
            pltpu.VMEM((6, BLOCK, D), BF16),
            pltpu.VMEM((2, 16, BLOCK, TILE), BF16),
            pltpu.VMEM((128, D), F32),
            pltpu.VMEM((TILE, D), F32),
            pltpu.VMEM((64, D), F32),
            pltpu.VMEM((8, 16, D), F32),
            first, first, first, first, first,
            second, second, second,
            pltpu.VMEM((2, 2, TILE // 2, HALF), BF16),
            dma((40,)),
            dma((COPIES,)),
            dma((COPIES,)),
        ],
        compiler_params=pltpu.CompilerParams(
            collective_id=0, has_side_effects=True, vmem_limit_bytes=62 * mib
        ),
        name="main",
    )(
        queries.reshape(TILES, TILE, D),
        mid_pos.T,
        leaf_pos.T,
        mid_cand.T,
        leaf_cand.T,
        coarse_pos.T,
        leaf_owner.reshape(2, 128),
        coarse_vectors,
        mid_vectors.reshape(4, BLOCK, D),
        leaf_vectors.reshape(2, BLOCK, D),
    )
    gm, gl, gq, gco = pl.pallas_call(
        grads_kernel,
        out_shape=(
            shape((4, BLOCK, D), F32),
            shape((2, BLOCK, D), F32),
            shape((TILE, D), F32),
            shape((16, D), F32),
        ),
        in_specs=[smem(), hbm(), hbm(), vmem(), vmem()],
        out_specs=(hbm(), hbm(), hbm(), hbm()),
        scratch_shapes=[
            pltpu.SMEM((6,), jnp.int32),
            pltpu.SMEM((6 * LIST + 1,), jnp.int32),
            pltpu.VMEM((SLOTS + 1, TILE, D), BF16),
            pltpu.VMEM((SLOTS + 1, BLOCK, TILE), BF16),
            pltpu.VMEM((6, BLOCK, D), F32),
            dma((SLOTS,)),
            dma((SLOTS,)),
            dma((6,)),
            dma((2,)),
        ],
        compiler_params=pltpu.CompilerParams(vmem_limit_bytes=60 * mib),
        name="grads",
    )(plan, sel.reshape(SLOTS, TILE, D), deltas.reshape(SLOTS, BLOCK, TILE), gq, gco)
    return gq, gco, gm.reshape(4 * BLOCK, D), gl.reshape(2 * BLOCK, D)


def solution(mesh):
    placed = (
        P("grp", None),
        P(),
        P(("grp", "mid"), None),
        P(("grp", "mid"), None),
        P(("grp", "mid"), None),
        P("grp", None),
        P("grp", None),
        P("grp", None),
        P("grp", None),
        P(),
    )
    return jax.shard_map(
        shards,
        mesh=mesh,
        in_specs=placed,
        out_specs=(
            P(("grp", "mid"), None),
            P(("grp", "mid"), None),
            P(("grp", "mid"), None),
            P(("grp", "mid"), None),
        ),
        check_vma=False,
    )
```

```python
import jax
import jax.numpy as jnp
from jax import lax
from jax.experimental import pallas as pl
from jax.experimental.pallas import tpu as pltpu
from jax.sharding import PartitionSpec as P

TILE = 128
BLOCK = 512
COARSE = 2048
K_CAND = 8
D = 768
NY, NX, NZ = 4, 4, 4
TILES = NX * NZ
BIG = 1 << 20
F32 = jnp.float32
BF16 = jnp.bfloat16
MESH = pl.DeviceIdType.MESH
THIRD = D // 3
HALF = D // 2
NEAR = 64
REST = TILE - NEAR


def mm(a, b, ca, cb):
    return lax.dot_general(a, b, (((ca,), (cb,)), ((), ())), preferred_element_type=F32)


def delta_of(scores, labels, positives):
    hit = labels == positives[0:1]
    for p in range(1, 4):
        hit = hit | (labels == positives[p : p + 1])
    return (0.125 * jnp.tanh(0.5 * scores) + jnp.where(hit, -0.125, 0.125)).astype(BF16)


class Place:
    def __init__(self):
        grp, mid = lax.axis_index("grp"), lax.axis_index("mid")
        self.y, self.c = grp // 2, lax.rem(grp, 2)
        self.x, self.z = mid // NZ, lax.rem(mid, NZ)
        self.mid = mid
        self.ahead = 1 + 2 * self.c
        self.behind = 3 - 2 * self.c

    def at(self, dy=0, dx=0, dz=0, other=False):
        y, x, z = lax.rem(self.y + dy, NY), lax.rem(self.x + dx, NX), lax.rem(self.z + dz, NZ)
        return (2 * y + (1 - self.c if other else self.c), NZ * x + z)

    def sibling(self):
        return (2 * self.y + 1 - self.c, self.mid)

    def tile(self, dx, dz):
        return NZ * lax.rem(self.x + dx, NX) + lax.rem(self.z + dz, NZ)

    def greet(self):
        near = [self.sibling(), self.at(dy=2)]
        for step in (self.ahead, self.behind):
            near += [self.at(dy=step), self.at(dy=step, other=True)]
            near += [self.at(dx=step), self.at(dz=step)]
        barrier = pltpu.get_barrier_semaphore()
        for device in near:
            pl.semaphore_signal(barrier, inc=1, device_id=device, device_id_type=MESH)
        pl.semaphore_wait(barrier, len(near))


class Net:
    def __init__(self, send_sem, recv_sem):
        self.send_sem, self.recv_sem, self.made, self.drained = send_sem, recv_sem, [], 0

    def send(self, src, dst, device):
        i = len(self.made)
        copy = pltpu.make_async_remote_copy(
            src_ref=src,
            dst_ref=dst,
            send_sem=self.send_sem.at[i],
            recv_sem=self.recv_sem.at[i],
            device_id=device,
            device_id_type=MESH,
        )
        copy.start()
        self.made.append(copy)
        return copy

    def drain(self, count):
        for copy in self.made[self.drained : count]:
            copy.wait_send()
        self.drained = count


COPIES = 200
OWN, BACK, FRONT, ACROSS = range(4)
SLOTS = 32
LIST = 16


def role_step(color, role):
    return (0, 3 - 2 * color, 1 + 2 * color, 2)[role]


def main_kernel(
    q, mp, lp, mc, lc, cp, owner, cv, midv, leafv,
    gq, gco, plan, sel, deltas,
    q_own, q_b, q_a, q_2, p_own, cvv, cvm, cpall,
    in00, in01, in02, in03, in10, in11, in12, in13,
    no00, no01, no02, no03, no10, no11, no12, no13,
    sm00, sm01, sm02, sm03, sm10, sm11, sm12, sm13,
    no_a, no_b, no_x, planv, smo, pk_as, pk_ao, pk_bs, pk_bo, pk_own, pk_x, pk_b, pk_f,
    out_own, out_x, out0b, out0f, out1o, out1b, out1f, out1x,
    ret_own, x_0, x_1, a0_0, a0_1, a1_0, a1_1, b0_0, b0_1, b1_0, b1_1,
    vectors, held_delta, gc, qc, gsib, gbuf,
    s2, sb, r2, rb, ra, u2, ub, ua, far, local_sem, send_sem, recv_sem,
):
    me = Place()
    c, a, b = me.c, me.ahead, me.behind
    net = Net(send_sem, recv_sem)
    local, done = [], []

    def start_local(src, dst):
        copy = pltpu.make_async_copy(src, dst, local_sem.at[len(local)])
        copy.start()
        local.append(copy)
        return copy

    def wait_local(copy):
        copy.wait()
        done.append(copy)

    load_q = start_local(q, q_own)
    load_v = [start_local(midv, vectors.at[pl.ds(0, 4)]), start_local(leafv, vectors.at[pl.ds(4, 2)])]
    load_c = start_local(cv, cvv)
    for t in range(TILES):
        p_own[t, 0:4, :] = mp[:, t * TILE : (t + 1) * TILE]
        p_own[t, 4:8, :] = lp[:, t * TILE : (t + 1) * TILE]
    p_own[16:18] = jnp.full((2, 8, 128), -1, jnp.int32)
    p_own[16, :, 0:TILES] = mc[...]
    p_own[17, :, 0:TILES] = lc[...]
    cpall[me.x, me.z, 0:4, :] = cp[...]
    cpall[me.x, me.z, 4:8, :] = cp[...]
    me.greet()

    m = me.mid
    up, down, across = me.at(dy=a), me.at(dy=b), me.at(dy=2)
    up_other, down_other = me.at(dy=a, other=True), me.at(dy=b, other=True)
    xa, xb, za, zb = me.at(dx=a), me.at(dx=b), me.at(dz=a), me.at(dz=b)
    sib = me.sibling()
    planes = {BACK: q_b, FRONT: q_a, ACROSS: q_2}
    slots = ((in00, in01, in02, in03), (in10, in11, in12, in13))
    notes = ((no00, no01, no02, no03), (no10, no11, no12, no13))
    facts = ((sm00, sm01, sm02, sm03), (sm10, sm11, sm12, sm13))
    outs = ((out_own, out0b, out0f, out_x), (out1o, out1b, out1f, out1x))

    rest, near = pl.ds(NEAR, REST), pl.ds(0, NEAR)
    y_in = {
        BACK: net.send(q.at[m, rest], q_b.at[m], up),
        FRONT: net.send(q.at[m, rest], q_a.at[m], down),
        ACROSS: net.send(q.at[m], q_2.at[m], across),
    }
    pos_own = cpall.at[me.x, me.z]
    cz_a = net.send(pos_own, pos_own, za)
    cz_b = net.send(pos_own, pos_own, zb)

    index = lax.broadcasted_iota(jnp.int32, (2, 128), 0) * 128 + lax.broadcasted_iota(
        jnp.int32, (2, 128), 1
    )
    code = 4 * (
        TILES * lax.broadcasted_iota(jnp.int32, (8, 128), 0)
        + lax.broadcasted_iota(jnp.int32, (8, 128), 1)
    )
    lane = lax.broadcasted_iota(jnp.int32, (1, 128), 1)
    mids, leaves = p_own[16], p_own[17]

    def whole(value):
        return jnp.broadcast_to(value, (1, 128))

    def plan_slots(label):
        step = (0, a, b, 2)[label]
        for which, core in enumerate((c, 1 - c)):
            device = (2 * lax.rem(me.y + step, NY) + core) * TILES + m
            held = [
                whole(
                    jnp.sum(
                        jnp.where(owner[...] == 2 * device + i, index, 0), axis=(0, 1), keepdims=True
                    )
                )
                for i in range(2)
            ]
            entries = []
            for live, block in (
                ((mids >> 2) == device, mids & 3),
                ((leaves == held[0]) | (leaves == held[1]), (leaves == held[1]).astype(jnp.int32)),
            ):
                found = code + block
                first = whole(jnp.min(jnp.where(live, found, BIG), axis=(0, 1), keepdims=True))
                final = whole(jnp.max(jnp.where(live, found, -1), axis=(0, 1), keepdims=True))
                some = first < BIG
                entries.append((some, jnp.where(some, first, 0)))
                two = some & (final != first)
                entries.append((two, jnp.where(two, final, 0)))
            tiles = [(value >> 2) & 15 for _, value in entries]
            spots = jnp.full((1, 128), 4, jnp.int32)
            for e in (3, 2, 1, 0):
                spots = jnp.where(entries[e][0] & (tiles[e] == lane), e, spots)
            at = 32 + 2 * label + which
            planv[at : at + 1, :] = spots
            for e, (valid, value) in enumerate(entries):
                follow = jnp.full((1, 128), 4, jnp.int32)
                for f in range(3, e, -1):
                    follow = jnp.where(valid & entries[f][0] & (tiles[f] == tiles[e]), f, follow)
                row = jnp.where(lane == 0, jnp.where(valid, value & 3, -1), follow)
                row = jnp.where(lane == 2, tiles[e], row)
                row = jnp.where(lane == 3, value >> 6, row)
                row = jnp.where(lane == 4, (value & 3) + 4 * (e // 2), row)
                at = 8 * label + 4 * which + e
                planv[at : at + 1, :] = row
    planv[...] = jnp.zeros((40, 128), jnp.int32)
    plan_slots(BACK)
    plan_slots(FRONT)
    to_smem = start_local(planv, smo)
    wait_local(load_q)
    wait_local(to_smem)
    notes_out = (no00, no_a, no_b, no_x)

    def fill_notes(label):
        out = notes_out[label]
        for e in range(8):
            at = 8 * label + e
            level = 4 * (e % 4 // 2)
            positives = p_own[smo[at, 2]][level : level + 4] - BLOCK * smo[at, 3]
            out[e, 0:4, :] = positives
            out[e, 4:5, :] = planv[at : at + 1, :]
            out[e, 5:8, :] = jnp.zeros((3, 128), jnp.int32)
        out[8, 0:2, :] = planv[32 + 2 * label : 34 + 2 * label, :]
        out[8, 2:8, :] = jnp.zeros((6, 128), jnp.int32)

    direct, note_in = {}, {}
    for label, targets in ((BACK, ((pk_as, up), (pk_ao, up_other))), (FRONT, ((pk_bs, down), (pk_bo, down_other)))):
        fill_notes(label)
        for which, (buffer, device) in enumerate(targets):
            for e in range(4):
                buffer[e] = q_own[smo[8 * label + 4 * which + e, 2], 0:NEAR]
            note_in[which, label] = net.send(notes_out[label], notes[which][label], device)
            direct[which, label] = net.send(buffer, slots[which][label].at[:, near], device)
    plan_slots(ACROSS)
    plan_slots(OWN)
    to_smem = start_local(planv, smo)
    wait_local(to_smem)
    fill_notes(ACROSS)
    note_in[0, ACROSS] = net.send(no_x, no03, across)
    fill_notes(OWN)
    for e in range(4):
        pk_own[e] = q_own[smo[4 + e, 2]]
    note_in[1, OWN] = net.send(no00, no10, sib)
    beside = {OWN: net.send(pk_own, in10, sib)}
    for e in range(4):
        in00[e] = q_own[smo[e, 2]]

    axes = ((za, zb, xa, xb), (xa, xb, za, zb))
    walk = (0, b, a, 2)

    def rows_of(role, h):
        size = (TILE if role == ACROSS else REST) // 2
        return pl.ds(h * size, size)

    def tile_of(h, first, last):
        return me.tile(last, first) if h == 0 else me.tile(first, last)

    second, second_f, last, last_f = {}, {}, {}, {}

    def send_second(role):
        y_in[role].wait_recv()
        for h, (to_a, to_b, _, _) in enumerate(axes):
            piece = planes[role].at[m, rows_of(role, h)]
            second[role, h] = (net.send(piece, piece, to_a), net.send(piece, piece, to_b))

    def send_last(role, key):
        for h, (_, _, to_a, to_b) in enumerate(axes):
            piece = planes[role].at[tile_of(h, walk[key], 0), rows_of(role, h)]
            last[role, h, key] = (net.send(piece, piece, to_a), net.send(piece, piece, to_b))

    def second_stage(role):
        for h, (to_a, _, _, _) in enumerate(axes):
            second[role, h][0].wait_recv()
            piece = planes[role].at[tile_of(h, b, 0), rows_of(role, h)]
            second_f[role, h] = net.send(piece, piece, to_a)
        send_last(role, BACK)
        for h in range(2):
            second[role, h][1].wait_recv()
        send_last(role, FRONT)

    def across_stage(role):
        for h in range(2):
            second_f[role, h].wait_recv()
        send_last(role, ACROSS)

    def forward_last(role):
        for key, step in enumerate(walk):
            for h, (_, _, to_a, _) in enumerate(axes):
                last[role, h, key][0].wait_recv()
                piece = planes[role].at[tile_of(h, step, b), rows_of(role, h)]
                last_f[role, h, key] = net.send(piece, piece, to_a)

    def complete(role):
        for key in range(4):
            for h in range(2):
                last[role, h, key][1].wait_recv()
                last_f[role, h, key].wait_recv()

    fetches = {}

    def fetch(which, role):
        if (which, role) in note_in:
            note_in[which, role].wait_recv()
        fetches[which, role] = start_local(notes[which][role], facts[which][role])

    def know(which, role):
        wait_local(fetches[which, role])

    def pack(role):
        know(0, role)
        rows = planes[role]
        buffer = {BACK: pk_b, FRONT: pk_f, ACROSS: pk_x}[role]
        for e in range(4):
            buffer[e] = rows[facts[0][role][4 + e, 4, 2]]
            if role == ACROSS and e % 2:
                duo = pl.ds(e - 1, 2)
                beside[role, e // 2] = net.send(buffer.at[duo], in13.at[duo], sib)
        if role != ACROSS:
            beside[role] = net.send(buffer, slots[1][role].at[:, rest], sib)
        for e in range(4):
            value = rows[facts[0][role][e, 4, 2]]
            if role == ACROSS:
                in03[e] = value
            else:
                slots[0][role][e, NEAR:TILE] = value

    labels = lax.broadcasted_iota(jnp.int32, (BLOCK, TILE), 0)
    returns = {}

    def pairs(which, role, half):
        block_of, rows, info, out = (
            facts[which][role], slots[which][role], notes[which][role], outs[which][role]
        )
        group = pl.ds(4 * role, 4)
        if half == 0:
            if which == 1 or role == OWN:
                know(which, role)
            if (which, role) in direct:
                direct[which, role].wait_recv()
            if which == 1 and role != ACROSS:
                beside[role].wait_recv()
        if which == 1 and role == ACROSS:
            beside[role, half].wait_recv()
        both = (2 * half, 2 * half + 1)
        blocks = [vectors[block_of[4 * which + e, 4, 4]] for e in both]
        scores = [mm(block, rows[e], 1, 1) for e, block in zip(both, blocks)]
        for e, block, score in zip(both, blocks, scores):
            delta = delta_of(score, labels, info[4 * which + e])
            held_delta[which, 4 * role + e] = delta
            out[e] = mm(delta, block, 0, 0).astype(BF16)
            at = 16 * which + 4 * role + e
            plan[at : at + 1, :] = info[4 * which + e, 4:5, :]
        if half == 1:
            start_local(rows, sel.at[which, group])
            start_local(held_delta.at[which, group], deltas.at[which, group])
            for e in (2, 1, 0):
                out[e] = out[e] + out[block_of[4 * which + e, 4, 1]]

    row_halves = (pl.ds(0, TILE // 2), pl.ds(TILE // 2, TILE // 2))
    ret_a0, ret_a1, ret_b0, ret_b1 = (a0_0, a0_1), (a1_0, a1_1), (b0_0, b0_1), (b1_0, b1_1)
    ret_x = (x_0, x_1)
    four = pl.ds(0, 4)

    def give_back(which, role, r):
        out = outs[which][role]
        back = {
            (0, BACK): (ret_a0, down),
            (0, FRONT): (ret_b0, up),
            (1, BACK): (ret_a1, up_other),
            (1, FRONT): (ret_b1, down_other),
        }[which, role]
        returns[which, role, r] = net.send(
            out.at[four, row_halves[r]], back[0][r].at[four], back[1]
        )

    for ref in outs[0] + outs[1] + (ret_own,):
        ref[4] = jnp.zeros((TILE, D), BF16)
    for ref in ret_x + ret_a0 + ret_a1 + ret_b0 + ret_b1:
        ref[4] = jnp.zeros((TILE // 2, D), BF16)
    steps = (0, b, a, 2)
    first_axis = ((xa, xb), (za, zb))
    first2, firsta, firstb = {}, {}, {}
    second2, seconda, secondb = {}, {}, {}
    term_in = {}

    def part(h, stream, unit, j):
        tile = me.tile(steps[unit], steps[j]) if h == 0 else me.tile(steps[j], steps[unit])
        cols = slice(h * HALF, (h + 1) * HALF)
        r = stream % 2
        rows = slice(r * TILE // 2, (r + 1) * TILE // 2)
        if stream < 2:
            return out_x[sm03[8, 0, tile], rows, cols] + ret_x[r][sm03[8, 1, tile], :, cols]
        value = out_own[smo[32 + 2 * OWN, tile], rows, cols]
        value += ret_own[smo[33 + 2 * OWN, tile], rows, cols]
        value += ret_a0[r][smo[32 + 2 * BACK, tile], :, cols]
        value += ret_a1[r][smo[33 + 2 * BACK, tile], :, cols]
        value += ret_b0[r][smo[32 + 2 * FRONT, tile], :, cols]
        return value + ret_b1[r][smo[33 + 2 * FRONT, tile], :, cols]

    def begin_sum(stream):
        if stream < 2:
            term_in[ACROSS, stream].wait_recv()
        if stream >= 2:
            if stream == 2:
                term_in[OWN].wait_recv()
            for which in range(2):
                for role in (BACK, FRONT):
                    returns[which, role, stream - 2].wait_recv()
        for h in range(2):
            for j in range(4):
                s2[h, stream, j] = part(h, stream, ACROSS, j)
            first2[h, stream] = net.send(s2.at[h, stream], r2.at[h, stream], first_axis[h][0])
            for j in range(4):
                sb[h, stream, j] = part(h, stream, BACK, j)
            firstb[h, stream] = net.send(sb.at[h, stream], rb.at[h, stream], first_axis[h][1])

    def pass_sum(stream):
        for h in range(2):
            first2[h, stream].wait_recv()
            for j in range(4):
                r2[h, stream, j] = r2[h, stream, j] + part(h, stream, FRONT, j)
            firsta[h, stream] = net.send(r2.at[h, stream], ra.at[h, stream], first_axis[h][0])

    def begin_second(stream):
        for h in range(2):
            firstb[h, stream].wait_recv()
            firsta[h, stream].wait_recv()
            to_a, to_b = first_axis[1 - h]
            for j in (ACROSS, BACK, FRONT, OWN):
                rb[h, stream, j] = part(h, stream, OWN, j) + rb[h, stream, j] + ra[h, stream, j]
                if j == ACROSS:
                    second2[h, stream] = net.send(rb.at[h, stream, j], u2.at[h, stream], to_a)
                if j == BACK:
                    secondb[h, stream] = net.send(rb.at[h, stream, j], ub.at[h, stream], to_b)

    def pass_second(stream):
        for h in range(2):
            second2[h, stream].wait_recv()
            u2[h, stream] = u2[h, stream] + rb[h, stream, FRONT]
            seconda[h, stream] = net.send(u2.at[h, stream], ua.at[h, stream], first_axis[1 - h][0])

    def end_second(stream):
        for h in range(2):
            secondb[h, stream].wait_recv()
            seconda[h, stream].wait_recv()
            ub[h, stream] = rb[h, stream, OWN] + ub[h, stream] + ua[h, stream]

    fetch(0, OWN)
    send_second(BACK)
    send_second(FRONT)
    send_last(BACK, OWN)
    send_second(ACROSS)
    for load in load_v:
        wait_local(load)
    pairs(0, OWN, 0)
    second_stage(BACK)
    cz_a.wait_recv()
    pos_b = cpall.at[me.x, lax.rem(me.z + b, NZ)]
    cz_f = net.send(pos_b, pos_b, za)
    send_last(FRONT, OWN)
    pairs(0, OWN, 1)
    second_stage(FRONT)
    across_stage(BACK)
    fetch(1, OWN)
    fetch(0, BACK)
    fetch(0, FRONT)
    cz_b.wait_recv()
    cz_f.wait_recv()
    pos_row = cpall.at[me.x]
    cx_a = net.send(pos_row, pos_row, xa)
    cx_b = net.send(pos_row, pos_row, xb)
    forward_last(BACK)
    pairs(1, OWN, 0)
    across_stage(FRONT)
    send_last(ACROSS, OWN)
    second_stage(ACROSS)
    pairs(1, OWN, 1)
    term_in[OWN] = net.send(out1o.at[four], ret_own.at[four], sib)
    complete(BACK)
    pack(BACK)
    across_stage(ACROSS)
    forward_last(FRONT)
    cx_a.wait_recv()
    pos_row_b = cpall.at[lax.rem(me.x + b, NX)]
    cx_f = net.send(pos_row_b, pos_row_b, xa)
    pairs(0, BACK, 0)
    pairs(0, BACK, 1)
    give_back(0, BACK, 0)
    fetch(1, BACK)
    fetch(1, FRONT)
    fetch(0, ACROSS)
    note_in[1, ACROSS] = net.send(no03, no13, sib)
    complete(FRONT)
    pack(FRONT)
    pairs(0, FRONT, 0)
    pairs(0, FRONT, 1)
    give_back(0, FRONT, 0)
    forward_last(ACROSS)
    pairs(1, BACK, 0)
    pairs(1, BACK, 1)
    give_back(1, BACK, 0)
    fetch(1, ACROSS)
    pairs(1, FRONT, 0)
    pairs(1, FRONT, 1)
    give_back(1, FRONT, 0)
    for role in (BACK, FRONT):
        for which in range(2):
            give_back(which, role, 1)
    complete(ACROSS)
    pack(ACROSS)
    pairs(0, ACROSS, 0)
    pairs(1, ACROSS, 0)
    pairs(1, ACROSS, 1)
    for r in range(2):
        term_in[ACROSS, r] = net.send(out1x.at[four, row_halves[r]], ret_x[r].at[four], sib)
    pairs(0, ACROSS, 1)
    early = len(net.made)
    wait_local(load_c)
    for j in range(8):
        color, role = j // 4, j % 4
        row = (2 * lax.rem(me.y + role_step(color, role), NY) + color) * TILES + m
        start = pl.multiple_of(row * 16, 16)
        cvm[pl.ds(16 * j, 16), :] = cvv[pl.ds(start, 16), :]
    place = lax.broadcasted_iota(jnp.int32, (128, 128), 0)
    chunk = place // 16
    color, role = chunk // 4, lax.rem(chunk, 4)
    step = jnp.where(role == ACROSS, 2, jnp.where(role == FRONT, 1 + 2 * color, 3 - 2 * color))
    step = jnp.where(role == OWN, 0, step)
    owner_grp = 2 * lax.rem(me.y + step, NY) + color
    coarse_ids = (owner_grp * TILES + m) * 16 + lax.rem(place, 16)

    def own_coarse():
        qm = q_own[m]
        total = jnp.zeros((TILE, D), F32)
        for i in range(COARSE // BLOCK):
            vectors = cvv[i * BLOCK : (i + 1) * BLOCK, :]
            labels = lax.broadcasted_iota(jnp.int32, (BLOCK, TILE), 0) + i * BLOCK
            delta = delta_of(mm(vectors, qm, 1, 1), labels, cpall[me.x, me.z])
            total += mm(delta, vectors, 0, 0)
        qc[...] = total

    def rows_coarse(lo, hi):
        def body(t, carry):
            qt = q_own[pl.ds(2 * t, 2)].reshape(2 * TILE, D)
            scores = mm(cvm[...], qt, 1, 1)
            delta = jnp.concatenate(
                [
                    delta_of(
                        scores[:, h * TILE : (h + 1) * TILE],
                        coarse_ids,
                        cpall[t // 2, 2 * lax.rem(t, 2) + h],
                    )
                    for h in range(2)
                ],
                axis=1,
            )
            gc[...] += mm(delta, qt, 1, 0)
            return carry

        lax.fori_loop(lo, hi, body, 0)


    gc[...] = jnp.zeros_like(gc)
    cx_b.wait_recv()
    cx_f.wait_recv()
    rows_coarse(0, 4)
    begin_sum(0)
    begin_sum(1)
    begin_sum(2)
    rows_coarse(4, 8)
    coarse = net.send(gc.at[pl.ds(64 * (1 - c), 64)], gsib, sib)
    pass_sum(0)
    pass_sum(1)
    pass_sum(2)
    own_coarse()
    begin_sum(3)
    begin_second(0)
    begin_second(1)
    begin_second(2)
    pass_sum(3)
    pass_second(0)
    pass_second(1)
    pass_second(2)
    coarse.wait_recv()
    for role in range(4):
        gbuf[role] = gc[pl.ds(64 * c + 16 * role, 16)] + gsib[16 * role : 16 * role + 16]
    coarse2 = net.send(gbuf.at[ACROSS], gbuf.at[5], up)
    coarseb = net.send(gbuf.at[BACK], gbuf.at[6], down)
    end_second(0)
    end_second(1)
    home = net.send(ub.at[:, pl.ds(0, 2)], far, across)
    begin_second(3)
    end_second(2)
    coarse2.wait_recv()
    gbuf[4] = gbuf[FRONT] + gbuf[5]
    coarsea = net.send(gbuf.at[4], gbuf.at[7], up)
    pass_second(3)
    net.drain(early)
    for copy in local:
        if not any(copy is other for other in done):
            wait_local(copy)
    coarsea.wait_recv()
    coarseb.wait_recv()
    gco[...] = gbuf[OWN] + gbuf[6] + gbuf[7]
    home.wait_recv()
    end_second(3)
    for h in range(2):
        cols = slice(h * HALF, (h + 1) * HALF)
        for r in range(2):
            rows = slice(r * TILE // 2, (r + 1) * TILE // 2)
            gq[rows, cols] = (
                qc[rows, cols] + ub[h, 2 + r].astype(F32) + far[h, r].astype(F32)
            )
    for copy in local:
        if not any(copy is other for other in done):
            copy.wait()
    net.drain(len(net.made))


def grads_kernel(
    plan, sel, deltas, gq_in, gco_in,
    gm, gl, gq, gco,
    counts, entries, rows, held, acc, row_sem, delta_sem, grad_sem, out_sem,
):
    results = [
        pltpu.make_async_copy(gq_in, gq, out_sem.at[0]),
        pltpu.make_async_copy(gco_in, gco, out_sem.at[1]),
    ]
    for copy in results:
        copy.start()
    stores = [(gm, 0), (gm, 1), (gm, 2), (gm, 3), (gl, 0), (gl, 1)]

    def row_copy(e):
        return pltpu.make_async_copy(sel.at[e], rows.at[e], row_sem.at[e])

    def delta_copy(e):
        return pltpu.make_async_copy(deltas.at[e], held.at[e], delta_sem.at[e])

    for key in range(6):
        counts[key] = 0
    for e in range(SLOTS):
        block = plan[e, 0]

        @pl.when(block >= 0)
        def _():
            row_copy(e).start()
            delta_copy(e).start()
            key = block + 4 * (e // 2 % 2)
            n = counts[key]
            entries[LIST * key + n] = e
            counts[key] = n + 1

    rows[SLOTS] = jnp.zeros((TILE, D), BF16)
    held[SLOTS] = jnp.zeros((BLOCK, TILE), BF16)

    def per_key(key, carry):
        n = counts[key]
        start = LIST * key

        @pl.when(n == 0)
        def _():
            acc[key] = jnp.zeros((BLOCK, D), F32)

        def batch(i, inner):
            at = start + 2 * i
            full = 2 * i + 1 < n
            e0 = entries[at]
            e1 = jnp.where(full, entries[at + 1], SLOTS)
            row_copy(e0).wait()
            delta_copy(e0).wait()

            @pl.when(full)
            def _():
                row_copy(e1).wait()
                delta_copy(e1).wait()

            both = jnp.concatenate([rows[e0], rows[e1]], axis=0)
            delta = jnp.concatenate([held[e0], held[e1]], axis=1)

            @pl.when(i == 0)
            def _():
                for n_col in range(3):
                    cols = slice(n_col * THIRD, (n_col + 1) * THIRD)
                    acc[key, :, cols] = mm(delta, both[:, cols], 1, 0)

            @pl.when(i != 0)
            def _():
                for n_col in range(3):
                    cols = slice(n_col * THIRD, (n_col + 1) * THIRD)
                    acc[key, :, cols] += mm(delta, both[:, cols], 1, 0)

            return inner

        lax.fori_loop(0, (n + 1) // 2, batch, 0)
        for i, (out, j) in enumerate(stores):

            @pl.when(key == i)
            def _():
                pltpu.make_async_copy(acc.at[i], out.at[j], grad_sem.at[i]).start()

        return carry

    lax.fori_loop(0, 6, per_key, 0)
    for i, (out, j) in enumerate(stores):
        pltpu.make_async_copy(acc.at[i], out.at[j], grad_sem.at[i]).wait()
    for copy in results:
        copy.wait()


def vmem():
    return pl.BlockSpec(memory_space=pltpu.VMEM)


def smem():
    return pl.BlockSpec(memory_space=pltpu.SMEM)


def hbm():
    return pl.BlockSpec(memory_space=pl.ANY)


def shape(dims, dtype):
    return jax.ShapeDtypeStruct(dims, dtype)


def shards(
    queries,
    coarse_vectors,
    mid_vectors,
    leaf_vectors,
    coarse_pos,
    mid_pos,
    leaf_pos,
    mid_cand,
    leaf_cand,
    leaf_owner,
):
    dma = pltpu.SemaphoreType.DMA
    mib = 1024 * 1024
    group = pltpu.VMEM((TILES, TILE, D), BF16)
    part = pltpu.VMEM((TILES, REST, D), BF16)
    four = pltpu.VMEM((4, TILE, D), BF16)
    five = pltpu.VMEM((5, TILE, D), BF16)
    half = pltpu.VMEM((5, TILE // 2, D), BF16)
    near = pltpu.VMEM((4, NEAR, D), BF16)
    rest = pltpu.VMEM((4, REST, D), BF16)
    notes = pltpu.VMEM((9, 8, 128), jnp.int32)
    facts = pltpu.SMEM((9, 8, 128), jnp.int32)
    first = pltpu.VMEM((2, 4, 4, TILE // 2, HALF), BF16)
    second = pltpu.VMEM((2, 4, TILE // 2, HALF), BF16)
    gq, gco, plan, sel, deltas = pl.pallas_call(
        main_kernel,
        out_shape=(
            shape((TILE, D), F32),
            shape((16, D), F32),
            shape((SLOTS, 128), jnp.int32),
            shape((2, 16, TILE, D), BF16),
            shape((2, 16, BLOCK, TILE), BF16),
        ),
        in_specs=[hbm(), vmem(), vmem(), vmem(), vmem(), vmem(), vmem(), hbm(), hbm(), hbm()],
        out_specs=(vmem(), vmem(), vmem(), hbm(), hbm()),
        scratch_shapes=[
            group, part, part, group,
            pltpu.VMEM((18, 8, 128), jnp.int32),
            pltpu.VMEM((COARSE, D), BF16),
            pltpu.VMEM((128, D), BF16),
            pltpu.VMEM((NX, NZ, 8, TILE), jnp.int32),
            four, four, four, four, four, four, four, four,
            notes, notes, notes, notes, notes, notes, notes, notes,
            facts, facts, facts, facts, facts, facts, facts, facts,
            notes, notes, notes,
            pltpu.VMEM((40, 128), jnp.int32),
            pltpu.SMEM((40, 128), jnp.int32),
            near, near, near, near, four, four, rest, rest,
            five, five, five, five, five, five, five, five,
            five,
            half, half, half, half, half, half, half, half, half, half,
            pltpu.VMEM((6, BLOCK, D), BF16),
            pltpu.VMEM((2, 16, BLOCK, TILE), BF16),
            pltpu.VMEM((128, D), F32),
            pltpu.VMEM((TILE, D), F32),
            pltpu.VMEM((64, D), F32),
            pltpu.VMEM((8, 16, D), F32),
            first, first, first, first, first,
            second, second, second,
            pltpu.VMEM((2, 2, TILE // 2, HALF), BF16),
            dma((40,)),
            dma((COPIES,)),
            dma((COPIES,)),
        ],
        compiler_params=pltpu.CompilerParams(
            collective_id=0, has_side_effects=True, vmem_limit_bytes=62 * mib
        ),
        name="main",
    )(
        queries.reshape(TILES, TILE, D),
        mid_pos.T,
        leaf_pos.T,
        mid_cand.T,
        leaf_cand.T,
        coarse_pos.T,
        leaf_owner.reshape(2, 128),
        coarse_vectors,
        mid_vectors.reshape(4, BLOCK, D),
        leaf_vectors.reshape(2, BLOCK, D),
    )
    gm, gl, gq, gco = pl.pallas_call(
        grads_kernel,
        out_shape=(
            shape((4, BLOCK, D), F32),
            shape((2, BLOCK, D), F32),
            shape((TILE, D), F32),
            shape((16, D), F32),
        ),
        in_specs=[smem(), hbm(), hbm(), vmem(), vmem()],
        out_specs=(hbm(), hbm(), hbm(), hbm()),
        scratch_shapes=[
            pltpu.SMEM((6,), jnp.int32),
            pltpu.SMEM((6 * LIST + 1,), jnp.int32),
            pltpu.VMEM((SLOTS + 1, TILE, D), BF16),
            pltpu.VMEM((SLOTS + 1, BLOCK, TILE), BF16),
            pltpu.VMEM((6, BLOCK, D), F32),
            dma((SLOTS,)),
            dma((SLOTS,)),
            dma((6,)),
            dma((2,)),
        ],
        compiler_params=pltpu.CompilerParams(vmem_limit_bytes=60 * mib),
        name="grads",
    )(plan, sel.reshape(SLOTS, TILE, D), deltas.reshape(SLOTS, BLOCK, TILE), gq, gco)
    return gq, gco, gm.reshape(4 * BLOCK, D), gl.reshape(2 * BLOCK, D)


def solution(mesh):
    placed = (
        P("grp", None),
        P(),
        P(("grp", "mid"), None),
        P(("grp", "mid"), None),
        P(("grp", "mid"), None),
        P("grp", None),
        P("grp", None),
        P("grp", None),
        P("grp", None),
        P(),
    )
    return jax.shard_map(
        shards,
        mesh=mesh,
        in_specs=placed,
        out_specs=(
            P(("grp", "mid"), None),
            P(("grp", "mid"), None),
            P(("grp", "mid"), None),
            P(("grp", "mid"), None),
        ),
        check_vma=False,
    )
```

```python
import jax
import jax.numpy as jnp
from jax import lax
from jax.experimental import pallas as pl
from jax.experimental.pallas import tpu as pltpu
from jax.sharding import PartitionSpec as P

TILE = 128
BLOCK = 512
COARSE = 2048
K_CAND = 8
D = 768
NY, NX, NZ = 4, 4, 4
TILES = NX * NZ
BIG = 1 << 20
F32 = jnp.float32
BF16 = jnp.bfloat16
MESH = pl.DeviceIdType.MESH
THIRD = D // 3
HALF = D // 2
NEAR = 64
REST = TILE - NEAR


def mm(a, b, ca, cb):
    return lax.dot_general(a, b, (((ca,), (cb,)), ((), ())), preferred_element_type=F32)


def delta_of(scores, labels, positives):
    hit = labels == positives[0:1]
    for p in range(1, 4):
        hit = hit | (labels == positives[p : p + 1])
    return (0.125 * jnp.tanh(0.5 * scores) + jnp.where(hit, -0.125, 0.125)).astype(BF16)


class Place:
    def __init__(self):
        grp, mid = lax.axis_index("grp"), lax.axis_index("mid")
        self.y, self.c = grp // 2, lax.rem(grp, 2)
        self.x, self.z = mid // NZ, lax.rem(mid, NZ)
        self.mid = mid
        self.ahead = 1 + 2 * self.c
        self.behind = 3 - 2 * self.c

    def at(self, dy=0, dx=0, dz=0, other=False):
        y, x, z = lax.rem(self.y + dy, NY), lax.rem(self.x + dx, NX), lax.rem(self.z + dz, NZ)
        return (2 * y + (1 - self.c if other else self.c), NZ * x + z)

    def sibling(self):
        return (2 * self.y + 1 - self.c, self.mid)

    def tile(self, dx, dz):
        return NZ * lax.rem(self.x + dx, NX) + lax.rem(self.z + dz, NZ)

    def greet(self):
        near = [self.sibling(), self.at(dy=2)]
        for step in (self.ahead, self.behind):
            near += [self.at(dy=step), self.at(dy=step, other=True)]
            near += [self.at(dx=step), self.at(dz=step)]
        barrier = pltpu.get_barrier_semaphore()
        for device in near:
            pl.semaphore_signal(barrier, inc=1, device_id=device, device_id_type=MESH)
        pl.semaphore_wait(barrier, len(near))


class Net:
    def __init__(self, send_sem, recv_sem):
        self.send_sem, self.recv_sem, self.made, self.drained = send_sem, recv_sem, [], 0

    def send(self, src, dst, device):
        i = len(self.made)
        copy = pltpu.make_async_remote_copy(
            src_ref=src,
            dst_ref=dst,
            send_sem=self.send_sem.at[i],
            recv_sem=self.recv_sem.at[i],
            device_id=device,
            device_id_type=MESH,
        )
        copy.start()
        self.made.append(copy)
        return copy

    def drain(self, count):
        for copy in self.made[self.drained : count]:
            copy.wait_send()
        self.drained = count


COPIES = 200
OWN, BACK, FRONT, ACROSS = range(4)
SLOTS = 32
LIST = 16


def role_step(color, role):
    return (0, 3 - 2 * color, 1 + 2 * color, 2)[role]


def main_kernel(
    q, mp, lp, mc, lc, cp, owner, cv, midv, leafv,
    gq, gco, plan, sel, deltas,
    q_own, q_b, q_a, q_2, p_own, cvv, cvm, cpall,
    in00, in01, in02, in03, in10, in11, in12, in13,
    no00, no01, no02, no03, no10, no11, no12, no13,
    sm00, sm01, sm02, sm03, sm10, sm11, sm12, sm13,
    no_a, no_b, no_x, planv, smo, pk_as, pk_ao, pk_bs, pk_bo, pk_own, pk_x, pk_b, pk_f,
    out_own, out_x, out0b, out0f, out1o, out1b, out1f, out1x,
    ret_own, x_0, x_1, a0_0, a0_1, a1_0, a1_1, b0_0, b0_1, b1_0, b1_1,
    vectors, held_delta, gc, qc, gsib, gbuf,
    s2, sb, r2, rb, ra, u2, ub, ua, far, local_sem, send_sem, recv_sem,
):
    me = Place()
    c, a, b = me.c, me.ahead, me.behind
    net = Net(send_sem, recv_sem)
    local, done = [], []

    def start_local(src, dst):
        copy = pltpu.make_async_copy(src, dst, local_sem.at[len(local)])
        copy.start()
        local.append(copy)
        return copy

    def wait_local(copy):
        copy.wait()
        done.append(copy)

    load_q = start_local(q, q_own)
    load_v = [start_local(midv, vectors.at[pl.ds(0, 4)]), start_local(leafv, vectors.at[pl.ds(4, 2)])]
    load_c = start_local(cv, cvv)
    for t in range(TILES):
        p_own[t, 0:4, :] = mp[:, t * TILE : (t + 1) * TILE]
        p_own[t, 4:8, :] = lp[:, t * TILE : (t + 1) * TILE]
    p_own[16:18] = jnp.full((2, 8, 128), -1, jnp.int32)
    p_own[16, :, 0:TILES] = mc[...]
    p_own[17, :, 0:TILES] = lc[...]
    cpall[me.x, me.z, 0:4, :] = cp[...]
    cpall[me.x, me.z, 4:8, :] = cp[...]
    me.greet()

    m = me.mid
    up, down, across = me.at(dy=a), me.at(dy=b), me.at(dy=2)
    up_other, down_other = me.at(dy=a, other=True), me.at(dy=b, other=True)
    xa, xb, za, zb = me.at(dx=a), me.at(dx=b), me.at(dz=a), me.at(dz=b)
    sib = me.sibling()
    planes = {BACK: q_b, FRONT: q_a, ACROSS: q_2}
    slots = ((in00, in01, in02, in03), (in10, in11, in12, in13))
    notes = ((no00, no01, no02, no03), (no10, no11, no12, no13))
    facts = ((sm00, sm01, sm02, sm03), (sm10, sm11, sm12, sm13))
    outs = ((out_own, out0b, out0f, out_x), (out1o, out1b, out1f, out1x))

    rest, near = pl.ds(NEAR, REST), pl.ds(0, NEAR)
    y_in = {
        BACK: net.send(q.at[m, rest], q_b.at[m], up),
        FRONT: net.send(q.at[m, rest], q_a.at[m], down),
        ACROSS: net.send(q.at[m], q_2.at[m], across),
    }
    pos_own = cpall.at[me.x, me.z]
    cz_a = net.send(pos_own, pos_own, za)
    cz_b = net.send(pos_own, pos_own, zb)

    index = lax.broadcasted_iota(jnp.int32, (2, 128), 0) * 128 + lax.broadcasted_iota(
        jnp.int32, (2, 128), 1
    )
    code = 4 * (
        TILES * lax.broadcasted_iota(jnp.int32, (8, 128), 0)
        + lax.broadcasted_iota(jnp.int32, (8, 128), 1)
    )
    lane = lax.broadcasted_iota(jnp.int32, (1, 128), 1)
    mids, leaves = p_own[16], p_own[17]

    def whole(value):
        return jnp.broadcast_to(value, (1, 128))

    def plan_slots(label):
        step = (0, a, b, 2)[label]
        for which, core in enumerate((c, 1 - c)):
            device = (2 * lax.rem(me.y + step, NY) + core) * TILES + m
            held = [
                whole(
                    jnp.sum(
                        jnp.where(owner[...] == 2 * device + i, index, 0), axis=(0, 1), keepdims=True
                    )
                )
                for i in range(2)
            ]
            entries = []
            for live, block in (
                ((mids >> 2) == device, mids & 3),
                ((leaves == held[0]) | (leaves == held[1]), (leaves == held[1]).astype(jnp.int32)),
            ):
                found = code + block
                first = whole(jnp.min(jnp.where(live, found, BIG), axis=(0, 1), keepdims=True))
                final = whole(jnp.max(jnp.where(live, found, -1), axis=(0, 1), keepdims=True))
                some = first < BIG
                entries.append((some, jnp.where(some, first, 0)))
                two = some & (final != first)
                entries.append((two, jnp.where(two, final, 0)))
            tiles = [(value >> 2) & 15 for _, value in entries]
            spots = jnp.full((1, 128), 4, jnp.int32)
            for e in (3, 2, 1, 0):
                spots = jnp.where(entries[e][0] & (tiles[e] == lane), e, spots)
            at = 32 + 2 * label + which
            planv[at : at + 1, :] = spots
            for e, (valid, value) in enumerate(entries):
                follow = jnp.full((1, 128), 4, jnp.int32)
                for f in range(3, e, -1):
                    follow = jnp.where(valid & entries[f][0] & (tiles[f] == tiles[e]), f, follow)
                row = jnp.where(lane == 0, jnp.where(valid, value & 3, -1), follow)
                row = jnp.where(lane == 2, tiles[e], row)
                row = jnp.where(lane == 3, value >> 6, row)
                row = jnp.where(lane == 4, (value & 3) + 4 * (e // 2), row)
                at = 8 * label + 4 * which + e
                planv[at : at + 1, :] = row
    planv[...] = jnp.zeros((40, 128), jnp.int32)
    plan_slots(BACK)
    plan_slots(FRONT)
    to_smem = start_local(planv, smo)
    wait_local(load_q)
    wait_local(to_smem)
    notes_out = (no00, no_a, no_b, no_x)

    def fill_notes(label):
        out = notes_out[label]
        for e in range(8):
            at = 8 * label + e
            level = 4 * (e % 4 // 2)
            positives = p_own[smo[at, 2]][level : level + 4] - BLOCK * smo[at, 3]
            out[e, 0:4, :] = positives
            out[e, 4:5, :] = planv[at : at + 1, :]
            out[e, 5:8, :] = jnp.zeros((3, 128), jnp.int32)
        out[8, 0:2, :] = planv[32 + 2 * label : 34 + 2 * label, :]
        out[8, 2:8, :] = jnp.zeros((6, 128), jnp.int32)

    direct, note_in = {}, {}
    for label, targets in ((BACK, ((pk_as, up), (pk_ao, up_other))), (FRONT, ((pk_bs, down), (pk_bo, down_other)))):
        fill_notes(label)
        for which, (buffer, device) in enumerate(targets):
            for e in range(4):
                buffer[e] = q_own[smo[8 * label + 4 * which + e, 2], 0:NEAR]
            note_in[which, label] = net.send(notes_out[label], notes[which][label], device)
            direct[which, label] = net.send(buffer, slots[which][label].at[:, near], device)
    plan_slots(ACROSS)
    plan_slots(OWN)
    to_smem = start_local(planv, smo)
    wait_local(to_smem)
    fill_notes(ACROSS)
    note_in[0, ACROSS] = net.send(no_x, no03, across)
    fill_notes(OWN)
    for e in range(4):
        pk_own[e] = q_own[smo[4 + e, 2]]
    note_in[1, OWN] = net.send(no00, no10, sib)
    beside = {OWN: net.send(pk_own, in10, sib)}
    for e in range(4):
        in00[e] = q_own[smo[e, 2]]

    axes = ((za, zb, xa, xb), (xa, xb, za, zb))
    walk = (0, b, a, 2)

    def rows_of(role, h):
        size = (TILE if role == ACROSS else REST) // 2
        return pl.ds(h * size, size)

    def tile_of(h, first, last):
        return me.tile(last, first) if h == 0 else me.tile(first, last)

    second, second_f, last, last_f = {}, {}, {}, {}

    def send_second(role):
        y_in[role].wait_recv()
        for h, (to_a, to_b, _, _) in enumerate(axes):
            piece = planes[role].at[m, rows_of(role, h)]
            second[role, h] = (net.send(piece, piece, to_a), net.send(piece, piece, to_b))

    def send_last(role, key):
        for h, (_, _, to_a, to_b) in enumerate(axes):
            piece = planes[role].at[tile_of(h, walk[key], 0), rows_of(role, h)]
            last[role, h, key] = (net.send(piece, piece, to_a), net.send(piece, piece, to_b))

    def second_stage(role):
        for h, (to_a, _, _, _) in enumerate(axes):
            second[role, h][0].wait_recv()
            piece = planes[role].at[tile_of(h, b, 0), rows_of(role, h)]
            second_f[role, h] = net.send(piece, piece, to_a)
        send_last(role, BACK)
        for h in range(2):
            second[role, h][1].wait_recv()
        send_last(role, FRONT)

    def across_stage(role):
        for h in range(2):
            second_f[role, h].wait_recv()
        send_last(role, ACROSS)

    def forward_last(role):
        for key, step in enumerate(walk):
            for h, (_, _, to_a, _) in enumerate(axes):
                last[role, h, key][0].wait_recv()
                piece = planes[role].at[tile_of(h, step, b), rows_of(role, h)]
                last_f[role, h, key] = net.send(piece, piece, to_a)

    def complete(role):
        for key in range(4):
            for h in range(2):
                last[role, h, key][1].wait_recv()
                last_f[role, h, key].wait_recv()

    fetches = {}

    def fetch(which, role):
        if (which, role) in note_in:
            note_in[which, role].wait_recv()
        fetches[which, role] = start_local(notes[which][role], facts[which][role])

    def know(which, role):
        wait_local(fetches[which, role])

    def pack(role):
        know(0, role)
        rows = planes[role]
        buffer = {BACK: pk_b, FRONT: pk_f, ACROSS: pk_x}[role]
        for e in range(4):
            buffer[e] = rows[facts[0][role][4 + e, 4, 2]]
            if role == ACROSS and e % 2:
                duo = pl.ds(e - 1, 2)
                beside[role, e // 2] = net.send(buffer.at[duo], in13.at[duo], sib)
        if role != ACROSS:
            beside[role] = net.send(buffer, slots[1][role].at[:, rest], sib)
        for e in range(4):
            value = rows[facts[0][role][e, 4, 2]]
            if role == ACROSS:
                in03[e] = value
            else:
                slots[0][role][e, NEAR:TILE] = value

    labels = lax.broadcasted_iota(jnp.int32, (BLOCK, TILE), 0)
    returns = {}

    def pairs(which, role, half):
        block_of, rows, info, out = (
            facts[which][role], slots[which][role], notes[which][role], outs[which][role]
        )
        group = pl.ds(4 * role, 4)
        if half == 0:
            if which == 1 or role == OWN:
                know(which, role)
            if (which, role) in direct:
                direct[which, role].wait_recv()
            if which == 1 and role != ACROSS:
                beside[role].wait_recv()
        if which == 1 and role == ACROSS:
            beside[role, half].wait_recv()
        both = (2 * half, 2 * half + 1)
        blocks = [vectors[block_of[4 * which + e, 4, 4]] for e in both]
        scores = [mm(block, rows[e], 1, 1) for e, block in zip(both, blocks)]
        for e, block, score in zip(both, blocks, scores):
            delta = delta_of(score, labels, info[4 * which + e])
            held_delta[which, 4 * role + e] = delta
            out[e] = mm(delta, block, 0, 0).astype(BF16)
            at = 16 * which + 4 * role + e
            plan[at : at + 1, :] = info[4 * which + e, 4:5, :]
        if half == 1:
            start_local(rows, sel.at[which, group])
            start_local(held_delta.at[which, group], deltas.at[which, group])
            for e in (2, 1, 0):
                out[e] = out[e] + out[block_of[4 * which + e, 4, 1]]

    row_halves = (pl.ds(0, TILE // 2), pl.ds(TILE // 2, TILE // 2))
    ret_a0, ret_a1, ret_b0, ret_b1 = (a0_0, a0_1), (a1_0, a1_1), (b0_0, b0_1), (b1_0, b1_1)
    ret_x = (x_0, x_1)
    four = pl.ds(0, 4)

    def give_back(which, role, r):
        out = outs[which][role]
        back = {
            (0, BACK): (ret_a0, down),
            (0, FRONT): (ret_b0, up),
            (1, BACK): (ret_a1, up_other),
            (1, FRONT): (ret_b1, down_other),
        }[which, role]
        returns[which, role, r] = net.send(
            out.at[four, row_halves[r]], back[0][r].at[four], back[1]
        )

    for ref in outs[0] + outs[1] + (ret_own,):
        ref[4] = jnp.zeros((TILE, D), BF16)
    for ref in ret_x + ret_a0 + ret_a1 + ret_b0 + ret_b1:
        ref[4] = jnp.zeros((TILE // 2, D), BF16)
    steps = (0, b, a, 2)
    first_axis = ((xa, xb), (za, zb))
    first2, firsta, firstb = {}, {}, {}
    second2, seconda, secondb = {}, {}, {}
    term_in = {}

    def part(h, stream, unit, j):
        tile = me.tile(steps[unit], steps[j]) if h == 0 else me.tile(steps[j], steps[unit])
        cols = slice(h * HALF, (h + 1) * HALF)
        r = stream % 2
        rows = slice(r * TILE // 2, (r + 1) * TILE // 2)
        if stream < 2:
            return out_x[sm03[8, 0, tile], rows, cols] + ret_x[r][sm03[8, 1, tile], :, cols]
        value = out_own[smo[32 + 2 * OWN, tile], rows, cols]
        value += ret_own[smo[33 + 2 * OWN, tile], rows, cols]
        value += ret_a0[r][smo[32 + 2 * BACK, tile], :, cols]
        value += ret_a1[r][smo[33 + 2 * BACK, tile], :, cols]
        value += ret_b0[r][smo[32 + 2 * FRONT, tile], :, cols]
        return value + ret_b1[r][smo[33 + 2 * FRONT, tile], :, cols]

    def begin_sum(stream):
        if stream < 2:
            term_in[ACROSS, stream].wait_recv()
        if stream >= 2:
            if stream == 2:
                term_in[OWN].wait_recv()
            for which in range(2):
                for role in (BACK, FRONT):
                    returns[which, role, stream - 2].wait_recv()
        for h in range(2):
            for j in range(4):
                s2[h, stream, j] = part(h, stream, ACROSS, j)
            first2[h, stream] = net.send(s2.at[h, stream], r2.at[h, stream], first_axis[h][0])
            for j in range(4):
                sb[h, stream, j] = part(h, stream, BACK, j)
            firstb[h, stream] = net.send(sb.at[h, stream], rb.at[h, stream], first_axis[h][1])

    def pass_sum(stream):
        for h in range(2):
            first2[h, stream].wait_recv()
            for j in range(4):
                r2[h, stream, j] = r2[h, stream, j] + part(h, stream, FRONT, j)
            firsta[h, stream] = net.send(r2.at[h, stream], ra.at[h, stream], first_axis[h][0])

    def begin_second(stream):
        for h in range(2):
            firstb[h, stream].wait_recv()
            firsta[h, stream].wait_recv()
            to_a, to_b = first_axis[1 - h]
            for j in (ACROSS, BACK, FRONT, OWN):
                rb[h, stream, j] = part(h, stream, OWN, j) + rb[h, stream, j] + ra[h, stream, j]
                if j == ACROSS:
                    second2[h, stream] = net.send(rb.at[h, stream, j], u2.at[h, stream], to_a)
                if j == BACK:
                    secondb[h, stream] = net.send(rb.at[h, stream, j], ub.at[h, stream], to_b)

    def pass_second(stream):
        for h in range(2):
            second2[h, stream].wait_recv()
            u2[h, stream] = u2[h, stream] + rb[h, stream, FRONT]
            seconda[h, stream] = net.send(u2.at[h, stream], ua.at[h, stream], first_axis[1 - h][0])

    def end_second(stream):
        for h in range(2):
            secondb[h, stream].wait_recv()
            seconda[h, stream].wait_recv()
            ub[h, stream] = rb[h, stream, OWN] + ub[h, stream] + ua[h, stream]

    fetch(0, OWN)
    send_second(BACK)
    send_second(FRONT)
    send_last(BACK, OWN)
    send_second(ACROSS)
    for load in load_v:
        wait_local(load)
    pairs(0, OWN, 0)
    second_stage(BACK)
    cz_a.wait_recv()
    pos_b = cpall.at[me.x, lax.rem(me.z + b, NZ)]
    cz_f = net.send(pos_b, pos_b, za)
    send_last(FRONT, OWN)
    pairs(0, OWN, 1)
    second_stage(FRONT)
    across_stage(BACK)
    fetch(1, OWN)
    fetch(0, BACK)
    fetch(0, FRONT)
    cz_b.wait_recv()
    cz_f.wait_recv()
    pos_row = cpall.at[me.x]
    cx_a = net.send(pos_row, pos_row, xa)
    cx_b = net.send(pos_row, pos_row, xb)
    forward_last(BACK)
    pairs(1, OWN, 0)
    across_stage(FRONT)
    send_last(ACROSS, OWN)
    second_stage(ACROSS)
    pairs(1, OWN, 1)
    term_in[OWN] = net.send(out1o.at[four], ret_own.at[four], sib)
    complete(BACK)
    pack(BACK)
    across_stage(ACROSS)
    forward_last(FRONT)
    cx_a.wait_recv()
    pos_row_b = cpall.at[lax.rem(me.x + b, NX)]
    cx_f = net.send(pos_row_b, pos_row_b, xa)
    pairs(0, BACK, 0)
    pairs(0, BACK, 1)
    give_back(0, BACK, 0)
    fetch(1, BACK)
    fetch(1, FRONT)
    fetch(0, ACROSS)
    note_in[1, ACROSS] = net.send(no03, no13, sib)
    complete(FRONT)
    pack(FRONT)
    pairs(0, FRONT, 0)
    pairs(0, FRONT, 1)
    give_back(0, FRONT, 0)
    give_back(0, BACK, 1)
    give_back(0, FRONT, 1)
    forward_last(ACROSS)
    pairs(1, BACK, 0)
    pairs(1, BACK, 1)
    give_back(1, BACK, 0)
    fetch(1, ACROSS)
    pairs(1, FRONT, 0)
    pairs(1, FRONT, 1)
    give_back(1, FRONT, 0)
    give_back(1, BACK, 1)
    give_back(1, FRONT, 1)
    complete(ACROSS)
    pack(ACROSS)
    pairs(0, ACROSS, 0)
    pairs(1, ACROSS, 0)
    pairs(1, ACROSS, 1)
    for r in range(2):
        term_in[ACROSS, r] = net.send(out1x.at[four, row_halves[r]], ret_x[r].at[four], sib)
    pairs(0, ACROSS, 1)
    early = len(net.made)
    wait_local(load_c)
    for j in range(8):
        color, role = j // 4, j % 4
        row = (2 * lax.rem(me.y + role_step(color, role), NY) + color) * TILES + m
        start = pl.multiple_of(row * 16, 16)
        cvm[pl.ds(16 * j, 16), :] = cvv[pl.ds(start, 16), :]
    place = lax.broadcasted_iota(jnp.int32, (128, 128), 0)
    chunk = place // 16
    color, role = chunk // 4, lax.rem(chunk, 4)
    step = jnp.where(role == ACROSS, 2, jnp.where(role == FRONT, 1 + 2 * color, 3 - 2 * color))
    step = jnp.where(role == OWN, 0, step)
    owner_grp = 2 * lax.rem(me.y + step, NY) + color
    coarse_ids = (owner_grp * TILES + m) * 16 + lax.rem(place, 16)

    def own_coarse():
        qm = q_own[m]
        total = jnp.zeros((TILE, D), F32)
        for i in range(COARSE // BLOCK):
            vectors = cvv[i * BLOCK : (i + 1) * BLOCK, :]
            labels = lax.broadcasted_iota(jnp.int32, (BLOCK, TILE), 0) + i * BLOCK
            delta = delta_of(mm(vectors, qm, 1, 1), labels, cpall[me.x, me.z])
            total += mm(delta, vectors, 0, 0)
        qc[...] = total

    def rows_coarse(lo, hi):
        def body(t, carry):
            qt = q_own[pl.ds(2 * t, 2)].reshape(2 * TILE, D)
            scores = mm(cvm[...], qt, 1, 1)
            delta = jnp.concatenate(
                [
                    delta_of(
                        scores[:, h * TILE : (h + 1) * TILE],
                        coarse_ids,
                        cpall[t // 2, 2 * lax.rem(t, 2) + h],
                    )
                    for h in range(2)
                ],
                axis=1,
            )
            gc[...] += mm(delta, qt, 1, 0)
            return carry

        lax.fori_loop(lo, hi, body, 0)


    gc[...] = jnp.zeros_like(gc)
    cx_b.wait_recv()
    cx_f.wait_recv()
    rows_coarse(0, 4)
    begin_sum(0)
    begin_sum(1)
    begin_sum(2)
    rows_coarse(4, 8)
    coarse = net.send(gc.at[pl.ds(64 * (1 - c), 64)], gsib, sib)
    pass_sum(0)
    pass_sum(1)
    pass_sum(2)
    own_coarse()
    begin_sum(3)
    begin_second(0)
    begin_second(1)
    begin_second(2)
    pass_sum(3)
    pass_second(0)
    pass_second(1)
    pass_second(2)
    coarse.wait_recv()
    for role in range(4):
        gbuf[role] = gc[pl.ds(64 * c + 16 * role, 16)] + gsib[16 * role : 16 * role + 16]
    coarse2 = net.send(gbuf.at[ACROSS], gbuf.at[5], up)
    coarseb = net.send(gbuf.at[BACK], gbuf.at[6], down)
    end_second(0)
    end_second(1)
    home = net.send(ub.at[:, pl.ds(0, 2)], far, across)
    begin_second(3)
    end_second(2)
    coarse2.wait_recv()
    gbuf[4] = gbuf[FRONT] + gbuf[5]
    coarsea = net.send(gbuf.at[4], gbuf.at[7], up)
    pass_second(3)
    net.drain(early)
    for copy in local:
        if not any(copy is other for other in done):
            wait_local(copy)
    coarsea.wait_recv()
    coarseb.wait_recv()
    gco[...] = gbuf[OWN] + gbuf[6] + gbuf[7]
    home.wait_recv()
    end_second(3)
    for h in range(2):
        cols = slice(h * HALF, (h + 1) * HALF)
        for r in range(2):
            rows = slice(r * TILE // 2, (r + 1) * TILE // 2)
            gq[rows, cols] = (
                qc[rows, cols] + ub[h, 2 + r].astype(F32) + far[h, r].astype(F32)
            )
    for copy in local:
        if not any(copy is other for other in done):
            copy.wait()
    net.drain(len(net.made))


def grads_kernel(
    plan, sel, deltas, gq_in, gco_in,
    gm, gl, gq, gco,
    counts, entries, rows, held, acc, row_sem, delta_sem, grad_sem, out_sem,
):
    results = [
        pltpu.make_async_copy(gq_in, gq, out_sem.at[0]),
        pltpu.make_async_copy(gco_in, gco, out_sem.at[1]),
    ]
    for copy in results:
        copy.start()
    stores = [(gm, 0), (gm, 1), (gm, 2), (gm, 3), (gl, 0), (gl, 1)]

    def row_copy(e):
        return pltpu.make_async_copy(sel.at[e], rows.at[e], row_sem.at[e])

    def delta_copy(e):
        return pltpu.make_async_copy(deltas.at[e], held.at[e], delta_sem.at[e])

    for key in range(6):
        counts[key] = 0
    for e in range(SLOTS):
        block = plan[e, 0]

        @pl.when(block >= 0)
        def _():
            row_copy(e).start()
            delta_copy(e).start()
            key = block + 4 * (e // 2 % 2)
            n = counts[key]
            entries[LIST * key + n] = e
            counts[key] = n + 1

    rows[SLOTS] = jnp.zeros((TILE, D), BF16)
    held[SLOTS] = jnp.zeros((BLOCK, TILE), BF16)

    def per_key(key, carry):
        n = counts[key]
        start = LIST * key

        @pl.when(n == 0)
        def _():
            acc[key] = jnp.zeros((BLOCK, D), F32)

        def batch(i, inner):
            at = start + 2 * i
            full = 2 * i + 1 < n
            e0 = entries[at]
            e1 = jnp.where(full, entries[at + 1], SLOTS)
            row_copy(e0).wait()
            delta_copy(e0).wait()

            @pl.when(full)
            def _():
                row_copy(e1).wait()
                delta_copy(e1).wait()

            both = jnp.concatenate([rows[e0], rows[e1]], axis=0)
            delta = jnp.concatenate([held[e0], held[e1]], axis=1)

            @pl.when(i == 0)
            def _():
                for n_col in range(3):
                    cols = slice(n_col * THIRD, (n_col + 1) * THIRD)
                    acc[key, :, cols] = mm(delta, both[:, cols], 1, 0)

            @pl.when(i != 0)
            def _():
                for n_col in range(3):
                    cols = slice(n_col * THIRD, (n_col + 1) * THIRD)
                    acc[key, :, cols] += mm(delta, both[:, cols], 1, 0)

            return inner

        lax.fori_loop(0, (n + 1) // 2, batch, 0)
        for i, (out, j) in enumerate(stores):

            @pl.when(key == i)
            def _():
                pltpu.make_async_copy(acc.at[i], out.at[j], grad_sem.at[i]).start()

        return carry

    lax.fori_loop(0, 6, per_key, 0)
    for i, (out, j) in enumerate(stores):
        pltpu.make_async_copy(acc.at[i], out.at[j], grad_sem.at[i]).wait()
    for copy in results:
        copy.wait()


def vmem():
    return pl.BlockSpec(memory_space=pltpu.VMEM)


def smem():
    return pl.BlockSpec(memory_space=pltpu.SMEM)


def hbm():
    return pl.BlockSpec(memory_space=pl.ANY)


def shape(dims, dtype):
    return jax.ShapeDtypeStruct(dims, dtype)


def shards(
    queries,
    coarse_vectors,
    mid_vectors,
    leaf_vectors,
    coarse_pos,
    mid_pos,
    leaf_pos,
    mid_cand,
    leaf_cand,
    leaf_owner,
):
    dma = pltpu.SemaphoreType.DMA
    mib = 1024 * 1024
    group = pltpu.VMEM((TILES, TILE, D), BF16)
    part = pltpu.VMEM((TILES, REST, D), BF16)
    four = pltpu.VMEM((4, TILE, D), BF16)
    five = pltpu.VMEM((5, TILE, D), BF16)
    half = pltpu.VMEM((5, TILE // 2, D), BF16)
    near = pltpu.VMEM((4, NEAR, D), BF16)
    rest = pltpu.VMEM((4, REST, D), BF16)
    notes = pltpu.VMEM((9, 8, 128), jnp.int32)
    facts = pltpu.SMEM((9, 8, 128), jnp.int32)
    first = pltpu.VMEM((2, 4, 4, TILE // 2, HALF), BF16)
    second = pltpu.VMEM((2, 4, TILE // 2, HALF), BF16)
    gq, gco, plan, sel, deltas = pl.pallas_call(
        main_kernel,
        out_shape=(
            shape((TILE, D), F32),
            shape((16, D), F32),
            shape((SLOTS, 128), jnp.int32),
            shape((2, 16, TILE, D), BF16),
            shape((2, 16, BLOCK, TILE), BF16),
        ),
        in_specs=[hbm(), vmem(), vmem(), vmem(), vmem(), vmem(), vmem(), hbm(), hbm(), hbm()],
        out_specs=(vmem(), vmem(), vmem(), hbm(), hbm()),
        scratch_shapes=[
            group, part, part, group,
            pltpu.VMEM((18, 8, 128), jnp.int32),
            pltpu.VMEM((COARSE, D), BF16),
            pltpu.VMEM((128, D), BF16),
            pltpu.VMEM((NX, NZ, 8, TILE), jnp.int32),
            four, four, four, four, four, four, four, four,
            notes, notes, notes, notes, notes, notes, notes, notes,
            facts, facts, facts, facts, facts, facts, facts, facts,
            notes, notes, notes,
            pltpu.VMEM((40, 128), jnp.int32),
            pltpu.SMEM((40, 128), jnp.int32),
            near, near, near, near, four, four, rest, rest,
            five, five, five, five, five, five, five, five,
            five,
            half, half, half, half, half, half, half, half, half, half,
            pltpu.VMEM((6, BLOCK, D), BF16),
            pltpu.VMEM((2, 16, BLOCK, TILE), BF16),
            pltpu.VMEM((128, D), F32),
            pltpu.VMEM((TILE, D), F32),
            pltpu.VMEM((64, D), F32),
            pltpu.VMEM((8, 16, D), F32),
            first, first, first, first, first,
            second, second, second,
            pltpu.VMEM((2, 2, TILE // 2, HALF), BF16),
            dma((40,)),
            dma((COPIES,)),
            dma((COPIES,)),
        ],
        compiler_params=pltpu.CompilerParams(
            collective_id=0, has_side_effects=True, vmem_limit_bytes=62 * mib
        ),
        name="main",
    )(
        queries.reshape(TILES, TILE, D),
        mid_pos.T,
        leaf_pos.T,
        mid_cand.T,
        leaf_cand.T,
        coarse_pos.T,
        leaf_owner.reshape(2, 128),
        coarse_vectors,
        mid_vectors.reshape(4, BLOCK, D),
        leaf_vectors.reshape(2, BLOCK, D),
    )
    gm, gl, gq, gco = pl.pallas_call(
        grads_kernel,
        out_shape=(
            shape((4, BLOCK, D), F32),
            shape((2, BLOCK, D), F32),
            shape((TILE, D), F32),
            shape((16, D), F32),
        ),
        in_specs=[smem(), hbm(), hbm(), vmem(), vmem()],
        out_specs=(hbm(), hbm(), hbm(), hbm()),
        scratch_shapes=[
            pltpu.SMEM((6,), jnp.int32),
            pltpu.SMEM((6 * LIST + 1,), jnp.int32),
            pltpu.VMEM((SLOTS + 1, TILE, D), BF16),
            pltpu.VMEM((SLOTS + 1, BLOCK, TILE), BF16),
            pltpu.VMEM((6, BLOCK, D), F32),
            dma((SLOTS,)),
            dma((SLOTS,)),
            dma((6,)),
            dma((2,)),
        ],
        compiler_params=pltpu.CompilerParams(vmem_limit_bytes=60 * mib),
        name="grads",
    )(plan, sel.reshape(SLOTS, TILE, D), deltas.reshape(SLOTS, BLOCK, TILE), gq, gco)
    return gq, gco, gm.reshape(4 * BLOCK, D), gl.reshape(2 * BLOCK, D)


def solution(mesh):
    placed = (
        P("grp", None),
        P(),
        P(("grp", "mid"), None),
        P(("grp", "mid"), None),
        P(("grp", "mid"), None),
        P("grp", None),
        P("grp", None),
        P("grp", None),
        P("grp", None),
        P(),
    )
    return jax.shard_map(
        shards,
        mesh=mesh,
        in_specs=placed,
        out_specs=(
            P(("grp", "mid"), None),
            P(("grp", "mid"), None),
            P(("grp", "mid"), None),
            P(("grp", "mid"), None),
        ),
        check_vma=False,
    )
```
